32 devices in a mesh: groups: 2 (over y), ctx: 4 (over z), head: 4 (over x, core).
Axes of the slice: x: 2, y: 2, z: 4, core: 2. Of those that a mesh axis runs over, the one named last changes fastest.
Arguments:
- query_raw: bfloat16 [8192, 2048], P(('groups', 'ctx'), 'head'), parts along dimension 0, may hold values from -6 to 6
- key_raw: bfloat16 [8192, 2048], P(('groups', 'ctx'), 'head'), parts along dimension 0, may hold values from -6 to 6
- value_raw: bfloat16 [8192, 4096], P(('groups', 'ctx'), 'head'), parts along dimension 0, may hold values from -6 to 6
- conv_query: bfloat16 [4, 2048], P(None, 'head'), may hold values from -3 to 3
- conv_key: bfloat16 [4, 2048], P(None, 'head'), may hold values from -3 to 3
- conv_value: bfloat16 [4, 4096], P(None, 'head'), may hold values from -3 to 3
- gate_log: float32 [8192, 32], P(('groups', 'ctx'), 'head'), parts along dimension 0, may hold values from -0.8 to 0, as said below
- beta_logit: float32 [8192, 32], P(('groups', 'ctx'), 'head'), parts along dimension 0, may hold values from -8 to 2, as said below
- norm_gain: float32 [128], replicated, may hold values from 0.1 to 1.9
Outputs:
- attended: bfloat16 [8192, 4096], P(('groups', 'ctx'), 'head'), parts along dimension 0
The draws below stay inside these ranges and needn't reach their ends.
There are 2 independent parts, one for each index of `groups`. The reference program is written for one: setup_inputs(seed, part) draws one part's arguments, and reference() takes and returns one part's arrays. A program takes and returns all parts, laid end to end along the dimension named above; an argument that names none is the same for every part. Nothing has to cross between parts.
Inputs may be any that keep to these rules, and one draw needn't show every extreme that they name: `gate_log`: decay logarithms are negative. `beta_logit`: write strengths are logits of numbers between 0 and 1.
All inputs are finite; a program needn't handle non-finite values.
Results may differ from the reference program's by a relative error of at most 0.012.
Values may be sent and summed in bfloat16 or wider, within the bound.
No kernel may reach another device: no remote copies, remote signals or barrier semaphores. Data moves between devices by JAX's collectives and lax.ppermute only.
A program may use at most 128 MiB of HBM per device.

```python
import jax
import jax.numpy as jnp
from jax import lax

DK = 128
DV = 128
KHEADS = 16
VHEADS = 32
KW = 4
SPAN = 64
NTOK = 4096


def head_classes(key):
    order = jax.random.permutation(jax.random.fold_in(key, 7), VHEADS)
    return order < VHEADS // 2


def draw_gate_log(key, part):
    slow_heads = head_classes(key)
    base = jax.random.fold_in(key, 11)
    slow_rate = jax.random.uniform(jax.random.fold_in(base, 1), (VHEADS,), jnp.float32, 0.1, 0.4) / NTOK
    quick_fading_speed = jnp.exp(jax.random.uniform(jax.random.fold_in(base, 2), (VHEADS,), jnp.float32, jnp.log(1.0 / 50.0), jnp.log(1.0 / 30.0)))
    fading_speed = jnp.where(slow_heads, slow_rate, quick_fading_speed)
    coarse_guess = jax.random.uniform(jax.random.fold_in(base, 3), (NTOK, VHEADS), jnp.float32, 0.5, 2.0)
    spots = jax.random.randint(jax.random.fold_in(base, 4), (2, VHEADS), 0, NTOK)
    error_readings = jax.random.uniform(jax.random.fold_in(base, 5), (2, VHEADS), jnp.float32, 0.22, 0.69)
    positions = jnp.arange(NTOK, dtype=jnp.int32)
    agreement_tallies = (positions[:, None, None] == spots[None, :, :]).astype(jnp.float32)
    spike_clusters = jnp.sum(agreement_tallies * error_readings[None, :, :], axis=1)
    return -(fading_speed[None, :] * coarse_guess) - spike_clusters


def draw_beta_logit(key, part):
    slow_heads = head_classes(key)
    base = jax.random.fold_in(key, 21)
    slow_base = jnp.log(DK / (2.0 * NTOK)) * jnp.ones((VHEADS,), jnp.float32)
    fast_base = jax.random.uniform(jax.random.fold_in(base, 1), (VHEADS,), jnp.float32, -1.0, 1.0)
    level = jnp.where(slow_heads, slow_base, fast_base)
    jitter = jax.random.uniform(jax.random.fold_in(base, 2), (NTOK, VHEADS), jnp.float32, -0.7, 0.7)
    return level[None, :] + jitter


def level_of(own_key, dims, cuts, smallest, top_value):
    def one(position, shards_of):
        draws = jax.random.uniform(jax.random.fold_in(jax.random.fold_in(own_key, 6), position), (shards_of,), jnp.float32, smallest / len(cuts), top_value / len(cuts))
        return jnp.repeat(jnp.exp(draws), dims[position] // shards_of).reshape((-1,) + (1,) * (len(dims) - position - 1))

    level = one(*cuts[0])
    for cut in cuts[1:]:
        level = level * one(*cut)
    return level


def normal_values(own_key, shape, spread, limit, cuts=(), kind=jnp.bfloat16):
    loudness = level_of(own_key, shape, cuts, -0.22, 0.18) if cuts else 1.0
    drawn = jax.random.normal(own_key, shape, jnp.float32) * spread * loudness
    return jnp.minimum(jnp.maximum(drawn, -limit), limit).astype(kind)


def setup_inputs(seed: int = 0, part: int = 0) -> dict:
    seeds = jax.random.split(jax.random.key(seed), 10)
    part_splits = jax.random.split(jax.random.fold_in(seeds[9], part), 10)
    return {
        "query_raw": normal_values(part_splits[0], (NTOK, KHEADS * DK), 1.0, 6.0, ((0, 4), (1, 4))),
        "key_raw": normal_values(part_splits[1], (NTOK, KHEADS * DK), 1.0, 6.0, ((0, 4), (1, 4))),
        "value_raw": normal_values(part_splits[2], (NTOK, VHEADS * DV), 1.0, 6.0, ((0, 4), (1, 4))),
        "conv_query": normal_values(seeds[3], (KW, KHEADS * DK), KW ** -0.5, 3.0, ((1, 4),)),
        "conv_key": normal_values(seeds[4], (KW, KHEADS * DK), KW ** -0.5, 3.0, ((1, 4),)),
        "conv_value": normal_values(seeds[5], (KW, VHEADS * DV), KW ** -0.5, 3.0, ((1, 4),)),
        "gate_log": draw_gate_log(jax.random.fold_in(jax.random.fold_in(seeds[9], part), 71), part),
        "beta_logit": draw_beta_logit(jax.random.fold_in(jax.random.fold_in(seeds[9], part), 71), part),
        "norm_gain": jnp.clip(1.0 + 0.18 * jax.random.normal(seeds[8], (DV,), jnp.float32), 0.1, 1.9),
    }


EPSILON = 1e-06
EXACTNESS = lax.Precision.HIGHEST

def conv_silu(values_in, prefix, kernel_function):
    padded = jnp.concatenate([prefix, values_in], axis=0)
    total = jnp.zeros(values_in.shape, jnp.float32)
    for start_offset in range(KW):
        total = total + padded[start_offset:start_offset + values_in.shape[0]].astype(jnp.float32) * kernel_function[start_offset].astype(jnp.float32)
    return jax.nn.silu(total).astype(jnp.bfloat16)

def unit_rows(values):
    return values * lax.rsqrt(lax.optimization_barrier(jnp.sum(values * values, axis=-1, keepdims=True)) + EPSILON)

def lower_inverse(inner):
    power = -inner
    inverse = jnp.eye(SPAN, dtype=jnp.float32) + power
    for level in range(SPAN.bit_length() - 2):
        power = jnp.dot(power, power, precision=EXACTNESS)
        inverse = inverse + jnp.dot(inverse, power, precision=EXACTNESS)
    return inverse

def span_pieces(query, keys, values, gates, betas):
    cum_gate = jnp.cumsum(gates)
    row_ids = lax.broadcasted_iota(jnp.int32, (SPAN, SPAN), 0)
    col_ids = lax.broadcasted_iota(jnp.int32, (SPAN, SPAN), 1)
    lower = row_ids >= col_ids
    decays = jnp.where(lower, jnp.exp(jnp.where(lower, cum_gate[:, None] - cum_gate[None, :], 0.0)), 0.0)
    keys_wide = keys.astype(jnp.float32)
    query_wide = query.astype(jnp.float32)
    gram = jnp.dot(keys, keys.T, preferred_element_type=jnp.float32)
    inner = jnp.where(row_ids > col_ids, betas[:, None] * gram * decays, 0.0)
    key_beta = keys_wide * betas[:, None]
    right_side = jnp.concatenate([key_beta * jnp.exp(cum_gate)[:, None], values * betas[:, None]], axis=1)
    solved = jnp.dot(lower_inverse(inner), right_side, precision=EXACTNESS)
    erase_rows = solved[:, :keys.shape[1]]
    write_rows = solved[:, keys.shape[1]:]
    scores = jnp.where(lower, jnp.dot(query, keys.T, preferred_element_type=jnp.float32) * decays, 0.0)
    query_dec = query_wide * jnp.exp(cum_gate)[:, None]
    key_dec = keys_wide * jnp.exp(cum_gate[-1] - cum_gate)[:, None]
    tail_decay = jnp.exp(cum_gate[-1])
    return (erase_rows, write_rows, scores, query_dec, key_dec, tail_decay)

def span_output(memory, pieces, gain):
    erase_rows, write_rows, scores, query_dec, key_dec, tail_decay = pieces
    corrected = write_rows - jnp.dot(erase_rows, memory, precision=EXACTNESS)
    output = jnp.dot(query_dec, memory, precision=EXACTNESS) + jnp.dot(scores, corrected, precision=EXACTNESS)
    memory = tail_decay * memory + jnp.dot(key_dec.T, corrected, precision=EXACTNESS)
    normed = output * lax.rsqrt(lax.optimization_barrier(jnp.mean(output * output, axis=-1, keepdims=True)) + EPSILON) * gain
    return (memory, normed.astype(jnp.bfloat16))

def reference(query_raw, key_raw, value_raw, conv_query, conv_key, conv_value, gate_log, beta_logit, norm_gain):
    tok_count = query_raw.shape[0]
    blocks = tok_count // SPAN
    ratio = VHEADS // KHEADS
    query_conv = conv_silu(query_raw, jnp.zeros((KW - 1, query_raw.shape[1]), query_raw.dtype), conv_query)
    key_conv = conv_silu(key_raw, jnp.zeros((KW - 1, key_raw.shape[1]), key_raw.dtype), conv_key)
    value_conv = conv_silu(value_raw, jnp.zeros((KW - 1, value_raw.shape[1]), value_raw.dtype), conv_value)
    query_unit = (unit_rows(query_conv.astype(jnp.float32).reshape(tok_count, KHEADS, DK)) * DK ** (-0.5)).astype(jnp.bfloat16)
    key_unit = unit_rows(key_conv.astype(jnp.float32).reshape(tok_count, KHEADS, DK)).astype(jnp.bfloat16)
    query_heads = query_unit.transpose(1, 0, 2).reshape(KHEADS, blocks, SPAN, DK)
    key_heads = key_unit.transpose(1, 0, 2).reshape(KHEADS, blocks, SPAN, DK)
    value_heads = value_conv.astype(jnp.float32).reshape(tok_count, VHEADS, DV).transpose(1, 0, 2).reshape(VHEADS, blocks, SPAN, DV)
    gate_heads = gate_log.T.reshape(VHEADS, blocks, SPAN)
    beta_heads = jax.nn.sigmoid(beta_logit).T.reshape(VHEADS, blocks, SPAN)

    def one_head(head_idx):
        group_idx = head_idx // ratio

        def advance(memory, inputs):
            pieces = span_pieces(inputs[0], inputs[1], inputs[2], inputs[3], inputs[4])
            return span_output(memory, pieces, norm_gain)
        inputs = (query_heads[group_idx], key_heads[group_idx], value_heads[head_idx], gate_heads[head_idx], beta_heads[head_idx])
        return lax.scan(advance, jnp.zeros((DK, DV), jnp.float32), inputs)[1]
    stacked = lax.map(one_head, jnp.arange(VHEADS, dtype=jnp.int32))
    return stacked.reshape(VHEADS, tok_count, DV).transpose(1, 0, 2).reshape(tok_count, VHEADS * DV)
```

```python
import jax
import jax.numpy as jnp
from jax import lax
from jax.experimental import pallas as pl
from jax.experimental.pallas import tpu as pltpu
from jax.sharding import PartitionSpec as P

DK = 128
DV = 128
KW = 4
CHUNK = 128
GROUP = 2
HALO = 8
RIM = 16
BASE = 16
EPSILON = 1e-06
F32 = jnp.float32
BF16 = jnp.bfloat16


def passed_along(value, axis):
    count = lax.axis_size(axis)
    return lax.ppermute(value, axis, [(source, source + 1) for source in range(count - 1)])


def dot(left, right):
    return jnp.dot(left, right, preferred_element_type=F32)


def diagonal_mask(size):
    rows = lax.broadcasted_iota(jnp.int32, (2 * CHUNK, 2 * CHUNK), 0)
    cols = lax.broadcasted_iota(jnp.int32, (2 * CHUNK, 2 * CHUNK), 1)
    return rows // size == cols // size


def odd_mask(size):
    rows = lax.broadcasted_iota(jnp.int32, (2 * CHUNK, 2 * CHUNK), 0)
    cols = lax.broadcasted_iota(jnp.int32, (2 * CHUNK, 2 * CHUNK), 1)
    return (rows // (2 * size) == cols // (2 * size)) & ((rows // size) % 2 == 1)


def levels():
    sizes = []
    size = BASE
    while size < CHUNK:
        sizes.append(size)
        size *= 2
    return sizes


def spread(strip, mask):
    count = 2 * CHUNK // strip.shape[0]
    return jnp.concatenate([strip] * count, axis=0) * mask


def inverses(negs, diag_ref, odd_ref):
    sizes = levels()
    lanes = lax.broadcasted_iota(jnp.int32, (1, 2 * CHUNK), 1) % CHUNK

    def strips(neg, size, step, first):
        out = neg[first : first + size]
        for turn in range(1, CHUNK // step):
            start = turn * step + first
            out = jnp.where(lanes // step == turn, neg[start : start + size], out)
        return out

    rows = lax.broadcasted_iota(jnp.int32, (BASE, 2 * CHUNK), 0)
    cols = lax.broadcasted_iota(jnp.int32, (BASE, 2 * CHUNK), 1)
    unit = (rows == cols % BASE).astype(F32)
    powers = [strips(neg, BASE, BASE, 0) for neg in negs]
    found = [unit + power for power in powers]
    shorts = [power.astype(BF16) for power in powers]
    weights = [spread(short, diag_ref[0]) for short in shorts]
    shorts = [dot(short, weight).astype(BF16) for short, weight in zip(shorts, weights)]
    reach = 2
    while reach < BASE:
        weights = [spread(short, diag_ref[0]) for short in shorts]
        last = 2 * reach >= BASE
        if last:
            found = [f + dot(f.astype(BF16), w) for f, w in zip(found, weights)]
        else:
            both = [
                dot(jnp.concatenate([s, f.astype(BF16)], axis=0), w)
                for s, f, w in zip(shorts, found, weights)
            ]
            shorts = [b[:BASE].astype(BF16) for b in both]
            found = [f + b[BASE:] for f, b in zip(found, both)]
        reach *= 2
    for place, size in enumerate(sizes):
        even = (lanes // size) % 2 == 0
        shorts = [f.astype(BF16) for f in found]
        lowers = [
            jnp.where(even, strips(neg, size, 2 * size, size), 0.0).astype(BF16) for neg in negs
        ]
        weights = [spread(short, diag_ref[place]) for short in shorts]
        halves = [dot(low, w).astype(BF16) for low, w in zip(lowers, weights)]
        weights = [spread(half, odd_ref[place]) for half in halves]
        corners = [dot(short, w) for short, w in zip(shorts, weights)]
        found = [
            jnp.concatenate([jnp.where(even, f, 0.0), jnp.where(even, corner, f)], axis=0)
            for f, corner in zip(found, corners)
        ]
    return found


def local_kernel(
    kheads,
    vheads,
    query_ref,
    key_ref,
    value_ref,
    rim_ref,
    taps_ref,
    gate_ref,
    logit_ref,
    rows_ref,
    local_ref,
    transit_ref,
    memory_ref,
    wide,
    state,
    diag_ref,
    odd_ref,
):
    step = pl.program_id(0)
    ratio = vheads // kheads
    span = GROUP * CHUNK
    tiles = 2 * kheads + vheads
    sizes = levels()

    @pl.when(step == 0)
    def _():
        for place, size in enumerate(sizes):
            diag_ref[place] = diagonal_mask(size).astype(BF16)
            odd_ref[place] = odd_mask(size).astype(BF16)
        rows = lax.broadcasted_iota(jnp.int32, (DK, DK + DV), 0)
        cols = lax.broadcasted_iota(jnp.int32, (DK, DK + DV), 1)
        for head in range(vheads):
            state[head] = (rows == cols).astype(F32)
        rim = rim_ref[...].astype(F32)
        for tile in range(tiles):
            wide[tile, 0:HALO] = rim[RIM - HALO :, tile * 128 : (tile + 1) * 128]

    @pl.when(step > 0)
    def _():
        for tile in range(tiles):
            wide[tile, 0:HALO] = wide[tile, span : span + HALO]

    taps = taps_ref[...].astype(F32) * 0.5

    def conv(tile):
        if tile < kheads:
            raw = query_ref[:, tile * 128 : (tile + 1) * 128]
        elif tile < 2 * kheads:
            raw = key_ref[:, (tile - kheads) * 128 : (tile - kheads + 1) * 128]
        else:
            raw = value_ref[:, (tile - 2 * kheads) * 128 : (tile - 2 * kheads + 1) * 128]
        raw = raw.astype(F32)
        wide[tile, HALO : HALO + span] = raw
        tap = taps[:, tile * 128 : (tile + 1) * 128]
        total = raw * tap[KW - 1 : KW]
        for back in range(1, KW):
            total += wide[tile, HALO - back : HALO - back + span] * tap[KW - 1 - back : KW - back]
        return (total + total * jnp.tanh(total)).astype(BF16)

    def unit(values, factor):
        values = values.astype(F32)
        scale = lax.rsqrt(jnp.sum(values * values, axis=-1, keepdims=True) + EPSILON)
        if factor != 1.0:
            scale = scale * factor
        return (values * scale).astype(BF16)

    queries = [unit(conv(tile), DK**-0.5) for tile in range(kheads)]
    keys = [unit(conv(kheads + tile), 1.0) for tile in range(kheads)]
    values = [conv(2 * kheads + tile) for tile in range(vheads)]

    rows = lax.broadcasted_iota(jnp.int32, (CHUNK, CHUNK), 0)
    cols = lax.broadcasted_iota(jnp.int32, (CHUNK, CHUNK), 1)
    lower = rows >= cols
    strict = rows > cols
    triangle = lower.astype(F32)

    items = []
    for part in range(GROUP):
        here = slice(part * CHUNK, (part + 1) * CHUNK)
        cum = jnp.dot(
            triangle,
            gate_ref[here],
            precision=lax.Precision.HIGHEST,
            preferred_element_type=F32,
        )
        cum_flat = cum.T
        beta_flat = jax.nn.sigmoid(logit_ref[here]).T
        for khead in range(kheads):
            query = queries[khead][here]
            key = keys[khead][here]
            key_flat = key.T
            grams = dot(jnp.concatenate([key, query], axis=0), key_flat)
            for which in range(ratio):
                head = khead * ratio + which
                cum_col = cum[:, head : head + 1]
                cum_row = cum_flat[head : head + 1]
                beta_row = beta_flat[head : head + 1]
                last = cum_row[:, CHUNK - 1 :]
                decays = jnp.exp(jnp.where(lower, cum_col - cum_row, -jnp.inf)) * beta_row
                growth = jnp.exp(cum_col)
                items.append(
                    dict(
                        part=part,
                        head=head,
                        neg=jnp.where(strict, -grams[:CHUNK] * decays, 0.0),
                        scores=(grams[CHUNK:] * decays).astype(BF16),
                        tail_keys=(
                            key_flat.astype(F32) * (jnp.exp(last - cum_row) * beta_row)
                        ).astype(BF16),
                        grown_keys=(key.astype(F32) * growth).astype(BF16),
                        grown_query=query.astype(F32) * growth,
                        tail=jnp.exp(last),
                    )
                )
    negs = [
        jnp.concatenate([items[i]["neg"], items[i + 1]["neg"]], axis=1)
        for i in range(0, len(items), 2)
    ]
    found = inverses(negs, diag_ref, odd_ref)
    for place, item in enumerate(items):
        side = place % 2
        part, head = item["part"], item["head"]
        here = slice(part * CHUNK, (part + 1) * CHUNK)
        inverse = found[place // 2][:, side * CHUNK : (side + 1) * CHUNK].astype(BF16)
        right = jnp.concatenate([item["grown_keys"], values[head][here]], axis=1)
        solved = dot(inverse, right).astype(BF16)
        product = dot(jnp.concatenate([item["tail_keys"], item["scores"]], axis=0), solved)
        item["erase"] = product[:CHUNK, :DK].astype(BF16)
        item["write"] = product[:CHUNK, DK:]
        item["meet"] = (item["grown_query"] - product[CHUNK:, :DK]).astype(BF16)
        item["own"] = product[CHUNK:, DK:]
    for item in items:
        part, head = item["part"], item["head"]
        here = slice(part * CHUNK, (part + 1) * CHUNK)
        there = slice(head * DV, (head + 1) * DV)
        now = state[head]
        product = dot(jnp.concatenate([item["erase"], item["meet"]], axis=0), now.astype(BF16))
        after = item["tail"] * now - product[:CHUNK]
        state[head, :, :DK] = after[:, :DK]
        state[head, :, DK:] = after[:, DK:] + item["write"]
        rows_ref[here, there] = product[CHUNK:, :DK].astype(BF16)
        local_ref[here, there] = (product[CHUNK:, DK:] + item["own"]).astype(local_ref.dtype)

    @pl.when(step == pl.num_programs(0) - 1)
    def _():
        for head in range(vheads):
            transit_ref[head] = state[head, :, :DK].astype(BF16)
            memory_ref[head] = state[head, :, DK:]


def local_pass(query_raw, key_raw, value_raw, rim, taps, gate_log, beta_logit):
    tok_count = query_raw.shape[0]
    kheads = query_raw.shape[1] // DK
    vheads = value_raw.shape[1] // DV
    tiles = 2 * kheads + vheads
    span = GROUP * CHUNK
    count = len(levels())

    def along(width):
        return pl.BlockSpec((span, width), lambda i: (i, 0))

    def whole(*shape):
        return pl.BlockSpec(shape, lambda i: (0,) * len(shape))

    def kernel(*refs):
        local_kernel(kheads, vheads, *refs)

    return pl.pallas_call(
        kernel,
        grid=(tok_count // span,),
        in_specs=[
            along(kheads * DK),
            along(kheads * DK),
            along(vheads * DV),
            whole(RIM, tiles * 128),
            whole(KW, tiles * 128),
            along(vheads),
            along(vheads),
        ],
        out_specs=[
            along(vheads * DV),
            along(vheads * DV),
            whole(vheads, DK, DK),
            whole(vheads, DK, DV),
        ],
        out_shape=[
            jax.ShapeDtypeStruct((tok_count, vheads * DV), BF16),
            jax.ShapeDtypeStruct((tok_count, vheads * DV), BF16),
            jax.ShapeDtypeStruct((vheads, DK, DK), BF16),
            jax.ShapeDtypeStruct((vheads, DK, DV), F32),
        ],
        scratch_shapes=[
            pltpu.VMEM((tiles, span + HALO, 128), F32),
            pltpu.VMEM((vheads, DK, DK + DV), F32),
            pltpu.VMEM((count, 2 * CHUNK, 2 * CHUNK), BF16),
            pltpu.VMEM((count, 2 * CHUNK, 2 * CHUNK), BF16),
        ],
        compiler_params=pltpu.CompilerParams(vmem_limit_bytes=48 * 1024 * 1024),
        name="local_pass",
    )(query_raw, key_raw, value_raw, rim, taps, gate_log, beta_logit)


def final_kernel(vheads, rows_ref, local_ref, start_ref, gain_ref, out_ref):
    gain = gain_ref[...]
    for head in range(vheads):
        there = slice(head * DV, (head + 1) * DV)
        output = dot(rows_ref[:, there], start_ref[head]) + local_ref[:, there].astype(F32)
        mean = jnp.mean(output * output, axis=-1, keepdims=True)
        out_ref[:, there] = (output * lax.rsqrt(mean + EPSILON) * gain).astype(BF16)


def final_pass(rows, local, start, gain):
    tok_count = rows.shape[0]
    vheads = start.shape[0]
    span = 256

    def along(width):
        return pl.BlockSpec((span, width), lambda i: (i, 0))

    def kernel(*refs):
        final_kernel(vheads, *refs)

    return pl.pallas_call(
        kernel,
        grid=(tok_count // span,),
        in_specs=[
            along(vheads * DV),
            along(vheads * DV),
            pl.BlockSpec((vheads, DK, DV), lambda i: (0, 0, 0)),
            pl.BlockSpec((1, DV), lambda i: (0, 0)),
        ],
        out_specs=along(vheads * DV),
        out_shape=jax.ShapeDtypeStruct((tok_count, vheads * DV), BF16),
        compiler_params=pltpu.CompilerParams(vmem_limit_bytes=32 * 1024 * 1024),
        name="final_pass",
    )(rows, local, start, gain)


def shards(
    query_raw, key_raw, value_raw, conv_query, conv_key, conv_value, gate_log, beta_logit, norm_gain
):
    rim_start = query_raw.shape[0] - RIM
    rim = passed_along(
        jnp.concatenate([query_raw[rim_start:], key_raw[rim_start:], value_raw[rim_start:]], axis=1),
        "ctx",
    )
    taps = jnp.concatenate([conv_query, conv_key, conv_value], axis=1)
    rows, local, transit, memory = local_pass(
        query_raw, key_raw, value_raw, rim, taps, gate_log, beta_logit
    )
    start = passed_along(memory.astype(BF16), "ctx")
    for _ in range(lax.axis_size("ctx") - 2):
        moved = jnp.einsum("hab,hbc->hac", transit, start, preferred_element_type=F32) + memory
        start = passed_along(moved.astype(BF16), "ctx")
    return final_pass(rows, local, start, norm_gain.reshape(1, DV))


def solution(mesh):
    return jax.shard_map(
        shards,
        mesh=mesh,
        in_specs=(
            P(("groups", "ctx"), "head"),
            P(("groups", "ctx"), "head"),
            P(("groups", "ctx"), "head"),
            P(None, "head"),
            P(None, "head"),
            P(None, "head"),
            P(("groups", "ctx"), "head"),
            P(("groups", "ctx"), "head"),
            P(),
        ),
        out_specs=P(("groups", "ctx"), "head"),
        check_vma=False,
    )
```

```python
import jax
import jax.numpy as jnp
from jax import lax
from jax.experimental import pallas as pl
from jax.experimental.pallas import tpu as pltpu
from jax.sharding import PartitionSpec as P

DK = 128
DV = 128
KW = 4
CHUNK = 128
HALF = 64
BASE = 16
HALO = 8
RIM = 16
PARTS = 2
SPAN_X = 512
SPAN_Y = 512
EPSILON = 1e-06
F32 = jnp.float32
BF16 = jnp.bfloat16
WIDE = DK + DV


def dot(left, right):
    return jnp.dot(left, right, preferred_element_type=F32)


def levels():
    sizes = []
    size = BASE
    while size < HALF:
        sizes.append(size)
        size *= 2
    return sizes


def iotas(shape):
    return lax.broadcasted_iota(jnp.int32, shape, 0), lax.broadcasted_iota(jnp.int32, shape, 1)


def fill_masks(diag_ref, odd_ref):
    rows, cols = iotas((CHUNK, CHUNK))
    for place, size in enumerate(levels()):
        diag_ref[place] = (rows // size == cols // size).astype(BF16)
        pair = rows // (2 * size) == cols // (2 * size)
        odd_ref[place] = (pair & ((rows // size) % 2 == 1)).astype(BF16)


def spread(strip, mask):
    count = CHUNK // strip.shape[0]
    return jnp.concatenate([strip] * count, axis=0) * mask


def half_inverses(negs, diag_ref, odd_ref):
    lanes = lax.broadcasted_iota(jnp.int32, (1, CHUNK), 1)

    def strips(neg, size, step, first):
        out = neg[first : first + size]
        for turn in range(1, CHUNK // step):
            start = turn * step + first
            out = jnp.where(lanes // step == turn, neg[start : start + size], out)
        return out

    rows, cols = iotas((BASE, CHUNK))
    unit = (rows == cols % BASE).astype(F32)
    powers = [strips(neg, BASE, BASE, 0) for neg in negs]
    found = [unit + power for power in powers]
    shorts = [power.astype(BF16) for power in powers]
    weights = [spread(short, diag_ref[0]) for short in shorts]
    shorts = [dot(short, weight).astype(BF16) for short, weight in zip(shorts, weights)]
    reach = 2
    while reach < BASE:
        weights = [spread(short, diag_ref[0]) for short in shorts]
        if 2 * reach >= BASE:
            found = [f + dot(f.astype(BF16), w) for f, w in zip(found, weights)]
        else:
            both = [
                dot(jnp.concatenate([s, f.astype(BF16)], axis=0), w)
                for s, f, w in zip(shorts, found, weights)
            ]
            shorts = [b[:BASE].astype(BF16) for b in both]
            found = [f + b[BASE:] for f, b in zip(found, both)]
        reach *= 2
    for place, size in enumerate(levels()):
        even = (lanes // size) % 2 == 0
        shorts = [f.astype(BF16) for f in found]
        lowers = [
            jnp.where(even, strips(neg, size, 2 * size, size), 0.0).astype(BF16) for neg in negs
        ]
        weights = [spread(short, diag_ref[place]) for short in shorts]
        middles = [dot(low, w).astype(BF16) for low, w in zip(lowers, weights)]
        weights = [spread(middle, odd_ref[place]) for middle in middles]
        corners = [dot(short, w) for short, w in zip(shorts, weights)]
        found = [
            jnp.concatenate([jnp.where(even, f, 0.0), jnp.where(even, corner, f)], axis=0)
            for f, corner in zip(found, corners)
        ]
    return [f.astype(BF16) for f in found]


def conv(raw, wide, tile, tap):
    span = raw.shape[0]
    raw = raw.astype(F32)
    wide[tile, HALO : HALO + span] = raw
    total = raw * tap[KW - 1 : KW]
    for back in range(1, KW):
        total += wide[tile, HALO - back : HALO - back + span] * tap[KW - 1 - back : KW - back]
    return (total + total * jnp.tanh(total)).astype(BF16)


def unit(values, factor):
    values = values.astype(F32)
    scale = lax.rsqrt(jnp.sum(values * values, axis=-1, keepdims=True) + EPSILON)
    if factor != 1.0:
        scale = scale * factor
    return (values * scale).astype(BF16)


def sums(gates, span):
    rows, cols = iotas((CHUNK, CHUNK))
    stacked = jnp.concatenate(
        [gates[:, at : at + CHUNK] for at in range(0, span, CHUNK)], axis=0
    )
    total = jnp.dot(
        stacked,
        (rows <= cols).astype(F32),
        precision=lax.Precision.HIGHEST,
        preferred_element_type=F32,
    )
    heads = gates.shape[0]
    return [total[at * heads : (at + 1) * heads] for at in range(span // CHUNK)]


def rim_kernel(query_ref, key_ref, value_ref, out_ref):
    first, second = query_ref.shape[1], key_ref.shape[1]
    out_ref[:, :first] = query_ref[...]
    out_ref[:, first : first + second] = key_ref[...]
    out_ref[:, first + second :] = value_ref[...]


def pack_rim(query_raw, key_raw, value_raw):
    last = query_raw.shape[0] // RIM - 1
    widths = [array.shape[1] for array in (query_raw, key_raw, value_raw)]
    return pl.pallas_call(
        rim_kernel,
        grid=(1,),
        in_specs=[pl.BlockSpec((RIM, width), lambda i: (last, 0)) for width in widths],
        out_specs=pl.BlockSpec((RIM, sum(widths)), lambda i: (0, 0)),
        out_shape=jax.ShapeDtypeStruct((RIM, sum(widths)), BF16),
        name="pack_rim",
    )(query_raw, key_raw, value_raw)


def memory_kernel(
    kheads,
    vheads,
    first_head,
    key_ref,
    value_ref,
    rim_key_ref,
    rim_value_ref,
    tap_key_ref,
    tap_value_ref,
    gate_ref,
    logit_ref,
    unit_ref,
    solved_ref,
    before_ref,
    transit_ref,
    memory_ref,
    wide,
    state,
    diag_ref,
    odd_ref,
):
    step = pl.program_id(0)
    ratio = vheads // kheads
    span = key_ref.shape[0]
    tiles = kheads + vheads

    @pl.when(step == 0)
    def _():
        fill_masks(diag_ref, odd_ref)
        rows, cols = iotas((DK, WIDE))
        for head in range(vheads):
            state[head] = (rows == cols).astype(F32)
        for tile in range(tiles):
            ref, at = (rim_key_ref, tile) if tile < kheads else (rim_value_ref, tile - kheads)
            wide[tile, 0:HALO] = ref[:, at * 128 : (at + 1) * 128].astype(F32)[RIM - HALO :]

    @pl.when(step > 0)
    def _():
        for tile in range(tiles):
            wide[tile, 0:HALO] = wide[tile, span : span + HALO]

    tap_key = tap_key_ref[...].astype(F32) * 0.5
    tap_value = tap_value_ref[...].astype(F32) * 0.5
    keys = []
    for tile in range(kheads):
        at = slice(tile * DK, (tile + 1) * DK)
        keys.append(unit(conv(key_ref[:, at], wide, tile, tap_key[:, at]), 1.0))
        unit_ref[:, at] = keys[tile]
    values = []
    for tile in range(vheads):
        at = slice(tile * DV, (tile + 1) * DV)
        values.append(conv(value_ref[:, at], wide, kheads + tile, tap_value[:, at]))

    rows, cols = iotas((CHUNK, CHUNK))
    strict = rows > cols
    cums = sums(gate_ref[...], span)
    betas = jax.nn.sigmoid(logit_ref[...])

    items = []
    for part in range(span // CHUNK):
        here = slice(part * CHUNK, (part + 1) * CHUNK)
        cum_flat = cums[part]
        cum = cum_flat.T
        for khead in range(kheads):
            key = keys[khead][here]
            key_flat = key.T
            gram = dot(key, key_flat)
            for which in range(ratio):
                head = khead * ratio + which
                place = first_head + head
                cum_col = cum[:, place : place + 1]
                cum_row = cum_flat[place : place + 1]
                beta_row = betas[place : place + 1, here]
                last = cum_row[:, CHUNK - 1 :]
                decays = jnp.exp(jnp.where(strict, cum_col - cum_row, -jnp.inf))
                items.append(
                    dict(
                        part=part,
                        head=head,
                        neg=(gram * decays) * -beta_row,
                        tail_keys=(
                            key_flat.astype(F32) * (jnp.exp(last - cum_row) * beta_row)
                        ).astype(BF16),
                        right=jnp.concatenate(
                            [
                                (key.astype(F32) * jnp.exp(cum_col)).astype(BF16),
                                values[head][here],
                            ],
                            axis=1,
                        ),
                        tail=jnp.exp(last),
                    )
                )
    found = half_inverses([item["neg"] for item in items], diag_ref, odd_ref)
    tops = [dot(f[:, :HALF], item["right"][:HALF]).astype(BF16) for f, item in zip(found, items)]
    rests = [
        (item["right"][HALF:].astype(F32) + dot(item["neg"][HALF:, :HALF].astype(BF16), top)).astype(
            BF16
        )
        for item, top in zip(items, tops)
    ]
    lows = [dot(f[:, HALF:], rest).astype(BF16) for f, rest in zip(found, rests)]
    for item, top, low in zip(items, tops, lows):
        start = item["part"] * CHUNK
        there = slice(item["head"] * WIDE, (item["head"] + 1) * WIDE)
        solved = jnp.concatenate([top, low], axis=0)
        solved_ref[start : start + CHUNK, there] = solved
        product = dot(item["tail_keys"], solved)
        item["erase"] = product[:, :DK].astype(BF16)
        item["write"] = product[:, DK:]
    for item in items:
        part, head = item["part"], item["head"]
        now = state[head]
        short = now.astype(BF16)
        before_ref[part, head] = short
        after = item["tail"] * now - dot(item["erase"], short)
        state[head, :, :DK] = after[:, :DK]
        state[head, :, DK:] = after[:, DK:] + item["write"]

    @pl.when(step == pl.num_programs(0) - 1)
    def _():
        for head in range(vheads):
            transit_ref[head] = state[head, :, :DK].astype(BF16)
            memory_ref[head] = state[head, :, DK:]


def memory_pass(part, key_raw, value_raw, rim, conv_key, conv_value, gate_flat, logit_flat):
    tok_count = key_raw.shape[0]
    all_kheads = key_raw.shape[1] // DK
    all_vheads = value_raw.shape[1] // DV
    kheads, vheads = all_kheads // PARTS, all_vheads // PARTS
    tiles = kheads + vheads
    span = min(SPAN_X, tok_count)
    chunks = tok_count // CHUNK
    count = len(levels())
    rim_key = PARTS + part
    rim_value = (2 * all_kheads) // vheads + part

    def along(width, column):
        return pl.BlockSpec((span, width), lambda i: (i, column))

    def fixed(shape, *place):
        return pl.BlockSpec(shape, lambda i: place)

    def kernel(*refs):
        memory_kernel(kheads, vheads, part * vheads, *refs)

    return pl.pallas_call(
        kernel,
        grid=(tok_count // span,),
        in_specs=[
            along(kheads * DK, part),
            along(vheads * DV, part),
            fixed((RIM, kheads * DK), 0, rim_key),
            fixed((RIM, vheads * DV), 0, rim_value),
            fixed((KW, kheads * DK), 0, part),
            fixed((KW, vheads * DV), 0, part),
            pl.BlockSpec((all_vheads, span), lambda i: (0, i)),
            pl.BlockSpec((all_vheads, span), lambda i: (0, i)),
        ],
        out_specs=[
            along(kheads * DK, 0),
            along(vheads * WIDE, 0),
            pl.BlockSpec((span // CHUNK, vheads, DK, WIDE), lambda i: (i, 0, 0, 0)),
            fixed((vheads, DK, DK), 0, 0, 0),
            fixed((vheads, DK, DV), 0, 0, 0),
        ],
        out_shape=[
            jax.ShapeDtypeStruct((tok_count, kheads * DK), BF16),
            jax.ShapeDtypeStruct((tok_count, vheads * WIDE), BF16),
            jax.ShapeDtypeStruct((chunks, vheads, DK, WIDE), BF16),
            jax.ShapeDtypeStruct((vheads, DK, DK), BF16),
            jax.ShapeDtypeStruct((vheads, DK, DV), F32),
        ],
        scratch_shapes=[
            pltpu.VMEM((tiles, span + HALO, 128), F32),
            pltpu.VMEM((vheads, DK, WIDE), F32),
            pltpu.VMEM((count, CHUNK, CHUNK), BF16),
            pltpu.VMEM((count, CHUNK, CHUNK), BF16),
        ],
        compiler_params=pltpu.CompilerParams(vmem_limit_bytes=40 * 1024 * 1024),
        cost_estimate=pl.CostEstimate(
            flops=2 * tok_count * vheads * 1000 * 1000, bytes_accessed=1 << 23, transcendentals=0
        ),
        name="memory_pass",
    )(key_raw, value_raw, rim, rim, conv_key, conv_value, gate_flat, logit_flat)


def rows_kernel(
    kheads,
    vheads,
    first_head,
    query_ref,
    rim_ref,
    tap_ref,
    key_ref,
    gate_ref,
    logit_ref,
    solved_ref,
    before_ref,
    rows_ref,
    local_ref,
    wide,
):
    step = pl.program_id(0)
    ratio = vheads // kheads
    span = query_ref.shape[0]

    @pl.when(step == 0)
    def _():
        for tile in range(kheads):
            wide[tile, 0:HALO] = rim_ref[:, tile * DK : (tile + 1) * DK].astype(F32)[RIM - HALO :]

    @pl.when(step > 0)
    def _():
        for tile in range(kheads):
            wide[tile, 0:HALO] = wide[tile, span : span + HALO]

    taps = tap_ref[...].astype(F32) * 0.5
    queries = []
    for tile in range(kheads):
        at = slice(tile * DK, (tile + 1) * DK)
        queries.append(unit(conv(query_ref[:, at], wide, tile, taps[:, at]), DK**-0.5))

    rows, cols = iotas((CHUNK, CHUNK))
    lower = rows >= cols
    cums = sums(gate_ref[...], span)
    betas = jax.nn.sigmoid(logit_ref[...])
    for part in range(span // CHUNK):
        here = slice(part * CHUNK, (part + 1) * CHUNK)
        cum_flat = cums[part]
        cum = cum_flat.T
        for khead in range(kheads):
            query = queries[khead][here]
            gram = lax.dot_general(
                query,
                key_ref[here, khead * DK : (khead + 1) * DK],
                (((1,), (1,)), ((), ())),
                preferred_element_type=F32,
            )
            for which in range(ratio):
                head = khead * ratio + which
                place = first_head + head
                there = slice(head * DV, (head + 1) * DV)
                cum_col = cum[:, place : place + 1]
                cum_row = cum_flat[place : place + 1]
                decays = jnp.exp(jnp.where(lower, cum_col - cum_row, -jnp.inf))
                scores = (gram * decays * betas[place : place + 1, here]).astype(BF16)
                product = dot(scores, solved_ref[here, head * WIDE : (head + 1) * WIDE])
                meet = query.astype(F32) * jnp.exp(cum_col) - product[:, :DK]
                final = dot(meet.astype(BF16), before_ref[part, head])
                rows_ref[here, there] = final[:, :DK].astype(BF16)
                local_ref[here, there] = (final[:, DK:] + product[:, DK:]).astype(BF16)


def rows_pass(part, query_raw, rim, conv_query, keys, gate_flat, logit_flat, solved, before):
    tok_count = query_raw.shape[0]
    kheads = query_raw.shape[1] // DK // PARTS
    all_vheads = gate_flat.shape[0]
    vheads = all_vheads // PARTS
    span = min(SPAN_Y, tok_count)

    def along(width, column):
        return pl.BlockSpec((span, width), lambda i: (i, column))

    def kernel(*refs):
        rows_kernel(kheads, vheads, part * vheads, *refs)

    return pl.pallas_call(
        kernel,
        grid=(tok_count // span,),
        in_specs=[
            along(kheads * DK, part),
            pl.BlockSpec((RIM, kheads * DK), lambda i: (0, part)),
            pl.BlockSpec((KW, kheads * DK), lambda i: (0, part)),
            along(kheads * DK, 0),
            pl.BlockSpec((all_vheads, span), lambda i: (0, i)),
            pl.BlockSpec((all_vheads, span), lambda i: (0, i)),
            along(vheads * WIDE, 0),
            pl.BlockSpec((span // CHUNK, vheads, DK, WIDE), lambda i: (i, 0, 0, 0)),
        ],
        out_specs=[along(vheads * DV, 0), along(vheads * DV, 0)],
        out_shape=[
            jax.ShapeDtypeStruct((tok_count, vheads * DV), BF16),
            jax.ShapeDtypeStruct((tok_count, vheads * DV), BF16),
        ],
        scratch_shapes=[pltpu.VMEM((kheads, span + HALO, 128), F32)],
        compiler_params=pltpu.CompilerParams(vmem_limit_bytes=32 * 1024 * 1024),
        cost_estimate=pl.CostEstimate(
            flops=2 * tok_count * vheads * 1000 * 500, bytes_accessed=1 << 23, transcendentals=0
        ),
        name="rows_pass",
    )(query_raw, rim, conv_query, keys, gate_flat, logit_flat, solved, before)


def final_kernel(vheads, rows_ref, local_ref, early_ref, late_ref, gain_ref, *rest):
    out_ref = rest[-1]
    gain = gain_ref[...]
    for head in range(vheads):
        there = slice(head * DV, (head + 1) * DV)
        start = early_ref[head] + late_ref[head]
        output = dot(rows_ref[:, there], start) + local_ref[:, there].astype(F32)
        mean = jnp.mean(output * output, axis=-1, keepdims=True)
        out_ref[:, there] = (output * lax.rsqrt(mean + EPSILON) * gain).astype(BF16)


def final_pass(part, rows, local, early, late, gain, earlier):
    tok_count = rows.shape[0]
    vheads = early.shape[0]
    span = min(256, tok_count)

    def along(width, column):
        return pl.BlockSpec((span, width), lambda i: (i, column))

    def kernel(*refs):
        final_kernel(vheads, *refs)

    whole = pl.BlockSpec((vheads, DK, DV), lambda i: (0, 0, 0))
    arrays = [rows, local, early, late, gain]
    specs = [
        along(vheads * DV, 0),
        along(vheads * DV, 0),
        whole,
        whole,
        pl.BlockSpec((1, DV), lambda i: (0, 0)),
    ]
    if earlier is not None:
        arrays.append(earlier)
        specs.append(pl.BlockSpec(memory_space=pl.ANY))
    return pl.pallas_call(
        kernel,
        grid=(tok_count // span,),
        in_specs=specs,
        out_specs=along(vheads * DV, part),
        out_shape=jax.ShapeDtypeStruct((tok_count, PARTS * vheads * DV), BF16),
        input_output_aliases={} if earlier is None else {5: 0},
        compiler_params=pltpu.CompilerParams(vmem_limit_bytes=32 * 1024 * 1024),
        name="final_pass",
    )(*arrays)


def shards(
    query_raw, key_raw, value_raw, conv_query, conv_key, conv_value, gate_log, beta_logit, norm_gain
):
    count = lax.axis_size("ctx")
    rim = lax.ppermute(
        pack_rim(query_raw, key_raw, value_raw), "ctx", [(at, at + 1) for at in range(count - 1)]
    )
    gate_flat, logit_flat = gate_log.T, beta_logit.T
    gain = norm_gain.reshape(1, DV)
    first = [
        memory_pass(part, key_raw, value_raw, rim, conv_key, conv_value, gate_flat, logit_flat)
        for part in range(PARTS)
    ]
    second, early, late = [], [], []
    for part in range(PARTS):
        keys, solved, before, transit, memory = first[part]
        second.append(
            rows_pass(
                part, query_raw, rim, conv_query, keys, gate_flat, logit_flat, solved, before
            )
        )
        got = lax.ppermute(memory.astype(BF16), "ctx", [(0, 1)])
        total = jnp.zeros_like(got)
        for source in range(1, count - 1):
            total = total + got
            moved = jnp.einsum("hab,hbc->hac", transit, got, preferred_element_type=F32) + memory
            got = lax.ppermute(moved.astype(BF16), "ctx", [(source, source + 1)])
        early.append(total)
        late.append(got)
    out = None
    for part in range(PARTS):
        rows, local = second[part]
        out = final_pass(part, rows, local, early[part], late[part], gain, out)
    return out


def solution(mesh):
    return jax.shard_map(
        shards,
        mesh=mesh,
        in_specs=(
            P(("groups", "ctx"), "head"),
            P(("groups", "ctx"), "head"),
            P(("groups", "ctx"), "head"),
            P(None, "head"),
            P(None, "head"),
            P(None, "head"),
            P(("groups", "ctx"), "head"),
            P(("groups", "ctx"), "head"),
            P(),
        ),
        out_specs=P(("groups", "ctx"), "head"),
        check_vma=False,
    )
```

```python
import jax
import jax.numpy as jnp
from jax import lax
from jax.experimental import pallas as pl
from jax.experimental.pallas import tpu as pltpu
from jax.sharding import PartitionSpec as P

DK = 128
DV = 128
KW = 4
CHUNK = 128
HALF = 64
BASE = 8
HALO = 8
RIM = 16
PARTS = 2
SPAN_X = 512
SPAN_Y = 512
EPSILON = 1e-06
LOG2E = 1.4426950408889634
F32 = jnp.float32
BF16 = jnp.bfloat16
WIDE = DK + DV


def dot(left, right):
    return jnp.dot(left, right, preferred_element_type=F32)


def levels():
    sizes = []
    size = BASE
    while size < HALF:
        sizes.append(size)
        size *= 2
    return sizes


def iotas(shape):
    return lax.broadcasted_iota(jnp.int32, shape, 0), lax.broadcasted_iota(jnp.int32, shape, 1)


def fill_masks(diag_ref):
    rows, cols = iotas((CHUNK, CHUNK))
    for place, size in enumerate(levels()):
        diag_ref[place] = (rows // size == cols // size).astype(BF16)


def packed(strip):
    if strip.shape[0] < 16:
        strip = jnp.concatenate([strip] * (16 // strip.shape[0]), axis=0)
    return strip.astype(BF16)


def spread(strip, mask):
    count = CHUNK // strip.shape[0]
    return jnp.concatenate([strip] * count, axis=0) * mask


def strips(neg, size, step, first):
    lanes = lax.broadcasted_iota(jnp.int32, (1, CHUNK), 1)
    out = neg[first : first + size]
    for turn in range(1, CHUNK // step):
        start = turn * step + first
        out = jnp.where(lanes // step == turn, neg[start : start + size], out)
    return out


def substitute(strip):
    rows, cols = iotas((8, CHUNK))
    halves = [strip[at : at + 8] for at in range(0, BASE, 8)]
    found = [(rows + at == cols % BASE).astype(F32) for at in range(0, BASE, 8)]
    for row in range(BASE - 1):
        at = cols // BASE * BASE + row
        solved = found[row // 8][row % 8 : row % 8 + 1]
        for half in range((row + 1) // 8, BASE // 8):
            column = jnp.take_along_axis(halves[half], at, axis=1)
            found[half] = found[half] + column * solved
    return jnp.concatenate(found, axis=0)


def half_inverses(negs, diag_ref):
    lanes = lax.broadcasted_iota(jnp.int32, (1, CHUNK), 1)
    found = [substitute(strips(neg, BASE, BASE, 0)) for neg in negs]
    pairs = range(0, len(negs), 2)
    for place, size in enumerate(levels()):
        even = (lanes // size) % 2 == 0

        def up(value):
            return pltpu.roll(value, size, 1)

        def down(value):
            return pltpu.roll(value, CHUNK - size, 1)

        lowers = [strips(neg, size, 2 * size, size) for neg in negs]
        evens = [packed(jnp.where(even, found[i], up(found[i + 1]))) for i in pairs]
        odds = [packed(jnp.where(even, down(found[i]), found[i + 1])) for i in pairs]
        both = [packed(jnp.where(even, lowers[i], up(lowers[i + 1]))) for i in pairs]
        weights = [spread(value, diag_ref[place]) for value in evens]
        middles = [dot(value, weight).astype(BF16) for value, weight in zip(both, weights)]
        weights = [spread(value, diag_ref[place]) for value in middles]
        corners = [dot(value, weight)[:size] for value, weight in zip(odds, weights)]
        wider = []
        for i, f in enumerate(found):
            corner = corners[i // 2] if i % 2 == 0 else down(corners[i // 2])
            wider.append(
                jnp.concatenate([jnp.where(even, f, 0.0), jnp.where(even, corner, f)], axis=0)
            )
        found = wider
    return [f.astype(BF16) for f in found]


def conv(raw, wide, tile, tap):
    span = raw.shape[0]
    raw = raw.astype(F32)
    wide[tile, HALO : HALO + span] = raw
    total = raw * tap[KW - 1 : KW]
    for back in range(1, KW):
        total += wide[tile, HALO - back : HALO - back + span] * tap[KW - 1 - back : KW - back]
    return (total + total * jnp.tanh(total)).astype(BF16)


def row_sums(values):
    return dot(values.astype(BF16), jnp.ones((values.shape[1], values.shape[1]), BF16))


def unit(values, factor):
    values = values.astype(F32)
    scale = lax.rsqrt(jnp.sum(values * values, axis=-1, keepdims=True) + EPSILON)
    if factor != 1.0:
        scale = scale * factor
    return (values * scale).astype(BF16)


def sums(gates, span):
    rows, cols = iotas((CHUNK, CHUNK))
    stacked = jnp.concatenate(
        [gates[:, at : at + CHUNK] for at in range(0, span, CHUNK)], axis=0
    )
    total = jnp.dot(
        stacked,
        (rows <= cols).astype(F32),
        precision=lax.Precision.HIGHEST,
        preferred_element_type=F32,
    )
    heads = gates.shape[0]
    return [total[at * heads : (at + 1) * heads] for at in range(span // CHUNK)]


def rim_kernel(query_ref, key_ref, value_ref, out_ref):
    first, second = query_ref.shape[1], key_ref.shape[1]
    out_ref[:, :first] = query_ref[...]
    out_ref[:, first : first + second] = key_ref[...]
    out_ref[:, first + second :] = value_ref[...]


def pack_rim(query_raw, key_raw, value_raw):
    last = query_raw.shape[0] // RIM - 1
    widths = [array.shape[1] for array in (query_raw, key_raw, value_raw)]
    return pl.pallas_call(
        rim_kernel,
        grid=(1,),
        in_specs=[pl.BlockSpec((RIM, width), lambda i: (last, 0)) for width in widths],
        out_specs=pl.BlockSpec((RIM, sum(widths)), lambda i: (0, 0)),
        out_shape=jax.ShapeDtypeStruct((RIM, sum(widths)), BF16),
        name="pack_rim",
    )(query_raw, key_raw, value_raw)


def log_weights(logit):
    return (jnp.minimum(logit, 0.0) - jnp.log(1.0 + jnp.exp(-jnp.abs(logit)))) * LOG2E


def memory_kernel(
    kheads,
    vheads,
    first_head,
    key_ref,
    value_ref,
    rim_key_ref,
    rim_value_ref,
    tap_key_ref,
    tap_value_ref,
    gate_ref,
    logit_ref,
    unit_ref,
    solved_ref,
    before_ref,
    transit_ref,
    memory_ref,
    wide,
    state,
    diag_ref,
    neg_ref,
    tail_ref,
    right_ref,
    sum_ref,
):
    step = pl.program_id(0)
    last_step = pl.num_programs(0) - 1
    ratio = vheads // kheads
    span = key_ref.shape[0]
    tiles = kheads + vheads
    parts = span // CHUNK
    places = [(part, head) for part in range(parts) for head in range(vheads)]

    def set_up():
        fill_masks(diag_ref)
        rows, cols = iotas((DK, WIDE))
        for head in range(vheads):
            state[head] = (rows == cols).astype(F32)
        for tile in range(tiles):
            ref, at = (rim_key_ref, tile) if tile < kheads else (rim_value_ref, tile - kheads)
            wide[tile, 0:HALO] = ref[:, at * 128 : (at + 1) * 128].astype(F32)[RIM - HALO :]

    def prepare():
        tap_key = tap_key_ref[...].astype(F32) * 0.5
        tap_value = tap_value_ref[...].astype(F32) * 0.5
        keys = []
        for tile in range(kheads):
            at = slice(tile * DK, (tile + 1) * DK)
            keys.append(unit(conv(key_ref[:, at], wide, tile, tap_key[:, at]), 1.0))
            unit_ref[:, at] = keys[tile]
        for tile in range(vheads):
            at = slice(tile * DV, (tile + 1) * DV)
            value = conv(value_ref[:, at], wide, kheads + tile, tap_value[:, at])
            for part in range(parts):
                right_ref[part * vheads + tile, :, DK:] = value[
                    part * CHUNK : (part + 1) * CHUNK
                ]
        for tile in range(tiles):
            wide[tile, 0:HALO] = wide[tile, span : span + HALO]
        rows, cols = iotas((CHUNK, CHUNK))
        strict = rows > cols
        cums = sums(gate_ref[...] * LOG2E, span)
        strengths = log_weights(logit_ref[...])
        for part in range(parts):
            here = slice(part * CHUNK, (part + 1) * CHUNK)
            cum_flat = cums[part]
            cum = cum_flat.T
            lift = strengths[:, here] - cum_flat
            last = cum_flat[:, CHUNK - 1 :]
            ends = jnp.exp2(last + lift)
            sum_ref[part] = jnp.broadcast_to(jnp.exp2(last), cum_flat.shape)
            for khead in range(kheads):
                key = keys[khead][here]
                flat = (-key).T
                gram = dot(key, flat)
                for which in range(ratio):
                    head = khead * ratio + which
                    item = part * vheads + head
                    place = first_head + head
                    cum_col = jnp.broadcast_to(cum[:, place : place + 1], (CHUNK, CHUNK))
                    powers = cum_col + lift[place : place + 1]
                    decays = jnp.exp2(jnp.where(strict, powers, -jnp.inf))
                    neg_ref[item] = gram * decays
                    tail_ref[item] = flat * ends[place : place + 1].astype(BF16)
                    right_ref[item, :, :DK] = key * jnp.exp2(cum_col).astype(BF16)

    def finish():
        negs = [neg_ref[item] for item in range(len(places))]
        found = half_inverses(negs, diag_ref)
        tops = [
            dot(f[:, :HALF], right_ref[item, :HALF]).astype(BF16)
            for item, f in enumerate(found)
        ]
        rests = [
            (
                right_ref[item, HALF:].astype(F32)
                + dot(neg_ref[item, HALF:, :HALF].astype(BF16), top)
            ).astype(BF16)
            for item, top in enumerate(tops)
        ]
        lows = [dot(f[:, HALF:], rest).astype(BF16) for f, rest in zip(found, rests)]
        erases, writes = [], []
        for item, (part, head) in enumerate(places):
            there = slice(head * WIDE, (head + 1) * WIDE)
            solved = jnp.concatenate([tops[item], lows[item]], axis=0)
            solved_ref[part * CHUNK : (part + 1) * CHUNK, there] = solved
            product = dot(tail_ref[item], solved)
            erases.append(product[:, :DK].astype(BF16))
            writes.append(product[:, DK:])
        for item, (part, head) in enumerate(places):
            now = state[head]
            short = now.astype(BF16)
            before_ref[part, head] = short
            tail = sum_ref[part, first_head + head : first_head + head + 1]
            change = dot(erases[item], short)
            state[head, :, :DK] = now[:, :DK] * tail + change[:, :DK]
            state[head, :, DK:] = now[:, DK:] * tail + (change[:, DK:] - writes[item])

    @pl.when(step == 0)
    def _():
        set_up()

    prepare()
    finish()

    @pl.when(step == last_step)
    def _():
        for head in range(vheads):
            transit_ref[head] = state[head, :, :DK].astype(BF16)
            memory_ref[head] = state[head, :, DK:]


def memory_pass(part, key_raw, value_raw, rim, conv_key, conv_value, gate_flat, logit_flat):
    tok_count = key_raw.shape[0]
    all_kheads = key_raw.shape[1] // DK
    all_vheads = value_raw.shape[1] // DV
    kheads, vheads = all_kheads // PARTS, all_vheads // PARTS
    tiles = kheads + vheads
    span = min(SPAN_X, tok_count)
    chunks = tok_count // CHUNK
    items = span // CHUNK * vheads
    blocks = tok_count // span
    count = len(levels())
    rim_key = PARTS + part
    rim_value = (2 * all_kheads) // vheads + part

    def ahead(width, column):
        return pl.BlockSpec((span, width), lambda i: (i, column))

    def fixed(shape, *place):
        return pl.BlockSpec(shape, lambda i: place)

    flat = pl.BlockSpec((all_vheads, span), lambda i: (0, i))

    def kernel(*refs):
        memory_kernel(kheads, vheads, part * vheads, *refs)

    return pl.pallas_call(
        kernel,
        grid=(blocks,),
        in_specs=[
            ahead(kheads * DK, part),
            ahead(vheads * DV, part),
            fixed((RIM, kheads * DK), 0, rim_key),
            fixed((RIM, vheads * DV), 0, rim_value),
            fixed((KW, kheads * DK), 0, part),
            fixed((KW, vheads * DV), 0, part),
            flat,
            flat,
        ],
        out_specs=[
            ahead(kheads * DK, 0),
            pl.BlockSpec((span, vheads * WIDE), lambda i: (i, 0)),
            pl.BlockSpec(
                (span // CHUNK, vheads, DK, WIDE), lambda i: (i, 0, 0, 0)
            ),
            fixed((vheads, DK, DK), 0, 0, 0),
            fixed((vheads, DK, DV), 0, 0, 0),
        ],
        out_shape=[
            jax.ShapeDtypeStruct((tok_count, kheads * DK), BF16),
            jax.ShapeDtypeStruct((tok_count, vheads * WIDE), BF16),
            jax.ShapeDtypeStruct((chunks, vheads, DK, WIDE), BF16),
            jax.ShapeDtypeStruct((vheads, DK, DK), BF16),
            jax.ShapeDtypeStruct((vheads, DK, DV), F32),
        ],
        scratch_shapes=[
            pltpu.VMEM((tiles, span + HALO, 128), F32),
            pltpu.VMEM((vheads, DK, WIDE), F32),
            pltpu.VMEM((count, CHUNK, CHUNK), BF16),
            pltpu.VMEM((items, CHUNK, CHUNK), F32),
            pltpu.VMEM((items, CHUNK, CHUNK), BF16),
            pltpu.VMEM((items, CHUNK, WIDE), BF16),
            pltpu.VMEM((span // CHUNK, all_vheads, CHUNK), F32),
        ],
        compiler_params=pltpu.CompilerParams(vmem_limit_bytes=40 * 1024 * 1024),
        cost_estimate=pl.CostEstimate(
            flops=2 * tok_count * vheads * 1000 * 1000, bytes_accessed=1 << 23, transcendentals=0
        ),
        name="memory_pass",
    )(key_raw, value_raw, rim, rim, conv_key, conv_value, gate_flat, logit_flat)


def rows_kernel(
    kheads,
    vheads,
    first_head,
    query_ref,
    rim_ref,
    tap_ref,
    key_ref,
    gate_ref,
    logit_ref,
    solved_ref,
    before_ref,
    rows_ref,
    local_ref,
    wide,
):
    step = pl.program_id(0)
    ratio = vheads // kheads
    span = query_ref.shape[0]

    @pl.when(step == 0)
    def _():
        for tile in range(kheads):
            wide[tile, 0:HALO] = rim_ref[:, tile * DK : (tile + 1) * DK].astype(F32)[RIM - HALO :]

    @pl.when(step > 0)
    def _():
        for tile in range(kheads):
            wide[tile, 0:HALO] = wide[tile, span : span + HALO]

    taps = tap_ref[...].astype(F32) * 0.5
    queries = []
    for tile in range(kheads):
        at = slice(tile * DK, (tile + 1) * DK)
        queries.append(unit(conv(query_ref[:, at], wide, tile, taps[:, at]), DK**-0.5))

    rows, cols = iotas((CHUNK, CHUNK))
    lower = rows >= cols
    cums = sums(gate_ref[...] * LOG2E, span)
    strengths = log_weights(logit_ref[...])
    for part in range(span // CHUNK):
        here = slice(part * CHUNK, (part + 1) * CHUNK)
        cum_flat = cums[part]
        cum = cum_flat.T
        lift = strengths[:, here] - cum_flat
        for khead in range(kheads):
            query = queries[khead][here]
            gram = lax.dot_general(
                query,
                key_ref[here, khead * DK : (khead + 1) * DK],
                (((1,), (1,)), ((), ())),
                preferred_element_type=F32,
            )
            for which in range(ratio):
                head = khead * ratio + which
                place = first_head + head
                there = slice(head * DV, (head + 1) * DV)
                cum_col = jnp.broadcast_to(cum[:, place : place + 1], (CHUNK, CHUNK))
                powers = cum_col + lift[place : place + 1]
                scores = (gram * jnp.exp2(jnp.where(lower, powers, -jnp.inf))).astype(BF16)
                product = dot(scores, solved_ref[here, head * WIDE : (head + 1) * WIDE])
                meet = query.astype(F32) * jnp.exp2(cum_col) - product[:, :DK]
                final = dot(meet.astype(BF16), before_ref[part, head])
                rows_ref[here, there] = final[:, :DK].astype(BF16)
                local_ref[here, there] = (final[:, DK:] + product[:, DK:]).astype(BF16)


def rows_pass(part, query_raw, rim, conv_query, keys, gate_flat, logit_flat, solved, before):
    tok_count = query_raw.shape[0]
    kheads = query_raw.shape[1] // DK // PARTS
    all_vheads = gate_flat.shape[0]
    vheads = all_vheads // PARTS
    span = min(SPAN_Y, tok_count)

    def along(width, column):
        return pl.BlockSpec((span, width), lambda i: (i, column))

    def kernel(*refs):
        rows_kernel(kheads, vheads, part * vheads, *refs)

    return pl.pallas_call(
        kernel,
        grid=(tok_count // span,),
        in_specs=[
            along(kheads * DK, part),
            pl.BlockSpec((RIM, kheads * DK), lambda i: (0, part)),
            pl.BlockSpec((KW, kheads * DK), lambda i: (0, part)),
            along(kheads * DK, 0),
            pl.BlockSpec((all_vheads, span), lambda i: (0, i)),
            pl.BlockSpec((all_vheads, span), lambda i: (0, i)),
            along(vheads * WIDE, 0),
            pl.BlockSpec((span // CHUNK, vheads, DK, WIDE), lambda i: (i, 0, 0, 0)),
        ],
        out_specs=[along(vheads * DV, 0), along(vheads * DV, 0)],
        out_shape=[
            jax.ShapeDtypeStruct((tok_count, vheads * DV), BF16),
            jax.ShapeDtypeStruct((tok_count, vheads * DV), BF16),
        ],
        scratch_shapes=[pltpu.VMEM((kheads, span + HALO, 128), F32)],
        compiler_params=pltpu.CompilerParams(vmem_limit_bytes=32 * 1024 * 1024),
        cost_estimate=pl.CostEstimate(
            flops=2 * tok_count * vheads * 1000 * 500, bytes_accessed=1 << 23, transcendentals=0
        ),
        name="rows_pass",
    )(query_raw, rim, conv_query, keys, gate_flat, logit_flat, solved, before)


def final_kernel(vheads, rows_ref, local_ref, early_ref, late_ref, gain_ref, *rest):
    out_ref = rest[-1]
    gain = gain_ref[...]
    for head in range(vheads):
        there = slice(head * DV, (head + 1) * DV)
        start = early_ref[head] + late_ref[head]
        output = dot(rows_ref[:, there], start) + local_ref[:, there].astype(F32)
        square = output * output
        if head % 2:
            total = row_sums(square)
        else:
            total = jnp.sum(square, axis=-1, keepdims=True)
        mean = total * (1.0 / DV)
        out_ref[:, there] = (output * lax.rsqrt(mean + EPSILON) * gain).astype(BF16)


def final_pass(part, rows, local, early, late, gain, earlier):
    tok_count = rows.shape[0]
    vheads = early.shape[0]
    span = min(512, tok_count)

    def along(width, column):
        return pl.BlockSpec((span, width), lambda i: (i, column))

    def kernel(*refs):
        final_kernel(vheads, *refs)

    whole = pl.BlockSpec((vheads, DK, DV), lambda i: (0, 0, 0))
    arrays = [rows, local, early, late, gain]
    specs = [
        along(vheads * DV, 0),
        along(vheads * DV, 0),
        whole,
        whole,
        pl.BlockSpec((1, DV), lambda i: (0, 0)),
    ]
    if earlier is not None:
        arrays.append(earlier)
        specs.append(pl.BlockSpec(memory_space=pl.ANY))
    return pl.pallas_call(
        kernel,
        grid=(tok_count // span,),
        in_specs=specs,
        out_specs=along(vheads * DV, part),
        out_shape=jax.ShapeDtypeStruct((tok_count, PARTS * vheads * DV), BF16),
        input_output_aliases={} if earlier is None else {5: 0},
        compiler_params=pltpu.CompilerParams(vmem_limit_bytes=32 * 1024 * 1024),
        name="final_pass",
    )(*arrays)


def shards(
    query_raw, key_raw, value_raw, conv_query, conv_key, conv_value, gate_log, beta_logit, norm_gain
):
    count = lax.axis_size("ctx")
    rim = lax.ppermute(
        pack_rim(query_raw, key_raw, value_raw), "ctx", [(at, at + 1) for at in range(count - 1)]
    )
    gate_flat, logit_flat = gate_log.T, beta_logit.T
    gain = norm_gain.reshape(1, DV)
    first = [
        memory_pass(part, key_raw, value_raw, rim, conv_key, conv_value, gate_flat, logit_flat)
        for part in range(PARTS)
    ]
    def after(value, *others):
        return lax.optimization_barrier((value, *others))[0]

    moved = [[found[4].astype(BF16)] for found in first]
    got = [[] for _ in first]
    second = [None] * PARTS

    def send(part):
        source = len(got[part])
        got[part].append(lax.ppermute(moved[part][source], "ctx", [(source, source + 1)]))

    def carry(part, *others):
        transit, memory = first[part][3:]
        arrived = after(got[part][-1], *others)
        ahead = jnp.einsum("hab,hbc->hac", transit, arrived, preferred_element_type=F32)
        moved[part].append((ahead + memory).astype(BF16))

    def rows_of(part, *others):
        keys, solved, before = first[part][:3]
        second[part] = rows_pass(
            part,
            query_raw,
            rim,
            conv_query,
            keys,
            gate_flat,
            logit_flat,
            after(solved, *others),
            before,
        )

    for turn in range(count - 1):
        for part in range(PARTS):
            send(part)
            if turn + 1 < count - 1:
                waits = [] if part == 0 or turn >= PARTS else [second[turn][1]]
                carry(part, *waits)
            if part == 0 and turn < PARTS:
                ready = [moved[part][-1] for part in range(PARTS)]
                rows_of(turn, *ready)
    out = None
    for part in range(PARTS):
        rows, local = second[part]
        early = sum(got[part][:-1], jnp.zeros_like(got[part][-1]))
        late = got[part][-1]
        if part + 1 < PARTS:
            late = after(late, moved[part + 1][-1])
        out = final_pass(part, rows, local, early, late, gain, out)
    return out


def solution(mesh):
    return jax.shard_map(
        shards,
        mesh=mesh,
        in_specs=(
            P(("groups", "ctx"), "head"),
            P(("groups", "ctx"), "head"),
            P(("groups", "ctx"), "head"),
            P(None, "head"),
            P(None, "head"),
            P(None, "head"),
            P(("groups", "ctx"), "head"),
            P(("groups", "ctx"), "head"),
            P(),
        ),
        out_specs=P(("groups", "ctx"), "head"),
        check_vma=False,
    )
```

```python
import jax
import jax.numpy as jnp
from jax import lax
from jax.experimental import pallas as pl
from jax.experimental.pallas import tpu as pltpu
from jax.sharding import PartitionSpec as P

DK = 128
DV = 128
KW = 4
CHUNK = 128
HALF = 64
BASE = 8
HALO = 8
RIM = 16
PARTS = 2
SPAN_X = 512
SPAN_Y = 512
EPSILON = 1e-06
LOG2E = 1.4426950408889634
F32 = jnp.float32
BF16 = jnp.bfloat16
WIDE = DK + DV
VMEM = pl.BlockSpec(memory_space=pltpu.VMEM)


def dot(left, right):
    return jnp.dot(left, right, preferred_element_type=F32)


def levels():
    sizes = []
    size = BASE
    while size < HALF:
        sizes.append(size)
        size *= 2
    return sizes


def iotas(shape):
    return lax.broadcasted_iota(jnp.int32, shape, 0), lax.broadcasted_iota(jnp.int32, shape, 1)


def fill_masks(diag_ref):
    rows, cols = iotas((CHUNK, CHUNK))
    for place, size in enumerate(levels()):
        diag_ref[place] = (rows // size == cols // size).astype(BF16)


def packed(strip):
    if strip.shape[0] < 16:
        strip = jnp.concatenate([strip] * (16 // strip.shape[0]), axis=0)
    return strip.astype(BF16)


def spread(strip, mask):
    count = CHUNK // strip.shape[0]
    return jnp.concatenate([strip] * count, axis=0) * mask


def strips(neg, size, step, first):
    lanes = lax.broadcasted_iota(jnp.int32, (1, CHUNK), 1)
    out = neg[first : first + size]
    for turn in range(1, CHUNK // step):
        start = turn * step + first
        out = jnp.where(lanes // step == turn, neg[start : start + size], out)
    return out


def substitute(strip):
    rows, cols = iotas((8, CHUNK))
    halves = [strip[at : at + 8] for at in range(0, BASE, 8)]
    found = [(rows + at == cols % BASE).astype(F32) for at in range(0, BASE, 8)]
    for row in range(BASE - 1):
        at = cols // BASE * BASE + row
        solved = found[row // 8][row % 8 : row % 8 + 1]
        for half in range((row + 1) // 8, BASE // 8):
            column = jnp.take_along_axis(halves[half], at, axis=1)
            found[half] = found[half] + column * solved
    return jnp.concatenate(found, axis=0)


def half_inverses(negs, diag_ref):
    lanes = lax.broadcasted_iota(jnp.int32, (1, CHUNK), 1)
    found = [substitute(strips(neg, BASE, BASE, 0)) for neg in negs]
    pairs = range(0, len(negs), 2)
    for place, size in enumerate(levels()):
        even = (lanes // size) % 2 == 0

        def up(value):
            return pltpu.roll(value, size, 1)

        def down(value):
            return pltpu.roll(value, CHUNK - size, 1)

        lowers = [strips(neg, size, 2 * size, size) for neg in negs]
        evens = [packed(jnp.where(even, found[i], up(found[i + 1]))) for i in pairs]
        odds = [packed(jnp.where(even, down(found[i]), found[i + 1])) for i in pairs]
        both = [packed(jnp.where(even, lowers[i], up(lowers[i + 1]))) for i in pairs]
        weights = [spread(value, diag_ref[place]) for value in evens]
        middles = [dot(value, weight).astype(BF16) for value, weight in zip(both, weights)]
        weights = [spread(value, diag_ref[place]) for value in middles]
        corners = [dot(value, weight)[:size] for value, weight in zip(odds, weights)]
        wider = []
        for i, f in enumerate(found):
            corner = corners[i // 2] if i % 2 == 0 else down(corners[i // 2])
            wider.append(
                jnp.concatenate([jnp.where(even, f, 0.0), jnp.where(even, corner, f)], axis=0)
            )
        found = wider
    return [f.astype(BF16) for f in found]


def conv(raw, wide, tile, tap):
    span = raw.shape[0]
    raw = raw.astype(F32)
    wide[tile, HALO : HALO + span] = raw
    total = raw * tap[KW - 1 : KW]
    for back in range(1, KW):
        total += wide[tile, HALO - back : HALO - back + span] * tap[KW - 1 - back : KW - back]
    return (total + total * jnp.tanh(total)).astype(BF16)


def row_sums(values):
    return dot(values.astype(BF16), jnp.ones((values.shape[1], values.shape[1]), BF16))


def unit(values, factor):
    values = values.astype(F32)
    scale = lax.rsqrt(jnp.sum(values * values, axis=-1, keepdims=True) + EPSILON)
    if factor != 1.0:
        scale = scale * factor
    return (values * scale).astype(BF16)


def sums(gates, span):
    rows, cols = iotas((CHUNK, CHUNK))
    stacked = jnp.concatenate(
        [gates[:, at : at + CHUNK] for at in range(0, span, CHUNK)], axis=0
    )
    total = jnp.dot(
        stacked,
        (rows <= cols).astype(F32),
        precision=lax.Precision.HIGHEST,
        preferred_element_type=F32,
    )
    heads = gates.shape[0]
    return [total[at * heads : (at + 1) * heads] for at in range(span // CHUNK)]


def rim_kernel(query_ref, key_ref, value_ref, out_ref):
    first, second = query_ref.shape[1], key_ref.shape[1]
    out_ref[:, :first] = query_ref[...]
    out_ref[:, first : first + second] = key_ref[...]
    out_ref[:, first + second :] = value_ref[...]


def pack_rim(query_raw, key_raw, value_raw):
    last = query_raw.shape[0] // RIM - 1
    widths = [array.shape[1] for array in (query_raw, key_raw, value_raw)]
    return pl.pallas_call(
        rim_kernel,
        grid=(1,),
        in_specs=[pl.BlockSpec((RIM, width), lambda i: (last, 0)) for width in widths],
        out_specs=pl.BlockSpec((RIM, sum(widths)), lambda i: (0, 0)),
        out_shape=jax.ShapeDtypeStruct((RIM, sum(widths)), BF16),
        name="pack_rim",
    )(query_raw, key_raw, value_raw)


def log_weights(logit):
    return (jnp.minimum(logit, 0.0) - jnp.log(1.0 + jnp.exp(-jnp.abs(logit)))) * LOG2E


def memory_kernel(
    kheads,
    vheads,
    part,
    span,
    key_ref,
    value_ref,
    rim_ref,
    tap_key_ref,
    tap_value_ref,
    gate_ref,
    logit_ref,
    unit_ref,
    solved_ref,
    before_ref,
    transit_ref,
    memory_ref,
    wide,
    state,
    diag_ref,
    neg_ref,
    tail_ref,
    right_ref,
    sum_ref,
):
    step = pl.program_id(0)
    last_step = pl.num_programs(0) - 1
    ratio = vheads // kheads
    tiles = kheads + vheads
    parts = span // CHUNK
    first_head = part * vheads
    base = pl.multiple_of(step * span, span)
    now_rows = pl.ds(base, span)
    key_from = part * kheads * DK
    value_from = part * vheads * DV
    rim_from = (key_ref.shape[1] + key_from, 2 * key_ref.shape[1] + value_from)
    places = [(chunk, head) for chunk in range(parts) for head in range(vheads)]

    def set_up():
        fill_masks(diag_ref)
        rows, cols = iotas((DK, WIDE))
        for head in range(vheads):
            state[head] = (rows == cols).astype(F32)
        for tile in range(tiles):
            at = rim_from[0] + tile * DK if tile < kheads else rim_from[1] + (tile - kheads) * DV
            wide[tile, 0:HALO] = rim_ref[:, at : at + 128].astype(F32)[RIM - HALO :]

    def prepare():
        tap_key = tap_key_ref[...].astype(F32) * 0.5
        tap_value = tap_value_ref[...].astype(F32) * 0.5
        keys = []
        for tile in range(kheads):
            at = slice(tile * DK, (tile + 1) * DK)
            place = slice(key_from + tile * DK, key_from + (tile + 1) * DK)
            keys.append(unit(conv(key_ref[now_rows, place], wide, tile, tap_key[:, place]), 1.0))
            unit_ref[now_rows, at] = keys[tile]
        for tile in range(vheads):
            place = slice(value_from + tile * DV, value_from + (tile + 1) * DV)
            value = conv(value_ref[now_rows, place], wide, kheads + tile, tap_value[:, place])
            for chunk in range(parts):
                right_ref[chunk * vheads + tile, :, DK:] = value[
                    chunk * CHUNK : (chunk + 1) * CHUNK
                ]
        for tile in range(tiles):
            wide[tile, 0:HALO] = wide[tile, span : span + HALO]
        rows, cols = iotas((CHUNK, CHUNK))
        strict = rows > cols
        cums = sums(gate_ref[:, now_rows] * LOG2E, span)
        strengths = log_weights(logit_ref[:, now_rows])
        for chunk in range(parts):
            here = slice(chunk * CHUNK, (chunk + 1) * CHUNK)
            cum_flat = cums[chunk]
            cum = cum_flat.T
            lift = strengths[:, here] - cum_flat
            last = cum_flat[:, CHUNK - 1 :]
            ends = jnp.exp2(last + lift)
            sum_ref[chunk] = jnp.broadcast_to(jnp.exp2(last), cum_flat.shape)
            for khead in range(kheads):
                key = keys[khead][here]
                flat = (-key).T
                gram = dot(key, flat)
                for which in range(ratio):
                    head = khead * ratio + which
                    item = chunk * vheads + head
                    place = first_head + head
                    cum_col = jnp.broadcast_to(cum[:, place : place + 1], (CHUNK, CHUNK))
                    powers = cum_col + lift[place : place + 1]
                    decays = jnp.exp2(jnp.where(strict, powers, -jnp.inf))
                    neg_ref[item] = gram * decays
                    tail_ref[item] = flat * ends[place : place + 1].astype(BF16)
                    right_ref[item, :, :DK] = key * jnp.exp2(cum_col).astype(BF16)

    def finish():
        negs = [neg_ref[item] for item in range(len(places))]
        found = half_inverses(negs, diag_ref)
        tops = [
            dot(f[:, :HALF], right_ref[item, :HALF]).astype(BF16)
            for item, f in enumerate(found)
        ]
        rests = [
            (
                right_ref[item, HALF:].astype(F32)
                + dot(neg_ref[item, HALF:, :HALF].astype(BF16), top)
            ).astype(BF16)
            for item, top in enumerate(tops)
        ]
        lows = [dot(f[:, HALF:], rest).astype(BF16) for f, rest in zip(found, rests)]
        erases, writes = [], []
        for item, (chunk, head) in enumerate(places):
            there = slice(head * WIDE, (head + 1) * WIDE)
            solved = jnp.concatenate([tops[item], lows[item]], axis=0)
            solved_ref[pl.ds(base + chunk * CHUNK, CHUNK), there] = solved
            product = dot(tail_ref[item], solved)
            erases.append(product[:, :DK].astype(BF16))
            writes.append(product[:, DK:])
        for item, (chunk, head) in enumerate(places):
            now = state[head]
            short = now.astype(BF16)
            before_ref[step * parts + chunk, head] = short
            tail = sum_ref[chunk, first_head + head : first_head + head + 1]
            change = dot(erases[item], short)
            state[head, :, :DK] = now[:, :DK] * tail + change[:, :DK]
            state[head, :, DK:] = now[:, DK:] * tail + (change[:, DK:] - writes[item])

    @pl.when(step == 0)
    def _():
        set_up()

    prepare()
    finish()

    @pl.when(step == last_step)
    def _():
        for head in range(vheads):
            transit_ref[head] = state[head, :, :DK].astype(BF16)
            memory_ref[head] = state[head, :, DK:]


def memory_pass(part, key_raw, value_raw, rim, conv_key, conv_value, gate_flat, logit_flat):
    tok_count = key_raw.shape[0]
    all_kheads = key_raw.shape[1] // DK
    all_vheads = value_raw.shape[1] // DV
    kheads, vheads = all_kheads // PARTS, all_vheads // PARTS
    tiles = kheads + vheads
    span = min(SPAN_X, tok_count)
    chunks = tok_count // CHUNK
    items = span // CHUNK * vheads
    blocks = tok_count // span
    count = len(levels())

    def kernel(*refs):
        memory_kernel(kheads, vheads, part, span, *refs)

    return pl.pallas_call(
        kernel,
        grid=(blocks,),
        in_specs=[VMEM] * 7,
        out_specs=[VMEM] * 5,
        out_shape=[
            jax.ShapeDtypeStruct((tok_count, kheads * DK), BF16),
            jax.ShapeDtypeStruct((tok_count, vheads * WIDE), BF16),
            jax.ShapeDtypeStruct((chunks, vheads, DK, WIDE), BF16),
            jax.ShapeDtypeStruct((vheads, DK, DK), BF16),
            jax.ShapeDtypeStruct((vheads, DK, DV), F32),
        ],
        scratch_shapes=[
            pltpu.VMEM((tiles, span + HALO, 128), F32),
            pltpu.VMEM((vheads, DK, WIDE), F32),
            pltpu.VMEM((count, CHUNK, CHUNK), BF16),
            pltpu.VMEM((items, CHUNK, CHUNK), F32),
            pltpu.VMEM((items, CHUNK, CHUNK), BF16),
            pltpu.VMEM((items, CHUNK, WIDE), BF16),
            pltpu.VMEM((span // CHUNK, all_vheads, CHUNK), F32),
        ],
        compiler_params=pltpu.CompilerParams(vmem_limit_bytes=20 * 1024 * 1024),
        cost_estimate=pl.CostEstimate(
            flops=2 * tok_count * vheads * 1000 * 1000, bytes_accessed=1 << 23, transcendentals=0
        ),
        name="memory_pass",
    )(key_raw, value_raw, rim, conv_key, conv_value, gate_flat, logit_flat)


def rows_kernel(
    kheads,
    vheads,
    group,
    span,
    query_ref,
    rim_ref,
    tap_ref,
    key_ref,
    gate_ref,
    logit_ref,
    solved_ref,
    before_ref,
    rows_ref,
    local_ref,
    wide,
):
    step = pl.program_id(0)
    ratio = vheads // kheads
    first_head = group * vheads
    base = pl.multiple_of(step * span, span)
    now_rows = pl.ds(base, span)
    query_from = group * kheads * DK

    @pl.when(step == 0)
    def _():
        for tile in range(kheads):
            at = slice(query_from + tile * DK, query_from + (tile + 1) * DK)
            wide[tile, 0:HALO] = rim_ref[:, at].astype(F32)[RIM - HALO :]

    @pl.when(step > 0)
    def _():
        for tile in range(kheads):
            wide[tile, 0:HALO] = wide[tile, span : span + HALO]

    taps = tap_ref[...].astype(F32) * 0.5
    queries = []
    for tile in range(kheads):
        at = slice(query_from + tile * DK, query_from + (tile + 1) * DK)
        queries.append(unit(conv(query_ref[now_rows, at], wide, tile, taps[:, at]), DK**-0.5))

    rows, cols = iotas((CHUNK, CHUNK))
    lower = rows >= cols
    cums = sums(gate_ref[:, now_rows] * LOG2E, span)
    strengths = log_weights(logit_ref[:, now_rows])
    for part in range(span // CHUNK):
        here = slice(part * CHUNK, (part + 1) * CHUNK)
        place_rows = pl.ds(base + part * CHUNK, CHUNK)
        cum_flat = cums[part]
        cum = cum_flat.T
        lift = strengths[:, here] - cum_flat
        for khead in range(kheads):
            query = queries[khead][here]
            gram = lax.dot_general(
                query,
                key_ref[place_rows, khead * DK : (khead + 1) * DK],
                (((1,), (1,)), ((), ())),
                preferred_element_type=F32,
            )
            for which in range(ratio):
                head = khead * ratio + which
                place = first_head + head
                there = slice(head * DV, (head + 1) * DV)
                cum_col = jnp.broadcast_to(cum[:, place : place + 1], (CHUNK, CHUNK))
                powers = cum_col + lift[place : place + 1]
                scores = (gram * jnp.exp2(jnp.where(lower, powers, -jnp.inf))).astype(BF16)
                product = dot(scores, solved_ref[place_rows, head * WIDE : (head + 1) * WIDE])
                meet = query.astype(F32) * jnp.exp2(cum_col) - product[:, :DK]
                final = dot(meet.astype(BF16), before_ref[step * (span // CHUNK) + part, head])
                rows_ref[place_rows, there] = final[:, :DK].astype(BF16)
                local_ref[place_rows, there] = (final[:, DK:] + product[:, DK:]).astype(BF16)


def rows_pass(part, query_raw, rim, conv_query, keys, gate_flat, logit_flat, solved, before):
    tok_count = query_raw.shape[0]
    kheads = query_raw.shape[1] // DK // PARTS
    all_vheads = gate_flat.shape[0]
    vheads = all_vheads // PARTS
    span = min(SPAN_Y, tok_count)

    def kernel(*refs):
        rows_kernel(kheads, vheads, part, span, *refs)

    return pl.pallas_call(
        kernel,
        grid=(tok_count // span,),
        in_specs=[VMEM] * 8,
        out_specs=[VMEM] * 2,
        out_shape=[
            jax.ShapeDtypeStruct((tok_count, vheads * DV), BF16),
            jax.ShapeDtypeStruct((tok_count, vheads * DV), BF16),
        ],
        scratch_shapes=[pltpu.VMEM((kheads, span + HALO, 128), F32)],
        compiler_params=pltpu.CompilerParams(vmem_limit_bytes=16 * 1024 * 1024),
        cost_estimate=pl.CostEstimate(
            flops=2 * tok_count * vheads * 1000 * 500, bytes_accessed=1 << 23, transcendentals=0
        ),
        name="rows_pass",
    )(query_raw, rim, conv_query, keys, gate_flat, logit_flat, solved, before)


def final_kernel(vheads, rows_ref, local_ref, early_ref, late_ref, gain_ref, *rest):
    out_ref = rest[-1]
    gain = gain_ref[...]
    span = out_ref.shape[0]
    now_rows = pl.ds(pl.multiple_of(pl.program_id(0) * span, span), span)
    for head in range(vheads):
        there = slice(head * DV, (head + 1) * DV)
        start = early_ref[head] + late_ref[head]
        output = dot(rows_ref[now_rows, there], start) + local_ref[now_rows, there].astype(F32)
        square = output * output
        if head % 2:
            total = row_sums(square)
        else:
            total = jnp.sum(square, axis=-1, keepdims=True)
        mean = total * (1.0 / DV)
        out_ref[:, there] = (output * lax.rsqrt(mean + EPSILON) * gain).astype(BF16)


def final_pass(part, rows, local, early, late, gain, earlier):
    tok_count = rows.shape[0]
    vheads = early.shape[0]
    span = min(512, tok_count)

    def along(width, column):
        return pl.BlockSpec((span, width), lambda i: (i, column))

    def kernel(*refs):
        final_kernel(vheads, *refs)

    arrays = [rows, local, early, late, gain]
    specs = [VMEM] * 5
    if earlier is not None:
        arrays.append(earlier)
        specs.append(pl.BlockSpec(memory_space=pl.ANY))
    return pl.pallas_call(
        kernel,
        grid=(tok_count // span,),
        in_specs=specs,
        out_specs=along(vheads * DV, part),
        out_shape=jax.ShapeDtypeStruct((tok_count, PARTS * vheads * DV), BF16),
        input_output_aliases={} if earlier is None else {5: 0},
        compiler_params=pltpu.CompilerParams(vmem_limit_bytes=12 * 1024 * 1024),
        name="final_pass",
    )(*arrays)


def shards(
    query_raw, key_raw, value_raw, conv_query, conv_key, conv_value, gate_log, beta_logit, norm_gain
):
    count = lax.axis_size("ctx")
    rim = lax.ppermute(
        pack_rim(query_raw, key_raw, value_raw), "ctx", [(at, at + 1) for at in range(count - 1)]
    )
    gate_flat, logit_flat = gate_log.T, beta_logit.T
    gain = norm_gain.reshape(1, DV)
    first = [
        memory_pass(part, key_raw, value_raw, rim, conv_key, conv_value, gate_flat, logit_flat)
        for part in range(PARTS)
    ]
    def after(value, *others):
        return lax.optimization_barrier((value, *others))[0]

    moved = [[found[4].astype(BF16)] for found in first]
    got = [[] for _ in first]
    second = [None] * PARTS

    def send(part):
        source = len(got[part])
        got[part].append(lax.ppermute(moved[part][source], "ctx", [(source, source + 1)]))

    def carry(part, *others):
        transit, memory = first[part][3:]
        arrived = after(got[part][-1], *others)
        ahead = jnp.einsum("hab,hbc->hac", transit, arrived, preferred_element_type=F32)
        moved[part].append((ahead + memory).astype(BF16))

    def rows_of(part, *others):
        keys, solved, before = first[part][:3]
        second[part] = rows_pass(
            part,
            query_raw,
            rim,
            conv_query,
            keys,
            gate_flat,
            logit_flat,
            after(solved, *others),
            before,
        )

    for turn in range(count - 1):
        for part in range(PARTS):
            send(part)
            if turn + 1 < count - 1:
                waits = [] if part == 0 or turn >= PARTS else [second[turn][1]]
                carry(part, *waits)
            if part == 0 and turn < PARTS:
                ready = [moved[part][-1] for part in range(PARTS)]
                rows_of(turn, *ready)
    out = None
    for part in range(PARTS):
        rows, local = second[part]
        early = sum(got[part][:-1], jnp.zeros_like(got[part][-1]))
        late = got[part][-1]
        if part + 1 < PARTS:
            late = after(late, moved[part + 1][-1])
        out = final_pass(part, rows, local, early, late, gain, out)
    return out


def solution(mesh):
    return jax.shard_map(
        shards,
        mesh=mesh,
        in_specs=(
            P(("groups", "ctx"), "head"),
            P(("groups", "ctx"), "head"),
            P(("groups", "ctx"), "head"),
            P(None, "head"),
            P(None, "head"),
            P(None, "head"),
            P(("groups", "ctx"), "head"),
            P(("groups", "ctx"), "head"),
            P(),
        ),
        out_specs=P(("groups", "ctx"), "head"),
        check_vma=False,
    )
```

```python
import jax
import jax.numpy as jnp
from jax import lax
from jax.experimental import pallas as pl
from jax.experimental.pallas import tpu as pltpu
from jax.sharding import PartitionSpec as P

DK = 128
DV = 128
KW = 4
CHUNK = 128
HALF = 64
BASE = 8
HALO = 8
RIM = 16
PARTS = 2
SPAN_X = 512
SPAN_Y = 512
SPAN_Z = 256
EPSILON = 1e-06
LOG2E = 1.4426950408889634
F32 = jnp.float32
BF16 = jnp.bfloat16
WIDE = DK + DV
VMEM = pl.BlockSpec(memory_space=pltpu.VMEM)


def dot(left, right):
    return jnp.dot(left, right, preferred_element_type=F32)


def levels():
    sizes = []
    size = BASE
    while size < HALF:
        sizes.append(size)
        size *= 2
    return sizes


def iotas(shape):
    return lax.broadcasted_iota(jnp.int32, shape, 0), lax.broadcasted_iota(jnp.int32, shape, 1)


def fill_masks(diag_ref):
    rows, cols = iotas((CHUNK, CHUNK))
    for place, size in enumerate(levels()):
        diag_ref[place] = (rows // size == cols // size).astype(BF16)


def packed(strip):
    if strip.shape[0] < 16:
        strip = jnp.concatenate([strip] * (16 // strip.shape[0]), axis=0)
    return strip.astype(BF16)


def spread(strip, mask):
    count = CHUNK // strip.shape[0]
    return jnp.concatenate([strip] * count, axis=0) * mask


def strips(neg, size, step, first):
    lanes = lax.broadcasted_iota(jnp.int32, (1, CHUNK), 1)
    out = neg[first : first + size]
    for turn in range(1, CHUNK // step):
        start = turn * step + first
        out = jnp.where(lanes // step == turn, neg[start : start + size], out)
    return out


def substitute(strip):
    rows, cols = iotas((8, CHUNK))
    halves = [strip[at : at + 8] for at in range(0, BASE, 8)]
    found = [(rows + at == cols % BASE).astype(F32) for at in range(0, BASE, 8)]
    for row in range(BASE - 1):
        at = cols // BASE * BASE + row
        solved = found[row // 8][row % 8 : row % 8 + 1]
        for half in range((row + 1) // 8, BASE // 8):
            column = jnp.take_along_axis(halves[half], at, axis=1)
            found[half] = found[half] + column * solved
    return jnp.concatenate(found, axis=0)


def half_inverses(negs, diag_ref):
    lanes = lax.broadcasted_iota(jnp.int32, (1, CHUNK), 1)
    found = [substitute(strips(neg, BASE, BASE, 0)) for neg in negs]
    pairs = range(0, len(negs), 2)
    for place, size in enumerate(levels()):
        even = (lanes // size) % 2 == 0

        def up(value):
            return pltpu.roll(value, size, 1)

        def down(value):
            return pltpu.roll(value, CHUNK - size, 1)

        lowers = [strips(neg, size, 2 * size, size) for neg in negs]
        evens = [packed(jnp.where(even, found[i], up(found[i + 1]))) for i in pairs]
        odds = [packed(jnp.where(even, down(found[i]), found[i + 1])) for i in pairs]
        both = [packed(jnp.where(even, lowers[i], up(lowers[i + 1]))) for i in pairs]
        weights = [spread(value, diag_ref[place]) for value in evens]
        middles = [dot(value, weight).astype(BF16) for value, weight in zip(both, weights)]
        weights = [spread(value, diag_ref[place]) for value in middles]
        corners = [dot(value, weight)[:size] for value, weight in zip(odds, weights)]
        wider = []
        for i, f in enumerate(found):
            corner = corners[i // 2] if i % 2 == 0 else down(corners[i // 2])
            wider.append(
                jnp.concatenate([jnp.where(even, f, 0.0), jnp.where(even, corner, f)], axis=0)
            )
        found = wider
    return [f.astype(BF16) for f in found]


def conv(raw, wide, tile, tap):
    span = raw.shape[0]
    raw = raw.astype(F32)
    wide[tile, HALO : HALO + span] = raw
    total = raw * tap[KW - 1 : KW]
    for back in range(1, KW):
        total += wide[tile, HALO - back : HALO - back + span] * tap[KW - 1 - back : KW - back]
    return (total + total * jnp.tanh(total)).astype(BF16)


def row_sums(values):
    return dot(values.astype(BF16), jnp.ones((values.shape[1], values.shape[1]), BF16))


def unit(values, factor):
    values = values.astype(F32)
    scale = lax.rsqrt(jnp.sum(values * values, axis=-1, keepdims=True) + EPSILON)
    if factor != 1.0:
        scale = scale * factor
    return (values * scale).astype(BF16)


def sums(gates, span):
    rows, cols = iotas((CHUNK, CHUNK))
    stacked = jnp.concatenate(
        [gates[:, at : at + CHUNK] for at in range(0, span, CHUNK)], axis=0
    )
    total = jnp.dot(
        stacked,
        (rows <= cols).astype(F32),
        precision=lax.Precision.HIGHEST,
        preferred_element_type=F32,
    )
    heads = gates.shape[0]
    return [total[at * heads : (at + 1) * heads] for at in range(span // CHUNK)]


def rim_kernel(query_ref, key_ref, value_ref, out_ref, done):
    copies = []
    at = 0
    for place, ref in enumerate((query_ref, key_ref, value_ref)):
        rows, width = ref.shape
        source = ref.at[pl.ds(rows - RIM, RIM), :]
        target = out_ref.at[:, pl.ds(at, width)]
        copies.append(pltpu.make_async_copy(source, target, done.at[place]))
        at += width
    for copy in copies:
        copy.start()
    for copy in copies:
        copy.wait()


def pack_rim(query_raw, key_raw, value_raw):
    width = query_raw.shape[1] + key_raw.shape[1] + value_raw.shape[1]
    anywhere = pl.BlockSpec(memory_space=pl.ANY)
    return pl.pallas_call(
        rim_kernel,
        in_specs=[anywhere] * 3,
        out_specs=anywhere,
        out_shape=jax.ShapeDtypeStruct((RIM, width), BF16),
        scratch_shapes=[pltpu.SemaphoreType.DMA((3,))],
        name="pack_rim",
    )(query_raw, key_raw, value_raw)


def log_weights(logit):
    return (jnp.minimum(logit, 0.0) - jnp.log(1.0 + jnp.exp(-jnp.abs(logit)))) * LOG2E


def memory_kernel(
    kheads,
    vheads,
    part,
    span,
    key_ref,
    value_ref,
    rim_ref,
    tap_key_ref,
    tap_value_ref,
    gate_ref,
    logit_ref,
    unit_ref,
    solved_ref,
    before_ref,
    transit_ref,
    memory_ref,
    wide,
    state,
    diag_ref,
    neg_ref,
    tail_ref,
    right_ref,
    sum_ref,
):
    ratio = vheads // kheads
    tiles = kheads + vheads
    parts = span // CHUNK
    first_head = part * vheads
    key_from = part * kheads * DK
    value_from = part * vheads * DV
    rim_from = (key_ref.shape[1] + key_from, 2 * key_ref.shape[1] + value_from)
    places = [(chunk, head) for chunk in range(parts) for head in range(vheads)]

    def set_up():
        fill_masks(diag_ref)
        rows, cols = iotas((DK, WIDE))
        for head in range(vheads):
            state[head] = (rows == cols).astype(F32)
        for tile in range(tiles):
            at = rim_from[0] + tile * DK if tile < kheads else rim_from[1] + (tile - kheads) * DV
            wide[tile, 0:HALO] = rim_ref[:, at : at + 128].astype(F32)[RIM - HALO :]

    def prepare(step):
        now_rows = pl.ds(pl.multiple_of(step * span, span), span)
        tap_key = tap_key_ref[...].astype(F32) * 0.5
        tap_value = tap_value_ref[...].astype(F32) * 0.5
        keys = []
        for tile in range(kheads):
            at = slice(tile * DK, (tile + 1) * DK)
            place = slice(key_from + tile * DK, key_from + (tile + 1) * DK)
            keys.append(unit(conv(key_ref[now_rows, place], wide, tile, tap_key[:, place]), 1.0))
            unit_ref[now_rows, at] = keys[tile]
        for tile in range(vheads):
            place = slice(value_from + tile * DV, value_from + (tile + 1) * DV)
            value = conv(value_ref[now_rows, place], wide, kheads + tile, tap_value[:, place])
            for chunk in range(parts):
                right_ref[chunk * vheads + tile, :, DK:] = value[
                    chunk * CHUNK : (chunk + 1) * CHUNK
                ]
        for tile in range(tiles):
            wide[tile, 0:HALO] = wide[tile, span : span + HALO]
        rows, cols = iotas((CHUNK, CHUNK))
        strict = rows > cols
        cums = sums(gate_ref[:, now_rows] * LOG2E, span)
        strengths = log_weights(logit_ref[:, now_rows])
        for chunk in range(parts):
            here = slice(chunk * CHUNK, (chunk + 1) * CHUNK)
            cum_flat = cums[chunk]
            cum = cum_flat.T
            lift = strengths[:, here] - cum_flat
            last = cum_flat[:, CHUNK - 1 :]
            ends = jnp.exp2(last + lift)
            sum_ref[chunk] = jnp.broadcast_to(jnp.exp2(last), cum_flat.shape)
            for khead in range(kheads):
                key = keys[khead][here]
                flat = (-key).T
                gram = dot(key, flat)
                for which in range(ratio):
                    head = khead * ratio + which
                    item = chunk * vheads + head
                    place = first_head + head
                    cum_col = jnp.broadcast_to(cum[:, place : place + 1], (CHUNK, CHUNK))
                    powers = cum_col + lift[place : place + 1]
                    decays = jnp.exp2(jnp.where(strict, powers, -jnp.inf))
                    neg_ref[item] = gram * decays
                    tail_ref[item] = flat * ends[place : place + 1].astype(BF16)
                    right_ref[item, :, :DK] = key * jnp.exp2(cum_col).astype(BF16)

    def finish(step):
        base = pl.multiple_of(step * span, span)
        negs = [neg_ref[item] for item in range(len(places))]
        found = half_inverses(negs, diag_ref)
        tops = [
            dot(f[:, :HALF], right_ref[item, :HALF]).astype(BF16)
            for item, f in enumerate(found)
        ]
        rests = [
            (
                right_ref[item, HALF:].astype(F32)
                + dot(neg_ref[item, HALF:, :HALF].astype(BF16), top)
            ).astype(BF16)
            for item, top in enumerate(tops)
        ]
        lows = [dot(f[:, HALF:], rest).astype(BF16) for f, rest in zip(found, rests)]
        erases, writes = [], []
        for item, (chunk, head) in enumerate(places):
            there = slice(head * WIDE, (head + 1) * WIDE)
            solved = jnp.concatenate([tops[item], lows[item]], axis=0)
            solved_ref[pl.ds(base + chunk * CHUNK, CHUNK), there] = solved
            product = dot(tail_ref[item], solved)
            erases.append(product[:, :DK].astype(BF16))
            writes.append(product[:, DK:])
        for item, (chunk, head) in enumerate(places):
            now = state[head]
            short = now.astype(BF16)
            before_ref[step * parts + chunk, head] = short
            tail = sum_ref[chunk, first_head + head : first_head + head + 1]
            change = dot(erases[item], short)
            state[head, :, :DK] = now[:, :DK] * tail + change[:, :DK]
            state[head, :, DK:] = now[:, DK:] * tail + (change[:, DK:] - writes[item])

    def advance(step, carry):
        prepare(step)
        finish(step)
        return carry

    set_up()
    lax.fori_loop(0, key_ref.shape[0] // span, advance, 0)
    for head in range(vheads):
        transit_ref[head] = state[head, :, :DK].astype(BF16)
        memory_ref[head] = state[head, :, DK:]


def memory_pass(part, key_raw, value_raw, rim, conv_key, conv_value, gate_flat, logit_flat):
    tok_count = key_raw.shape[0]
    all_kheads = key_raw.shape[1] // DK
    all_vheads = value_raw.shape[1] // DV
    kheads, vheads = all_kheads // PARTS, all_vheads // PARTS
    tiles = kheads + vheads
    span = min(SPAN_X, tok_count)
    chunks = tok_count // CHUNK
    items = span // CHUNK * vheads
    count = len(levels())

    def kernel(*refs):
        memory_kernel(kheads, vheads, part, span, *refs)

    return pl.pallas_call(
        kernel,
        in_specs=[VMEM] * 7,
        out_specs=[VMEM] * 5,
        out_shape=[
            jax.ShapeDtypeStruct((tok_count, kheads * DK), BF16),
            jax.ShapeDtypeStruct((tok_count, vheads * WIDE), BF16),
            jax.ShapeDtypeStruct((chunks, vheads, DK, WIDE), BF16),
            jax.ShapeDtypeStruct((vheads, DK, DK), BF16),
            jax.ShapeDtypeStruct((vheads, DK, DV), F32),
        ],
        scratch_shapes=[
            pltpu.VMEM((tiles, span + HALO, 128), F32),
            pltpu.VMEM((vheads, DK, WIDE), F32),
            pltpu.VMEM((count, CHUNK, CHUNK), BF16),
            pltpu.VMEM((items, CHUNK, CHUNK), F32),
            pltpu.VMEM((items, CHUNK, CHUNK), BF16),
            pltpu.VMEM((items, CHUNK, WIDE), BF16),
            pltpu.VMEM((span // CHUNK, all_vheads, CHUNK), F32),
        ],
        compiler_params=pltpu.CompilerParams(vmem_limit_bytes=20 * 1024 * 1024),
        cost_estimate=pl.CostEstimate(
            flops=2 * tok_count * vheads * 1000 * 1000, bytes_accessed=1 << 23, transcendentals=0
        ),
        name="memory_pass",
    )(key_raw, value_raw, rim, conv_key, conv_value, gate_flat, logit_flat)


def rows_kernel(
    kheads,
    vheads,
    group,
    span,
    query_ref,
    rim_ref,
    tap_ref,
    key_ref,
    gate_ref,
    logit_ref,
    solved_ref,
    before_ref,
    rows_ref,
    local_ref,
    wide,
):
    ratio = vheads // kheads
    first_head = group * vheads
    query_from = group * kheads * DK
    for tile in range(kheads):
        at = slice(query_from + tile * DK, query_from + (tile + 1) * DK)
        wide[tile, 0:HALO] = rim_ref[:, at].astype(F32)[RIM - HALO :]

    def advance(step, carry):
        base = pl.multiple_of(step * span, span)
        now_rows = pl.ds(base, span)
        taps = tap_ref[...].astype(F32) * 0.5
        queries = []
        for tile in range(kheads):
            at = slice(query_from + tile * DK, query_from + (tile + 1) * DK)
            queries.append(unit(conv(query_ref[now_rows, at], wide, tile, taps[:, at]), DK**-0.5))

        for tile in range(kheads):
            wide[tile, 0:HALO] = wide[tile, span : span + HALO]
        rows, cols = iotas((CHUNK, CHUNK))
        lower = rows >= cols
        cums = sums(gate_ref[:, now_rows] * LOG2E, span)
        strengths = log_weights(logit_ref[:, now_rows])
        for part in range(span // CHUNK):
            here = slice(part * CHUNK, (part + 1) * CHUNK)
            place_rows = pl.ds(base + part * CHUNK, CHUNK)
            cum_flat = cums[part]
            cum = cum_flat.T
            lift = strengths[:, here] - cum_flat
            for khead in range(kheads):
                query = queries[khead][here]
                gram = lax.dot_general(
                    query,
                    key_ref[place_rows, khead * DK : (khead + 1) * DK],
                    (((1,), (1,)), ((), ())),
                    preferred_element_type=F32,
                )
                for which in range(ratio):
                    head = khead * ratio + which
                    place = first_head + head
                    there = slice(head * DV, (head + 1) * DV)
                    cum_col = jnp.broadcast_to(cum[:, place : place + 1], (CHUNK, CHUNK))
                    powers = cum_col + lift[place : place + 1]
                    scores = (gram * jnp.exp2(jnp.where(lower, powers, -jnp.inf))).astype(BF16)
                    product = dot(scores, solved_ref[place_rows, head * WIDE : (head + 1) * WIDE])
                    meet = query.astype(F32) * jnp.exp2(cum_col) - product[:, :DK]
                    final = dot(meet.astype(BF16), before_ref[step * (span // CHUNK) + part, head])
                    rows_ref[place_rows, there] = final[:, :DK].astype(BF16)
                    local_ref[place_rows, there] = (final[:, DK:] + product[:, DK:]).astype(BF16)
        return carry

    lax.fori_loop(0, query_ref.shape[0] // span, advance, 0)


def rows_pass(part, query_raw, rim, conv_query, keys, gate_flat, logit_flat, solved, before):
    tok_count = query_raw.shape[0]
    kheads = query_raw.shape[1] // DK // PARTS
    all_vheads = gate_flat.shape[0]
    vheads = all_vheads // PARTS
    span = min(SPAN_Y, tok_count)

    def kernel(*refs):
        rows_kernel(kheads, vheads, part, span, *refs)

    return pl.pallas_call(
        kernel,
        in_specs=[VMEM] * 8,
        out_specs=[VMEM] * 2,
        out_shape=[
            jax.ShapeDtypeStruct((tok_count, vheads * DV), BF16),
            jax.ShapeDtypeStruct((tok_count, vheads * DV), BF16),
        ],
        scratch_shapes=[pltpu.VMEM((kheads, span + HALO, 128), F32)],
        compiler_params=pltpu.CompilerParams(vmem_limit_bytes=16 * 1024 * 1024),
        cost_estimate=pl.CostEstimate(
            flops=2 * tok_count * vheads * 1000 * 500, bytes_accessed=1 << 23, transcendentals=0
        ),
        name="rows_pass",
    )(query_raw, rim, conv_query, keys, gate_flat, logit_flat, solved, before)


def final_kernel(part, span, rows_ref, local_ref, early_ref, late_ref, gain_ref, *rest):
    out_ref, ready, done = rest[-3:]
    gain = gain_ref[...]
    vheads = early_ref.shape[0]
    width = vheads * DV
    starts = [early_ref[head] + late_ref[head] for head in range(vheads)]
    copies = []
    for turn in range(rows_ref.shape[0] // span):
        here = slice(turn * span, (turn + 1) * span)
        for head in range(vheads):
            there = slice(head * DV, (head + 1) * DV)
            output = dot(rows_ref[here, there], starts[head]) + local_ref[here, there].astype(F32)
            square = output * output
            if head % 2:
                total = row_sums(square)
            else:
                total = jnp.sum(square, axis=-1, keepdims=True)
            scale = lax.rsqrt(total * (1.0 / DV) + EPSILON)
            ready[here, there] = (output * scale * gain).astype(BF16)
        target = out_ref.at[pl.ds(turn * span, span), pl.ds(part * width, width)]
        source = ready.at[pl.ds(turn * span, span), :]
        copies.append(pltpu.make_async_copy(source, target, done.at[turn]))
        copies[-1].start()
    for copy in copies:
        copy.wait()


def final_pass(part, rows, local, early, late, gain, earlier):
    tok_count = rows.shape[0]
    vheads = early.shape[0]
    span = min(SPAN_Z, tok_count)

    def kernel(*refs):
        final_kernel(part, span, *refs)

    anywhere = pl.BlockSpec(memory_space=pl.ANY)
    arrays = [rows, local, early, late, gain]
    specs = [VMEM] * 5
    if earlier is not None:
        arrays.append(earlier)
        specs.append(anywhere)
    return pl.pallas_call(
        kernel,
        in_specs=specs,
        out_specs=anywhere,
        out_shape=jax.ShapeDtypeStruct((tok_count, PARTS * vheads * DV), BF16),
        scratch_shapes=[
            pltpu.VMEM((tok_count, vheads * DV), BF16),
            pltpu.SemaphoreType.DMA((tok_count // span,)),
        ],
        input_output_aliases={} if earlier is None else {5: 0},
        compiler_params=pltpu.CompilerParams(vmem_limit_bytes=12 * 1024 * 1024),
        name="final_pass",
    )(*arrays)


def shards(
    query_raw, key_raw, value_raw, conv_query, conv_key, conv_value, gate_log, beta_logit, norm_gain
):
    count = lax.axis_size("ctx")
    rim = lax.ppermute(
        pack_rim(query_raw, key_raw, value_raw), "ctx", [(at, at + 1) for at in range(count - 1)]
    )
    gate_flat, logit_flat = gate_log.T, beta_logit.T
    gain = norm_gain.reshape(1, DV)
    first = [
        memory_pass(part, key_raw, value_raw, rim, conv_key, conv_value, gate_flat, logit_flat)
        for part in range(PARTS)
    ]
    def after(value, *others):
        return lax.optimization_barrier((value, *others))[0]

    moved = [[found[4].astype(BF16)] for found in first]
    got = [[] for _ in first]
    second = [None] * PARTS

    def send(part):
        source = len(got[part])
        got[part].append(lax.ppermute(moved[part][source], "ctx", [(source, source + 1)]))

    def carry(part, *others):
        transit, memory = first[part][3:]
        arrived = after(got[part][-1], *others)
        ahead = jnp.einsum("hab,hbc->hac", transit, arrived, preferred_element_type=F32)
        moved[part].append((ahead + memory).astype(BF16))

    def rows_of(part, *others):
        keys, solved, before = first[part][:3]
        second[part] = rows_pass(
            part,
            query_raw,
            rim,
            conv_query,
            keys,
            gate_flat,
            logit_flat,
            after(solved, *others),
            before,
        )

    for turn in range(count - 1):
        for part in range(PARTS):
            send(part)
            if turn + 1 < count - 1:
                waits = [] if part == 0 or turn >= PARTS else [second[turn][1]]
                carry(part, *waits)
            if part == 0 and turn < PARTS:
                ready = [moved[part][-1] for part in range(PARTS)]
                rows_of(turn, *ready)
    out = None
    for part in range(PARTS):
        rows, local = second[part]
        early = sum(got[part][:-1], jnp.zeros_like(got[part][-1]))
        late = got[part][-1]
        if part + 1 < PARTS:
            late = after(late, moved[part + 1][-1])
        out = final_pass(part, rows, local, early, late, gain, out)
    return out


def solution(mesh):
    return jax.shard_map(
        shards,
        mesh=mesh,
        in_specs=(
            P(("groups", "ctx"), "head"),
            P(("groups", "ctx"), "head"),
            P(("groups", "ctx"), "head"),
            P(None, "head"),
            P(None, "head"),
            P(None, "head"),
            P(("groups", "ctx"), "head"),
            P(("groups", "ctx"), "head"),
            P(),
        ),
        out_specs=P(("groups", "ctx"), "head"),
        check_vma=False,
    )
```

```python
import jax
import jax.numpy as jnp
from jax import lax
from jax.experimental import pallas as pl
from jax.experimental.pallas import tpu as pltpu
from jax.sharding import PartitionSpec as P

DK = 128
DV = 128
KW = 4
CHUNK = 128
HALF = 64
BASE = 8
HALO = 8
RIM = 16
PARTS = 2
SPAN_X = 512
SPAN_Y = 256
SPAN_Z = 256
EPSILON = 1e-06
LOG2E = 1.4426950408889634
F32 = jnp.float32
BF16 = jnp.bfloat16
WIDE = DK + DV
VMEM = pl.BlockSpec(memory_space=pltpu.VMEM)


def dot(left, right):
    return jnp.dot(left, right, preferred_element_type=F32)


def levels():
    sizes = []
    size = BASE
    while size < HALF:
        sizes.append(size)
        size *= 2
    return sizes


def iotas(shape):
    return lax.broadcasted_iota(jnp.int32, shape, 0), lax.broadcasted_iota(jnp.int32, shape, 1)


def fill_masks(diag_ref):
    rows, cols = iotas((CHUNK, CHUNK))
    for place, size in enumerate(levels()):
        diag_ref[place] = (rows // size == cols // size).astype(BF16)


def packed(strip):
    if strip.shape[0] < 16:
        strip = jnp.concatenate([strip] * (16 // strip.shape[0]), axis=0)
    return strip.astype(BF16)


def spread(strip, mask):
    count = CHUNK // strip.shape[0]
    return jnp.concatenate([strip] * count, axis=0) * mask


def strips(neg, size, step, first):
    lanes = lax.broadcasted_iota(jnp.int32, (1, CHUNK), 1)
    out = neg[first : first + size]
    for turn in range(1, CHUNK // step):
        start = turn * step + first
        out = jnp.where(lanes // step == turn, neg[start : start + size], out)
    return out


def substitute(strip):
    rows, cols = iotas((8, CHUNK))
    halves = [strip[at : at + 8] for at in range(0, BASE, 8)]
    found = [(rows + at == cols % BASE).astype(F32) for at in range(0, BASE, 8)]
    for row in range(BASE - 1):
        at = cols // BASE * BASE + row
        solved = found[row // 8][row % 8 : row % 8 + 1]
        for half in range((row + 1) // 8, BASE // 8):
            column = jnp.take_along_axis(halves[half], at, axis=1)
            found[half] = found[half] + column * solved
    return jnp.concatenate(found, axis=0)


def half_inverses(negs, diag_ref):
    lanes = lax.broadcasted_iota(jnp.int32, (1, CHUNK), 1)
    found = [substitute(strips(neg, BASE, BASE, 0)) for neg in negs]
    pairs = range(0, len(negs), 2)
    for place, size in enumerate(levels()):
        even = (lanes // size) % 2 == 0

        def up(value):
            return pltpu.roll(value, size, 1)

        def down(value):
            return pltpu.roll(value, CHUNK - size, 1)

        lowers = [strips(neg, size, 2 * size, size) for neg in negs]
        evens = [packed(jnp.where(even, found[i], up(found[i + 1]))) for i in pairs]
        odds = [packed(jnp.where(even, down(found[i]), found[i + 1])) for i in pairs]
        both = [packed(jnp.where(even, lowers[i], up(lowers[i + 1]))) for i in pairs]
        weights = [spread(value, diag_ref[place]) for value in evens]
        middles = [dot(value, weight).astype(BF16) for value, weight in zip(both, weights)]
        weights = [spread(value, diag_ref[place]) for value in middles]
        corners = [dot(value, weight)[:size] for value, weight in zip(odds, weights)]
        wider = []
        for i, f in enumerate(found):
            corner = corners[i // 2] if i % 2 == 0 else down(corners[i // 2])
            wider.append(
                jnp.concatenate([jnp.where(even, f, 0.0), jnp.where(even, corner, f)], axis=0)
            )
        found = wider
    return [f.astype(BF16) for f in found]


def conv(raw, wide, tile, tap):
    span = raw.shape[0]
    raw = raw.astype(F32)
    wide[tile, HALO : HALO + span] = raw
    total = raw * tap[KW - 1 : KW]
    for back in range(1, KW):
        total += wide[tile, HALO - back : HALO - back + span] * tap[KW - 1 - back : KW - back]
    return (total + total * jnp.tanh(total)).astype(BF16)


def row_sums(values):
    return dot(values.astype(BF16), jnp.ones((values.shape[1], values.shape[1]), BF16))


def unit(values, factor):
    values = values.astype(F32)
    scale = lax.rsqrt(jnp.sum(values * values, axis=-1, keepdims=True) + EPSILON)
    if factor != 1.0:
        scale = scale * factor
    return (values * scale).astype(BF16)


def sums(gates, span):
    rows, cols = iotas((CHUNK, CHUNK))
    stacked = jnp.concatenate(
        [gates[:, at : at + CHUNK] for at in range(0, span, CHUNK)], axis=0
    )
    total = jnp.dot(
        stacked,
        (rows <= cols).astype(F32),
        precision=lax.Precision.HIGHEST,
        preferred_element_type=F32,
    )
    heads = gates.shape[0]
    return [total[at * heads : (at + 1) * heads] for at in range(span // CHUNK)]


def rim_kernel(query_ref, key_ref, value_ref, out_ref):
    first, second = query_ref.shape[1], key_ref.shape[1]
    out_ref[:, :first] = query_ref[...]
    out_ref[:, first : first + second] = key_ref[...]
    out_ref[:, first + second :] = value_ref[...]


def pack_rim(query_raw, key_raw, value_raw):
    last = query_raw.shape[0] // RIM - 1
    widths = [array.shape[1] for array in (query_raw, key_raw, value_raw)]
    return pl.pallas_call(
        rim_kernel,
        grid=(1,),
        in_specs=[pl.BlockSpec((RIM, width), lambda i: (last, 0)) for width in widths],
        out_specs=pl.BlockSpec((RIM, sum(widths)), lambda i: (0, 0)),
        out_shape=jax.ShapeDtypeStruct((RIM, sum(widths)), BF16),
        name="pack_rim",
    )(query_raw, key_raw, value_raw)


def log_weights(logit):
    return (jnp.minimum(logit, 0.0) - jnp.log(1.0 + jnp.exp(-jnp.abs(logit)))) * LOG2E


def memory_kernel(
    kheads,
    vheads,
    span,
    key_ref,
    value_ref,
    rim_ref,
    tap_key_ref,
    tap_value_ref,
    gate_ref,
    logit_ref,
    unit_ref,
    solved_ref,
    before_ref,
    transit_ref,
    memory_ref,
    wide,
    state,
    diag_ref,
    neg_ref,
    tail_ref,
    right_ref,
    sum_ref,
):
    ratio = vheads // kheads
    tiles = kheads + vheads
    parts = span // CHUNK
    blocks = key_ref.shape[0] // span
    all_keys = key_ref.shape[1]

    def lanes(at, size):
        return pl.ds(pl.multiple_of(at, 128), size)

    def pick(part, options):
        out = options[0]
        for turn in range(1, PARTS):
            out = jnp.where(part == turn, options[turn], out)
        return out

    places = [(chunk, head) for chunk in range(parts) for head in range(vheads)]

    def set_up(part):
        rows, cols = iotas((DK, WIDE))
        for head in range(vheads):
            state[head] = (rows == cols).astype(F32)
        for tile in range(tiles):
            if tile < kheads:
                at = all_keys + (part * kheads + tile) * DK
            else:
                at = 2 * all_keys + (part * vheads + tile - kheads) * DV
            wide[tile, 0:HALO] = rim_ref[:, lanes(at, 128)].astype(F32)[RIM - HALO :]

    def prepare(part, step):
        now_rows = pl.ds(pl.multiple_of(step * span, span), span)
        keys = []
        for tile in range(kheads):
            at = slice(tile * DK, (tile + 1) * DK)
            place = lanes((part * kheads + tile) * DK, DK)
            tap = tap_key_ref[:, place].astype(F32) * 0.5
            keys.append(unit(conv(key_ref[now_rows, place], wide, tile, tap), 1.0))
            unit_ref[part, now_rows, at] = keys[tile]
        for tile in range(vheads):
            place = lanes((part * vheads + tile) * DV, DV)
            tap = tap_value_ref[:, place].astype(F32) * 0.5
            value = conv(value_ref[now_rows, place], wide, kheads + tile, tap)
            for chunk in range(parts):
                right_ref[chunk * vheads + tile, :, DK:] = value[
                    chunk * CHUNK : (chunk + 1) * CHUNK
                ]
        for tile in range(tiles):
            wide[tile, 0:HALO] = wide[tile, span : span + HALO]
        rows, cols = iotas((CHUNK, CHUNK))
        strict = rows > cols
        cums = sums(gate_ref[:, now_rows] * LOG2E, span)
        strengths = log_weights(logit_ref[:, now_rows])
        for chunk in range(parts):
            here = slice(chunk * CHUNK, (chunk + 1) * CHUNK)
            cum_flat = cums[chunk]
            cum = cum_flat.T
            lift = strengths[:, here] - cum_flat
            last = cum_flat[:, CHUNK - 1 :]
            ends = jnp.exp2(last + lift)
            sum_ref[chunk] = jnp.broadcast_to(jnp.exp2(last), cum_flat.shape)
            for khead in range(kheads):
                key = keys[khead][here]
                flat = (-key).T
                gram = dot(key, flat)
                for which in range(ratio):
                    head = khead * ratio + which
                    item = chunk * vheads + head
                    choices = range(head, PARTS * vheads, vheads)
                    cum_col = pick(part, [cum[:, at : at + 1] for at in choices])
                    cum_col = jnp.broadcast_to(cum_col, (CHUNK, CHUNK))
                    powers = cum_col + pick(part, [lift[at : at + 1] for at in choices])
                    end = pick(part, [ends[at : at + 1] for at in choices])
                    decays = jnp.exp2(jnp.where(strict, powers, -jnp.inf))
                    neg_ref[item] = gram * decays
                    tail_ref[item] = flat * end.astype(BF16)
                    right_ref[item, :, :DK] = key * jnp.exp2(cum_col).astype(BF16)

    def finish(part, step):
        base = pl.multiple_of(step * span, span)
        negs = [neg_ref[item] for item in range(len(places))]
        found = half_inverses(negs, diag_ref)
        tops = [
            dot(f[:, :HALF], right_ref[item, :HALF]).astype(BF16)
            for item, f in enumerate(found)
        ]
        rests = [
            (
                right_ref[item, HALF:].astype(F32)
                + dot(neg_ref[item, HALF:, :HALF].astype(BF16), top)
            ).astype(BF16)
            for item, top in enumerate(tops)
        ]
        lows = [dot(f[:, HALF:], rest).astype(BF16) for f, rest in zip(found, rests)]
        erases, writes = [], []
        for item, (chunk, head) in enumerate(places):
            there = slice(head * WIDE, (head + 1) * WIDE)
            solved = jnp.concatenate([tops[item], lows[item]], axis=0)
            solved_ref[part, pl.ds(base + chunk * CHUNK, CHUNK), there] = solved
            product = dot(tail_ref[item], solved)
            erases.append(product[:, :DK].astype(BF16))
            writes.append(product[:, DK:])
        for item, (chunk, head) in enumerate(places):
            now = state[head]
            short = now.astype(BF16)
            before_ref[part, step * parts + chunk, head] = short
            choices = range(head, PARTS * vheads, vheads)
            tail = pick(part, [sum_ref[chunk, at : at + 1] for at in choices])
            tail = jnp.broadcast_to(tail, (DK, CHUNK))
            change = dot(erases[item], short)
            state[head, :, :DK] = now[:, :DK] * tail + change[:, :DK]
            state[head, :, DK:] = now[:, DK:] * tail + (change[:, DK:] - writes[item])

    def advance(turn, carry):
        part, step = turn // blocks, turn % blocks

        @pl.when(step == 0)
        def _():
            set_up(part)

        prepare(part, step)
        finish(part, step)

        @pl.when(step == blocks - 1)
        def _():
            for head in range(vheads):
                transit_ref[part, head] = state[head, :, :DK].astype(BF16)
                memory_ref[part, head] = state[head, :, DK:]

        return carry

    fill_masks(diag_ref)
    lax.fori_loop(0, PARTS * blocks, advance, 0)


def memory_pass(key_raw, value_raw, rim, conv_key, conv_value, gate_flat, logit_flat):
    tok_count = key_raw.shape[0]
    all_kheads = key_raw.shape[1] // DK
    all_vheads = value_raw.shape[1] // DV
    kheads, vheads = all_kheads // PARTS, all_vheads // PARTS
    tiles = kheads + vheads
    span = min(SPAN_X, tok_count)
    chunks = tok_count // CHUNK
    items = span // CHUNK * vheads
    count = len(levels())

    def kernel(*refs):
        memory_kernel(kheads, vheads, span, *refs)

    return pl.pallas_call(
        kernel,
        in_specs=[VMEM] * 7,
        out_specs=[VMEM] * 5,
        out_shape=[
            jax.ShapeDtypeStruct((PARTS, tok_count, kheads * DK), BF16),
            jax.ShapeDtypeStruct((PARTS, tok_count, vheads * WIDE), BF16),
            jax.ShapeDtypeStruct((PARTS, chunks, vheads, DK, WIDE), BF16),
            jax.ShapeDtypeStruct((PARTS, vheads, DK, DK), BF16),
            jax.ShapeDtypeStruct((PARTS, vheads, DK, DV), F32),
        ],
        scratch_shapes=[
            pltpu.VMEM((tiles, span + HALO, 128), F32),
            pltpu.VMEM((vheads, DK, WIDE), F32),
            pltpu.VMEM((count, CHUNK, CHUNK), BF16),
            pltpu.VMEM((items, CHUNK, CHUNK), F32),
            pltpu.VMEM((items, CHUNK, CHUNK), BF16),
            pltpu.VMEM((items, CHUNK, WIDE), BF16),
            pltpu.VMEM((span // CHUNK, all_vheads, CHUNK), F32),
        ],
        compiler_params=pltpu.CompilerParams(vmem_limit_bytes=20 * 1024 * 1024),
        cost_estimate=pl.CostEstimate(
            flops=2 * tok_count * vheads * 1000 * 1000, bytes_accessed=1 << 23, transcendentals=0
        ),
        name="memory_pass",
    )(key_raw, value_raw, rim, conv_key, conv_value, gate_flat, logit_flat)


def rows_kernel(
    kheads,
    vheads,
    group,
    span,
    query_ref,
    rim_ref,
    tap_ref,
    key_ref,
    gate_ref,
    logit_ref,
    solved_ref,
    before_ref,
    rows_ref,
    local_ref,
    wide,
):
    ratio = vheads // kheads
    first_head = group * vheads
    query_from = group * kheads * DK
    for tile in range(kheads):
        at = slice(query_from + tile * DK, query_from + (tile + 1) * DK)
        wide[tile, 0:HALO] = rim_ref[:, at].astype(F32)[RIM - HALO :]

    def advance(step, carry):
        base = pl.multiple_of(step * span, span)
        now_rows = pl.ds(base, span)
        taps = tap_ref[...].astype(F32) * 0.5
        queries = []
        for tile in range(kheads):
            at = slice(query_from + tile * DK, query_from + (tile + 1) * DK)
            queries.append(unit(conv(query_ref[now_rows, at], wide, tile, taps[:, at]), DK**-0.5))

        for tile in range(kheads):
            wide[tile, 0:HALO] = wide[tile, span : span + HALO]
        rows, cols = iotas((CHUNK, CHUNK))
        lower = rows >= cols
        cums = sums(gate_ref[:, now_rows] * LOG2E, span)
        strengths = log_weights(logit_ref[:, now_rows])
        for part in range(span // CHUNK):
            here = slice(part * CHUNK, (part + 1) * CHUNK)
            place_rows = pl.ds(base + part * CHUNK, CHUNK)
            cum_flat = cums[part]
            cum = cum_flat.T
            lift = strengths[:, here] - cum_flat
            for khead in range(kheads):
                query = queries[khead][here]
                gram = lax.dot_general(
                    query,
                    key_ref[group, place_rows, khead * DK : (khead + 1) * DK],
                    (((1,), (1,)), ((), ())),
                    preferred_element_type=F32,
                )
                for which in range(ratio):
                    head = khead * ratio + which
                    place = first_head + head
                    there = slice(head * DV, (head + 1) * DV)
                    cum_col = jnp.broadcast_to(cum[:, place : place + 1], (CHUNK, CHUNK))
                    powers = cum_col + lift[place : place + 1]
                    scores = (gram * jnp.exp2(jnp.where(lower, powers, -jnp.inf))).astype(BF16)
                    product = dot(scores, solved_ref[group, place_rows, head * WIDE : (head + 1) * WIDE])
                    meet = query.astype(F32) * jnp.exp2(cum_col) - product[:, :DK]
                    final = dot(meet.astype(BF16), before_ref[group, step * (span // CHUNK) + part, head])
                    rows_ref[place_rows, there] = final[:, :DK].astype(BF16)
                    local_ref[place_rows, there] = (final[:, DK:] + product[:, DK:]).astype(BF16)
        return carry

    lax.fori_loop(0, query_ref.shape[0] // span, advance, 0)


def rows_pass(part, query_raw, rim, conv_query, keys, gate_flat, logit_flat, solved, before):
    tok_count = query_raw.shape[0]
    kheads = query_raw.shape[1] // DK // PARTS
    all_vheads = gate_flat.shape[0]
    vheads = all_vheads // PARTS
    span = min(SPAN_Y, tok_count)

    def kernel(*refs):
        rows_kernel(kheads, vheads, part, span, *refs)

    return pl.pallas_call(
        kernel,
        in_specs=[VMEM] * 8,
        out_specs=[VMEM] * 2,
        out_shape=[
            jax.ShapeDtypeStruct((tok_count, vheads * DV), BF16),
            jax.ShapeDtypeStruct((tok_count, vheads * DV), BF16),
        ],
        scratch_shapes=[pltpu.VMEM((kheads, span + HALO, 128), F32)],
        compiler_params=pltpu.CompilerParams(vmem_limit_bytes=16 * 1024 * 1024),
        cost_estimate=pl.CostEstimate(
            flops=2 * tok_count * vheads * 1000 * 500, bytes_accessed=1 << 23, transcendentals=0
        ),
        name="rows_pass",
    )(query_raw, rim, conv_query, keys, gate_flat, logit_flat, solved, before)


def final_kernel(part, span, rows_ref, local_ref, early_ref, late_ref, gain_ref, *rest):
    out_ref, ready, done = rest[-3:]
    gain = gain_ref[...]
    vheads = early_ref.shape[0]
    width = vheads * DV
    starts = [early_ref[head] + late_ref[head] for head in range(vheads)]

    def copy_of(turn):
        here = pl.ds(pl.multiple_of(turn * span, span), span)
        target = out_ref.at[here, pl.ds(part * width, width)]
        return pltpu.make_async_copy(ready.at[here, :], target, done.at[turn])

    def advance(turn, carry):
        here = pl.ds(pl.multiple_of(turn * span, span), span)
        for head in range(vheads):
            there = slice(head * DV, (head + 1) * DV)
            output = dot(rows_ref[here, there], starts[head]) + local_ref[here, there].astype(F32)
            square = output * output
            if head % 2:
                total = row_sums(square)
            else:
                total = jnp.sum(square, axis=-1, keepdims=True)
            scale = lax.rsqrt(total * (1.0 / DV) + EPSILON)
            ready[here, there] = (output * scale * gain).astype(BF16)
        copy_of(turn).start()
        return carry

    turns = rows_ref.shape[0] // span
    lax.fori_loop(0, turns, advance, 0)
    for turn in range(turns):
        copy_of(turn).wait()


def final_pass(part, rows, local, early, late, gain, earlier):
    tok_count = rows.shape[0]
    vheads = early.shape[0]
    span = min(SPAN_Z, tok_count)

    def kernel(*refs):
        final_kernel(part, span, *refs)

    anywhere = pl.BlockSpec(memory_space=pl.ANY)
    arrays = [rows, local, early, late, gain]
    specs = [VMEM] * 5
    if earlier is not None:
        arrays.append(earlier)
        specs.append(anywhere)
    return pl.pallas_call(
        kernel,
        in_specs=specs,
        out_specs=anywhere,
        out_shape=jax.ShapeDtypeStruct((tok_count, PARTS * vheads * DV), BF16),
        scratch_shapes=[
            pltpu.VMEM((tok_count, vheads * DV), BF16),
            pltpu.SemaphoreType.DMA((tok_count // span,)),
        ],
        input_output_aliases={} if earlier is None else {5: 0},
        compiler_params=pltpu.CompilerParams(vmem_limit_bytes=12 * 1024 * 1024),
        name="final_pass",
    )(*arrays)


def shards(
    query_raw, key_raw, value_raw, conv_query, conv_key, conv_value, gate_log, beta_logit, norm_gain
):
    count = lax.axis_size("ctx")
    rim = lax.ppermute(
        pack_rim(query_raw, key_raw, value_raw), "ctx", [(at, at + 1) for at in range(count - 1)]
    )
    gate_flat, logit_flat = gate_log.T, beta_logit.T
    gain = norm_gain.reshape(1, DV)
    keys, solved, before, transit, memory = memory_pass(
        key_raw, value_raw, rim, conv_key, conv_value, gate_flat, logit_flat
    )
    def after(value, *others):
        return lax.optimization_barrier((value, *others))[0]

    moved = [[memory[part].astype(BF16)] for part in range(PARTS)]
    got = [[] for _ in range(PARTS)]
    second = [None] * PARTS

    def send(part):
        source = len(got[part])
        got[part].append(lax.ppermute(moved[part][source], "ctx", [(source, source + 1)]))

    def carry(part, *others):
        arrived = after(got[part][-1], *others)
        ahead = jnp.einsum("hab,hbc->hac", transit[part], arrived, preferred_element_type=F32)
        moved[part].append((ahead + memory[part]).astype(BF16))

    def rows_of(part, *others):
        second[part] = rows_pass(
            part,
            query_raw,
            rim,
            conv_query,
            keys,
            gate_flat,
            logit_flat,
            after(solved, *others),
            before,
        )

    for turn in range(count - 1):
        for part in range(PARTS):
            send(part)
            if turn + 1 < count - 1:
                waits = [] if part == 0 or turn >= PARTS else [second[turn][1]]
                carry(part, *waits)
            if part == 0 and turn < PARTS:
                ready = [moved[part][-1] for part in range(PARTS)]
                rows_of(turn, *ready)
    out = None
    for part in range(PARTS):
        rows, local = second[part]
        early = sum(got[part][:-1], jnp.zeros_like(got[part][-1]))
        late = got[part][-1]
        if part + 1 < PARTS:
            late = after(late, moved[part + 1][-1])
        out = final_pass(part, rows, local, early, late, gain, out)
    return out


def solution(mesh):
    return jax.shard_map(
        shards,
        mesh=mesh,
        in_specs=(
            P(("groups", "ctx"), "head"),
            P(("groups", "ctx"), "head"),
            P(("groups", "ctx"), "head"),
            P(None, "head"),
            P(None, "head"),
            P(None, "head"),
            P(("groups", "ctx"), "head"),
            P(("groups", "ctx"), "head"),
            P(),
        ),
        out_specs=P(("groups", "ctx"), "head"),
        check_vma=False,
    )
```

```python
import jax
import jax.numpy as jnp
from jax import lax
from jax.experimental import pallas as pl
from jax.experimental.pallas import tpu as pltpu
from jax.sharding import PartitionSpec as P

DK = 128
DV = 128
KW = 4
CHUNK = 128
HALF = 64
BASE = 8
HALO = 8
RIM = 16
FOLD = 4
PARTS = 2
SPAN_X = 512
SPAN_Y = 512
EPSILON = 1e-06
LOG2E = 1.4426950408889634
F32 = jnp.float32
BF16 = jnp.bfloat16
WIDE = DK + DV
VMEM = pl.BlockSpec(memory_space=pltpu.VMEM)


def dot(left, right):
    return jnp.dot(left, right, preferred_element_type=F32)


def levels():
    sizes = []
    size = BASE
    while size < HALF:
        sizes.append(size)
        size *= 2
    return sizes


def iotas(shape):
    return lax.broadcasted_iota(jnp.int32, shape, 0), lax.broadcasted_iota(jnp.int32, shape, 1)


def fill_masks(diag_ref):
    rows, cols = iotas((CHUNK, CHUNK))
    for place, size in enumerate(levels()):
        diag_ref[place] = (rows // size == cols // size).astype(BF16)


def packed(strip):
    if strip.shape[0] < 16:
        strip = jnp.concatenate([strip] * (16 // strip.shape[0]), axis=0)
    return strip.astype(BF16)


def spread(strip, mask):
    count = CHUNK // strip.shape[0]
    return jnp.concatenate([strip] * count, axis=0) * mask


def strips(neg, size, step, first):
    lanes = lax.broadcasted_iota(jnp.int32, (1, CHUNK), 1)
    out = neg[first : first + size]
    for turn in range(1, CHUNK // step):
        start = turn * step + first
        out = jnp.where(lanes // step == turn, neg[start : start + size], out)
    return out


def substitute(strip):
    rows, cols = iotas((8, CHUNK))
    halves = [strip[at : at + 8] for at in range(0, BASE, 8)]
    found = [(rows + at == cols % BASE).astype(F32) for at in range(0, BASE, 8)]
    for row in range(BASE - 1):
        at = cols // BASE * BASE + row
        solved = found[row // 8][row % 8 : row % 8 + 1]
        for half in range((row + 1) // 8, BASE // 8):
            column = jnp.take_along_axis(halves[half], at, axis=1)
            found[half] = found[half] + column * solved
    return jnp.concatenate(found, axis=0)


def half_inverses(negs, diag_ref):
    lanes = lax.broadcasted_iota(jnp.int32, (1, CHUNK), 1)
    found = [substitute(strips(neg, BASE, BASE, 0)) for neg in negs]
    pairs = range(0, len(negs), 2)
    for place, size in enumerate(levels()):
        even = (lanes // size) % 2 == 0

        def up(value):
            return pltpu.roll(value, size, 1)

        def down(value):
            return pltpu.roll(value, CHUNK - size, 1)

        lowers = [strips(neg, size, 2 * size, size) for neg in negs]
        evens = [packed(jnp.where(even, found[i], up(found[i + 1]))) for i in pairs]
        odds = [packed(jnp.where(even, down(found[i]), found[i + 1])) for i in pairs]
        both = [packed(jnp.where(even, lowers[i], up(lowers[i + 1]))) for i in pairs]
        weights = [spread(value, diag_ref[place]) for value in evens]
        middles = [dot(value, weight).astype(BF16) for value, weight in zip(both, weights)]
        weights = [spread(value, diag_ref[place]) for value in middles]
        corners = [dot(value, weight)[:size] for value, weight in zip(odds, weights)]
        wider = []
        for i, f in enumerate(found):
            corner = corners[i // 2] if i % 2 == 0 else down(corners[i // 2])
            wider.append(
                jnp.concatenate([jnp.where(even, f, 0.0), jnp.where(even, corner, f)], axis=0)
            )
        found = wider
    return [f.astype(BF16) for f in found]


def conv(raw, wide, tile, tap):
    span = raw.shape[0]
    raw = raw.astype(F32)
    wide[tile, HALO : HALO + span] = raw
    total = raw * tap[KW - 1 : KW]
    for back in range(1, KW):
        total += wide[tile, HALO - back : HALO - back + span] * tap[KW - 1 - back : KW - back]
    return (total + total * jnp.tanh(total)).astype(BF16)


def row_sums(values):
    return dot(values.astype(BF16), jnp.ones((values.shape[1], values.shape[1]), BF16))


def unit(values, factor):
    values = values.astype(F32)
    scale = lax.rsqrt(jnp.sum(values * values, axis=-1, keepdims=True) + EPSILON)
    if factor != 1.0:
        scale = scale * factor
    return (values * scale).astype(BF16)


def sums(gates, span):
    rows, cols = iotas((CHUNK, CHUNK))
    stacked = jnp.concatenate(
        [gates[:, at : at + CHUNK] for at in range(0, span, CHUNK)], axis=0
    )
    total = jnp.dot(
        stacked,
        (rows <= cols).astype(F32),
        precision=lax.Precision.HIGHEST,
        preferred_element_type=F32,
    )
    heads = gates.shape[0]
    return [total[at * heads : (at + 1) * heads] for at in range(span // CHUNK)]


def rim_kernel(query_ref, key_ref, value_ref, out_ref, rows):
    piece = rows.shape[1]
    rows[...] = jnp.zeros_like(rows)
    at = 0
    for ref in (query_ref, key_ref, value_ref):
        last = ref[...].astype(F32)
        for tile in range(0, ref.shape[1], 128):
            place, lane = (at + tile) // piece, (at + tile) % piece
            for back in range(KW - 1):
                row = back * FOLD + place
                source = RIM - (KW - 1) + back
                rows[row : row + 1, lane : lane + 128] = last[source : source + 1, tile : tile + 128]
        at += ref.shape[1]
    out_ref[...] = rows[...].astype(BF16)


def pack_rim(query_raw, key_raw, value_raw):
    last = query_raw.shape[0] // RIM - 1
    widths = [array.shape[1] for array in (query_raw, key_raw, value_raw)]
    piece = sum(widths) // FOLD
    return pl.pallas_call(
        rim_kernel,
        grid=(1,),
        in_specs=[pl.BlockSpec((RIM, width), lambda i: (last, 0)) for width in widths],
        out_specs=pl.BlockSpec((RIM, piece), lambda i: (0, 0)),
        out_shape=jax.ShapeDtypeStruct((RIM, piece), BF16),
        scratch_shapes=[pltpu.VMEM((RIM, piece), F32)],
        name="pack_rim",
    )(query_raw, key_raw, value_raw)


def unpack_rim(rim, wide, tile, at):
    piece = rim.shape[1]
    for back in range(KW - 1):
        row = back * FOLD + at // piece
        place = HALO - (KW - 1) + back
        wide[tile, place : place + 1] = rim[row : row + 1, at % piece : at % piece + 128]


def log_weights(logit):
    return (jnp.minimum(logit, 0.0) - jnp.log(1.0 + jnp.exp(-jnp.abs(logit)))) * LOG2E


def memory_kernel(
    kheads,
    vheads,
    part,
    span,
    key_ref,
    value_ref,
    rim_ref,
    tap_key_ref,
    tap_value_ref,
    gate_ref,
    logit_ref,
    unit_ref,
    solved_ref,
    before_ref,
    transit_ref,
    memory_ref,
    wide,
    state,
    diag_ref,
    neg_ref,
    tail_ref,
    right_ref,
    sum_ref,
):
    ratio = vheads // kheads
    tiles = kheads + vheads
    parts = span // CHUNK
    first_head = part * vheads
    key_from = part * kheads * DK
    value_from = part * vheads * DV
    rim_from = (key_ref.shape[1] + key_from, 2 * key_ref.shape[1] + value_from)
    places = [(chunk, head) for chunk in range(parts) for head in range(vheads)]

    def set_up():
        fill_masks(diag_ref)
        rows, cols = iotas((DK, WIDE))
        for head in range(vheads):
            state[head] = (rows == cols).astype(F32)
        rim = rim_ref[...].astype(F32)
        for tile in range(tiles):
            at = rim_from[0] + tile * DK if tile < kheads else rim_from[1] + (tile - kheads) * DV
            unpack_rim(rim, wide, tile, at)

    def prepare(step):
        now_rows = pl.ds(pl.multiple_of(step * span, span), span)
        tap_key = tap_key_ref[...].astype(F32) * 0.5
        tap_value = tap_value_ref[...].astype(F32) * 0.5
        keys = []
        for tile in range(kheads):
            at = slice(tile * DK, (tile + 1) * DK)
            place = slice(key_from + tile * DK, key_from + (tile + 1) * DK)
            keys.append(unit(conv(key_ref[now_rows, place], wide, tile, tap_key[:, place]), 1.0))
            unit_ref[now_rows, at] = keys[tile]
        for tile in range(vheads):
            place = slice(value_from + tile * DV, value_from + (tile + 1) * DV)
            value = conv(value_ref[now_rows, place], wide, kheads + tile, tap_value[:, place])
            for chunk in range(parts):
                right_ref[chunk * vheads + tile, :, DK:] = value[
                    chunk * CHUNK : (chunk + 1) * CHUNK
                ]
        for tile in range(tiles):
            wide[tile, 0:HALO] = wide[tile, span : span + HALO]
        rows, cols = iotas((CHUNK, CHUNK))
        strict = rows > cols
        cums = sums(gate_ref[:, now_rows] * LOG2E, span)
        strengths = log_weights(logit_ref[:, now_rows])
        for chunk in range(parts):
            here = slice(chunk * CHUNK, (chunk + 1) * CHUNK)
            cum_flat = cums[chunk]
            cum = cum_flat.T
            lift = strengths[:, here] - cum_flat
            last = cum_flat[:, CHUNK - 1 :]
            ends = jnp.exp2(last + lift)
            sum_ref[chunk] = jnp.broadcast_to(jnp.exp2(last), cum_flat.shape)
            for khead in range(kheads):
                key = keys[khead][here]
                flat = (-key).T
                gram = dot(key, flat)
                for which in range(ratio):
                    head = khead * ratio + which
                    item = chunk * vheads + head
                    place = first_head + head
                    cum_col = jnp.broadcast_to(cum[:, place : place + 1], (CHUNK, CHUNK))
                    powers = cum_col + lift[place : place + 1]
                    decays = jnp.exp2(jnp.where(strict, powers, -jnp.inf))
                    neg_ref[item] = gram * decays
                    tail_ref[item] = flat * ends[place : place + 1].astype(BF16)
                    right_ref[item, :, :DK] = key * jnp.exp2(cum_col).astype(BF16)

    def finish(step):
        base = pl.multiple_of(step * span, span)
        negs = [neg_ref[item] for item in range(len(places))]
        found = half_inverses(negs, diag_ref)
        tops = [
            dot(f[:, :HALF], right_ref[item, :HALF]).astype(BF16)
            for item, f in enumerate(found)
        ]
        rests = [
            (
                right_ref[item, HALF:].astype(F32)
                + dot(neg_ref[item, HALF:, :HALF].astype(BF16), top)
            ).astype(BF16)
            for item, top in enumerate(tops)
        ]
        lows = [dot(f[:, HALF:], rest).astype(BF16) for f, rest in zip(found, rests)]
        erases, writes = [], []
        for item, (chunk, head) in enumerate(places):
            there = slice(head * WIDE, (head + 1) * WIDE)
            solved = jnp.concatenate([tops[item], lows[item]], axis=0)
            solved_ref[pl.ds(base + chunk * CHUNK, CHUNK), there] = solved
            product = dot(tail_ref[item], solved)
            erases.append(product[:, :DK].astype(BF16))
            writes.append(product[:, DK:])
        for item, (chunk, head) in enumerate(places):
            now = state[head]
            short = now.astype(BF16)
            before_ref[step * parts + chunk, head] = short
            tail = sum_ref[chunk, first_head + head : first_head + head + 1]
            change = dot(erases[item], short)
            state[head, :, :DK] = now[:, :DK] * tail + change[:, :DK]
            state[head, :, DK:] = now[:, DK:] * tail + (change[:, DK:] - writes[item])

    def advance(step, carry):
        prepare(step)
        finish(step)
        return carry

    set_up()
    lax.fori_loop(0, key_ref.shape[0] // span, advance, 0)
    for head in range(vheads):
        transit_ref[head] = state[head, :, :DK].astype(BF16)
        memory_ref[head] = state[head, :, DK:]


def memory_pass(part, key_raw, value_raw, rim, conv_key, conv_value, gate_flat, logit_flat):
    tok_count = key_raw.shape[0]
    all_kheads = key_raw.shape[1] // DK
    all_vheads = value_raw.shape[1] // DV
    kheads, vheads = all_kheads // PARTS, all_vheads // PARTS
    tiles = kheads + vheads
    span = min(SPAN_X, tok_count)
    chunks = tok_count // CHUNK
    items = span // CHUNK * vheads
    count = len(levels())

    def kernel(*refs):
        memory_kernel(kheads, vheads, part, span, *refs)

    return pl.pallas_call(
        kernel,
        in_specs=[VMEM] * 7,
        out_specs=[VMEM] * 5,
        out_shape=[
            jax.ShapeDtypeStruct((tok_count, kheads * DK), BF16),
            jax.ShapeDtypeStruct((tok_count, vheads * WIDE), BF16),
            jax.ShapeDtypeStruct((chunks, vheads, DK, WIDE), BF16),
            jax.ShapeDtypeStruct((vheads, DK, DK), BF16),
            jax.ShapeDtypeStruct((vheads, DK, DV), F32),
        ],
        scratch_shapes=[
            pltpu.VMEM((tiles, span + HALO, 128), F32),
            pltpu.VMEM((vheads, DK, WIDE), F32),
            pltpu.VMEM((count, CHUNK, CHUNK), BF16),
            pltpu.VMEM((items, CHUNK, CHUNK), F32),
            pltpu.VMEM((items, CHUNK, CHUNK), BF16),
            pltpu.VMEM((items, CHUNK, WIDE), BF16),
            pltpu.VMEM((span // CHUNK, all_vheads, CHUNK), F32),
        ],
        compiler_params=pltpu.CompilerParams(vmem_limit_bytes=20 * 1024 * 1024),
        cost_estimate=pl.CostEstimate(
            flops=2 * tok_count * vheads * 1000 * 1000, bytes_accessed=1 << 23, transcendentals=0
        ),
        name="memory_pass",
    )(key_raw, value_raw, rim, conv_key, conv_value, gate_flat, logit_flat)


def rows_kernel(
    kheads,
    vheads,
    group,
    span,
    query_ref,
    rim_ref,
    tap_ref,
    key_ref,
    gate_ref,
    logit_ref,
    solved_ref,
    before_ref,
    rows_ref,
    local_ref,
    wide,
):
    ratio = vheads // kheads
    first_head = group * vheads
    query_from = group * kheads * DK
    for tile in range(kheads):
        unpack_rim(rim_ref[...].astype(F32), wide, tile, query_from + tile * DK)

    def advance(step, carry):
        base = pl.multiple_of(step * span, span)
        now_rows = pl.ds(base, span)
        taps = tap_ref[...].astype(F32) * 0.5
        queries = []
        for tile in range(kheads):
            at = slice(query_from + tile * DK, query_from + (tile + 1) * DK)
            queries.append(unit(conv(query_ref[now_rows, at], wide, tile, taps[:, at]), DK**-0.5))

        for tile in range(kheads):
            wide[tile, 0:HALO] = wide[tile, span : span + HALO]
        rows, cols = iotas((CHUNK, CHUNK))
        lower = rows >= cols
        cums = sums(gate_ref[:, now_rows] * LOG2E, span)
        strengths = log_weights(logit_ref[:, now_rows])
        for part in range(span // CHUNK):
            here = slice(part * CHUNK, (part + 1) * CHUNK)
            place_rows = pl.ds(base + part * CHUNK, CHUNK)
            cum_flat = cums[part]
            cum = cum_flat.T
            lift = strengths[:, here] - cum_flat
            for khead in range(kheads):
                query = queries[khead][here]
                gram = lax.dot_general(
                    query,
                    key_ref[place_rows, khead * DK : (khead + 1) * DK],
                    (((1,), (1,)), ((), ())),
                    preferred_element_type=F32,
                )
                for which in range(ratio):
                    head = khead * ratio + which
                    place = first_head + head
                    there = slice(head * DV, (head + 1) * DV)
                    cum_col = jnp.broadcast_to(cum[:, place : place + 1], (CHUNK, CHUNK))
                    powers = cum_col + lift[place : place + 1]
                    scores = (gram * jnp.exp2(jnp.where(lower, powers, -jnp.inf))).astype(BF16)
                    product = dot(scores, solved_ref[place_rows, head * WIDE : (head + 1) * WIDE])
                    meet = query.astype(F32) * jnp.exp2(cum_col) - product[:, :DK]
                    final = dot(meet.astype(BF16), before_ref[step * (span // CHUNK) + part, head])
                    rows_ref[place_rows, there] = final[:, :DK].astype(BF16)
                    local_ref[place_rows, there] = (final[:, DK:] + product[:, DK:]).astype(BF16)
        return carry

    lax.fori_loop(0, query_ref.shape[0] // span, advance, 0)


def rows_pass(part, query_raw, rim, conv_query, keys, gate_flat, logit_flat, solved, before):
    tok_count = query_raw.shape[0]
    kheads = query_raw.shape[1] // DK // PARTS
    all_vheads = gate_flat.shape[0]
    vheads = all_vheads // PARTS
    span = min(SPAN_Y, tok_count)

    def kernel(*refs):
        rows_kernel(kheads, vheads, part, span, *refs)

    return pl.pallas_call(
        kernel,
        in_specs=[VMEM] * 8,
        out_specs=[VMEM] * 2,
        out_shape=[
            jax.ShapeDtypeStruct((tok_count, vheads * DV), BF16),
            jax.ShapeDtypeStruct((tok_count, vheads * DV), BF16),
        ],
        scratch_shapes=[pltpu.VMEM((kheads, span + HALO, 128), F32)],
        compiler_params=pltpu.CompilerParams(vmem_limit_bytes=16 * 1024 * 1024),
        cost_estimate=pl.CostEstimate(
            flops=2 * tok_count * vheads * 1000 * 500, bytes_accessed=1 << 23, transcendentals=0
        ),
        name="rows_pass",
    )(query_raw, rim, conv_query, keys, gate_flat, logit_flat, solved, before)


def final_kernel(vheads, rows_ref, local_ref, early_ref, late_ref, gain_ref, *rest):
    out_ref = rest[-1]
    gain = gain_ref[...]
    span = out_ref.shape[0]
    now_rows = pl.ds(pl.multiple_of(pl.program_id(0) * span, span), span)
    for head in range(vheads):
        there = slice(head * DV, (head + 1) * DV)
        start = early_ref[head] + late_ref[head]
        output = dot(rows_ref[now_rows, there], start) + local_ref[now_rows, there].astype(F32)
        square = output * output
        if head % 2:
            total = row_sums(square)
        else:
            total = jnp.sum(square, axis=-1, keepdims=True)
        mean = total * (1.0 / DV)
        out_ref[:, there] = (output * lax.rsqrt(mean + EPSILON) * gain).astype(BF16)


def final_pass(part, rows, local, early, late, gain, earlier):
    tok_count = rows.shape[0]
    vheads = early.shape[0]
    span = min(512, tok_count)

    def along(width, column):
        return pl.BlockSpec((span, width), lambda i: (i, column))

    def kernel(*refs):
        final_kernel(vheads, *refs)

    arrays = [rows, local, early, late, gain]
    specs = [VMEM] * 5
    if earlier is not None:
        arrays.append(earlier)
        specs.append(pl.BlockSpec(memory_space=pl.ANY))
    return pl.pallas_call(
        kernel,
        grid=(tok_count // span,),
        in_specs=specs,
        out_specs=along(vheads * DV, part),
        out_shape=jax.ShapeDtypeStruct((tok_count, PARTS * vheads * DV), BF16),
        input_output_aliases={} if earlier is None else {5: 0},
        compiler_params=pltpu.CompilerParams(vmem_limit_bytes=12 * 1024 * 1024),
        name="final_pass",
    )(*arrays)


def shards(
    query_raw, key_raw, value_raw, conv_query, conv_key, conv_value, gate_log, beta_logit, norm_gain
):
    count = lax.axis_size("ctx")
    rim = lax.ppermute(
        pack_rim(query_raw, key_raw, value_raw), "ctx", [(at, at + 1) for at in range(count - 1)]
    )
    gate_flat, logit_flat = gate_log.T, beta_logit.T
    gain = norm_gain.reshape(1, DV)
    first = [
        memory_pass(part, key_raw, value_raw, rim, conv_key, conv_value, gate_flat, logit_flat)
        for part in range(PARTS)
    ]
    def after(value, *others):
        return lax.optimization_barrier((value, *others))[0]

    moved = [[found[4].astype(BF16)] for found in first]
    got = [[] for _ in first]
    second = [None] * PARTS

    def send(part):
        source = len(got[part])
        got[part].append(lax.ppermute(moved[part][source], "ctx", [(source, source + 1)]))

    def carry(part, *others):
        transit, memory = first[part][3:]
        arrived = after(got[part][-1], *others)
        ahead = jnp.einsum("hab,hbc->hac", transit, arrived, preferred_element_type=F32)
        moved[part].append((ahead + memory).astype(BF16))

    def rows_of(part, *others):
        keys, solved, before = first[part][:3]
        second[part] = rows_pass(
            part,
            query_raw,
            rim,
            conv_query,
            keys,
            gate_flat,
            logit_flat,
            after(solved, *others),
            before,
        )

    for turn in range(count - 1):
        for part in range(PARTS):
            send(part)
            if turn + 1 < count - 1:
                waits = [] if part == 0 or turn >= PARTS else [second[turn][1]]
                carry(part, *waits)
            if part == 0 and turn < PARTS:
                ready = [moved[part][-1] for part in range(PARTS)]
                rows_of(turn, *ready)
    out = None
    for part in range(PARTS):
        rows, local = second[part]
        early = sum(got[part][:-1], jnp.zeros_like(got[part][-1]))
        late = got[part][-1]
        if part + 1 < PARTS:
            late = after(late, moved[part + 1][-1])
        out = final_pass(part, rows, local, early, late, gain, out)
    return out


def solution(mesh):
    return jax.shard_map(
        shards,
        mesh=mesh,
        in_specs=(
            P(("groups", "ctx"), "head"),
            P(("groups", "ctx"), "head"),
            P(("groups", "ctx"), "head"),
            P(None, "head"),
            P(None, "head"),
            P(None, "head"),
            P(("groups", "ctx"), "head"),
            P(("groups", "ctx"), "head"),
            P(),
        ),
        out_specs=P(("groups", "ctx"), "head"),
        check_vma=False,
    )
```

```python
import jax
import jax.numpy as jnp
from jax import lax
from jax.experimental import pallas as pl
from jax.experimental.pallas import tpu as pltpu
from jax.sharding import PartitionSpec as P

DK = 128
DV = 128
KW = 4
CHUNK = 128
HALF = 64
BASE = 8
HALO = 8
RIM = 16
FOLD = 4
PARTS = 2
SPAN_X = 1024
SPAN_Y = 512
EPSILON = 1e-06
LOG2E = 1.4426950408889634
F32 = jnp.float32
BF16 = jnp.bfloat16
WIDE = DK + DV
VMEM = pl.BlockSpec(memory_space=pltpu.VMEM)


def dot(left, right):
    return jnp.dot(left, right, preferred_element_type=F32)


def levels():
    sizes = []
    size = BASE
    while size < HALF:
        sizes.append(size)
        size *= 2
    return sizes


def iotas(shape):
    return lax.broadcasted_iota(jnp.int32, shape, 0), lax.broadcasted_iota(jnp.int32, shape, 1)


def fill_masks(diag_ref):
    rows, cols = iotas((CHUNK, CHUNK))
    for place, size in enumerate(levels()):
        diag_ref[place] = (rows // size == cols // size).astype(BF16)


def packed(strip):
    if strip.shape[0] < 16:
        strip = jnp.concatenate([strip] * (16 // strip.shape[0]), axis=0)
    return strip.astype(BF16)


def spread(strip, mask):
    count = CHUNK // strip.shape[0]
    return jnp.concatenate([strip] * count, axis=0) * mask


def strips(neg, size, step, first):
    lanes = lax.broadcasted_iota(jnp.int32, (1, CHUNK), 1)
    out = neg[first : first + size]
    for turn in range(1, CHUNK // step):
        start = turn * step + first
        out = jnp.where(lanes // step == turn, neg[start : start + size], out)
    return out


def substitute(strip):
    rows, cols = iotas((8, CHUNK))
    halves = [strip[at : at + 8] for at in range(0, BASE, 8)]
    found = [(rows + at == cols % BASE).astype(F32) for at in range(0, BASE, 8)]
    for row in range(BASE - 1):
        at = cols // BASE * BASE + row
        solved = found[row // 8][row % 8 : row % 8 + 1]
        for half in range((row + 1) // 8, BASE // 8):
            column = jnp.take_along_axis(halves[half], at, axis=1)
            found[half] = found[half] + column * solved
    return jnp.concatenate(found, axis=0)


def half_inverses(negs, diag_ref):
    lanes = lax.broadcasted_iota(jnp.int32, (1, CHUNK), 1)
    found = [substitute(strips(neg, BASE, BASE, 0)) for neg in negs]
    pairs = range(0, len(negs), 2)
    for place, size in enumerate(levels()):
        even = (lanes // size) % 2 == 0

        def up(value):
            return pltpu.roll(value, size, 1)

        def down(value):
            return pltpu.roll(value, CHUNK - size, 1)

        lowers = [strips(neg, size, 2 * size, size) for neg in negs]
        evens = [packed(jnp.where(even, found[i], up(found[i + 1]))) for i in pairs]
        odds = [packed(jnp.where(even, down(found[i]), found[i + 1])) for i in pairs]
        both = [packed(jnp.where(even, lowers[i], up(lowers[i + 1]))) for i in pairs]
        weights = [spread(value, diag_ref[place]) for value in evens]
        middles = [dot(value, weight).astype(BF16) for value, weight in zip(both, weights)]
        weights = [spread(value, diag_ref[place]) for value in middles]
        corners = [dot(value, weight)[:size] for value, weight in zip(odds, weights)]
        wider = []
        for i, f in enumerate(found):
            corner = corners[i // 2] if i % 2 == 0 else down(corners[i // 2])
            wider.append(
                jnp.concatenate([jnp.where(even, f, 0.0), jnp.where(even, corner, f)], axis=0)
            )
        found = wider
    return [f.astype(BF16) for f in found]


def conv(raw, wide, tile, tap):
    span = raw.shape[0]
    raw = raw.astype(F32)
    wide[tile, HALO : HALO + span] = raw
    total = raw * tap[KW - 1 : KW]
    for back in range(1, KW):
        total += wide[tile, HALO - back : HALO - back + span] * tap[KW - 1 - back : KW - back]
    return (total + total * jnp.tanh(total)).astype(BF16)


def row_sums(values):
    return dot(values.astype(BF16), jnp.ones((values.shape[1], values.shape[1]), BF16))


def unit(values, factor):
    values = values.astype(F32)
    scale = lax.rsqrt(jnp.sum(values * values, axis=-1, keepdims=True) + EPSILON)
    if factor != 1.0:
        scale = scale * factor
    return (values * scale).astype(BF16)


def sums(gates, span):
    rows, cols = iotas((CHUNK, CHUNK))
    stacked = jnp.concatenate(
        [gates[:, at : at + CHUNK] for at in range(0, span, CHUNK)], axis=0
    )
    total = jnp.dot(
        stacked,
        (rows <= cols).astype(F32),
        precision=lax.Precision.HIGHEST,
        preferred_element_type=F32,
    )
    heads = gates.shape[0]
    return [total[at * heads : (at + 1) * heads] for at in range(span // CHUNK)]


def rim_kernel(query_ref, key_ref, value_ref, out_ref, rows):
    piece = rows.shape[1]
    rows[...] = jnp.zeros_like(rows)
    at = 0
    for ref in (query_ref, key_ref, value_ref):
        last = ref[...].astype(F32)
        for tile in range(0, ref.shape[1], 128):
            place, lane = (at + tile) // piece, (at + tile) % piece
            for back in range(KW - 1):
                row = back * FOLD + place
                source = RIM - (KW - 1) + back
                rows[row : row + 1, lane : lane + 128] = last[source : source + 1, tile : tile + 128]
        at += ref.shape[1]
    out_ref[...] = rows[...].astype(BF16)


def pack_rim(query_raw, key_raw, value_raw):
    last = query_raw.shape[0] // RIM - 1
    widths = [array.shape[1] for array in (query_raw, key_raw, value_raw)]
    piece = sum(widths) // FOLD
    return pl.pallas_call(
        rim_kernel,
        grid=(1,),
        in_specs=[pl.BlockSpec((RIM, width), lambda i: (last, 0)) for width in widths],
        out_specs=pl.BlockSpec((RIM, piece), lambda i: (0, 0)),
        out_shape=jax.ShapeDtypeStruct((RIM, piece), BF16),
        scratch_shapes=[pltpu.VMEM((RIM, piece), F32)],
        name="pack_rim",
    )(query_raw, key_raw, value_raw)


def unpack_rim(rim, wide, tile, at):
    piece = rim.shape[1]
    for back in range(KW - 1):
        row = back * FOLD + at // piece
        place = HALO - (KW - 1) + back
        wide[tile, place : place + 1] = rim[row : row + 1, at % piece : at % piece + 128]


def log_weights(logit):
    return (jnp.minimum(logit, 0.0) - jnp.log(1.0 + jnp.exp(-jnp.abs(logit)))) * LOG2E


def memory_kernel(
    kheads,
    vheads,
    part,
    span,
    key_ref,
    value_ref,
    rim_ref,
    tap_key_ref,
    tap_value_ref,
    gate_ref,
    logit_ref,
    unit_ref,
    solved_ref,
    before_ref,
    transit_ref,
    memory_ref,
    wide,
    state,
    diag_ref,
    neg_ref,
    tail_ref,
    right_ref,
    sum_ref,
):
    ratio = vheads // kheads
    tiles = kheads + vheads
    parts = span // CHUNK
    first_head = part * vheads
    key_from = part * kheads * DK
    value_from = part * vheads * DV
    rim_from = (key_ref.shape[1] + key_from, 2 * key_ref.shape[1] + value_from)
    places = [(chunk, head) for chunk in range(parts) for head in range(vheads)]

    def set_up():
        fill_masks(diag_ref)
        rows, cols = iotas((DK, WIDE))
        for head in range(vheads):
            state[head] = (rows == cols).astype(F32)
        rim = rim_ref[...].astype(F32)
        for tile in range(tiles):
            at = rim_from[0] + tile * DK if tile < kheads else rim_from[1] + (tile - kheads) * DV
            unpack_rim(rim, wide, tile, at)

    def prepare(step):
        now_rows = pl.ds(pl.multiple_of(step * span, span), span)
        tap_key = tap_key_ref[...].astype(F32) * 0.5
        tap_value = tap_value_ref[...].astype(F32) * 0.5
        keys = []
        for tile in range(kheads):
            at = slice(tile * DK, (tile + 1) * DK)
            place = slice(key_from + tile * DK, key_from + (tile + 1) * DK)
            keys.append(unit(conv(key_ref[now_rows, place], wide, tile, tap_key[:, place]), 1.0))
            unit_ref[now_rows, at] = keys[tile]
        for tile in range(vheads):
            place = slice(value_from + tile * DV, value_from + (tile + 1) * DV)
            value = conv(value_ref[now_rows, place], wide, kheads + tile, tap_value[:, place])
            for chunk in range(parts):
                right_ref[chunk * vheads + tile, :, DK:] = value[
                    chunk * CHUNK : (chunk + 1) * CHUNK
                ]
        for tile in range(tiles):
            wide[tile, 0:HALO] = wide[tile, span : span + HALO]
        rows, cols = iotas((CHUNK, CHUNK))
        strict = rows > cols
        cums = sums(gate_ref[:, now_rows] * LOG2E, span)
        strengths = log_weights(logit_ref[:, now_rows])
        for chunk in range(parts):
            here = slice(chunk * CHUNK, (chunk + 1) * CHUNK)
            cum_flat = cums[chunk]
            cum = cum_flat.T
            lift = strengths[:, here] - cum_flat
            last = cum_flat[:, CHUNK - 1 :]
            ends = jnp.exp2(last + lift)
            sum_ref[chunk] = jnp.broadcast_to(jnp.exp2(last), cum_flat.shape)
            for khead in range(kheads):
                key = keys[khead][here]
                flat = (-key).T
                gram = dot(key, flat)
                for which in range(ratio):
                    head = khead * ratio + which
                    item = chunk * vheads + head
                    place = first_head + head
                    cum_col = jnp.broadcast_to(cum[:, place : place + 1], (CHUNK, CHUNK))
                    powers = cum_col + lift[place : place + 1]
                    decays = jnp.exp2(jnp.where(strict, powers, -jnp.inf))
                    neg_ref[item] = gram * decays
                    tail_ref[item] = flat * ends[place : place + 1].astype(BF16)
                    right_ref[item, :, :DK] = key * jnp.exp2(cum_col).astype(BF16)

    def finish(step):
        base = pl.multiple_of(step * span, span)
        negs = [neg_ref[item] for item in range(len(places))]
        found = half_inverses(negs, diag_ref)
        tops = [
            dot(f[:, :HALF], right_ref[item, :HALF]).astype(BF16)
            for item, f in enumerate(found)
        ]
        rests = [
            (
                right_ref[item, HALF:].astype(F32)
                + dot(neg_ref[item, HALF:, :HALF].astype(BF16), top)
            ).astype(BF16)
            for item, top in enumerate(tops)
        ]
        lows = [dot(f[:, HALF:], rest).astype(BF16) for f, rest in zip(found, rests)]
        erases, writes = [], []
        for item, (chunk, head) in enumerate(places):
            there = slice(head * WIDE, (head + 1) * WIDE)
            solved = jnp.concatenate([tops[item], lows[item]], axis=0)
            solved_ref[pl.ds(base + chunk * CHUNK, CHUNK), there] = solved
            product = dot(tail_ref[item], solved)
            erases.append(product[:, :DK].astype(BF16))
            writes.append(product[:, DK:])
        for item, (chunk, head) in enumerate(places):
            now = state[head]
            short = now.astype(BF16)
            before_ref[step * parts + chunk, head] = short
            tail = sum_ref[chunk, first_head + head : first_head + head + 1]
            change = dot(erases[item], short)
            state[head, :, :DK] = now[:, :DK] * tail + change[:, :DK]
            state[head, :, DK:] = now[:, DK:] * tail + (change[:, DK:] - writes[item])

    def advance(step, carry):
        prepare(step)
        finish(step)
        return carry

    set_up()
    lax.fori_loop(0, key_ref.shape[0] // span, advance, 0)
    for head in range(vheads):
        transit_ref[head] = state[head, :, :DK].astype(BF16)
        memory_ref[head] = state[head, :, DK:]


def memory_pass(part, key_raw, value_raw, rim, conv_key, conv_value, gate_flat, logit_flat):
    tok_count = key_raw.shape[0]
    all_kheads = key_raw.shape[1] // DK
    all_vheads = value_raw.shape[1] // DV
    kheads, vheads = all_kheads // PARTS, all_vheads // PARTS
    tiles = kheads + vheads
    span = min(SPAN_X, tok_count)
    chunks = tok_count // CHUNK
    items = span // CHUNK * vheads
    count = len(levels())

    def kernel(*refs):
        memory_kernel(kheads, vheads, part, span, *refs)

    return pl.pallas_call(
        kernel,
        in_specs=[VMEM] * 7,
        out_specs=[VMEM] * 5,
        out_shape=[
            jax.ShapeDtypeStruct((tok_count, kheads * DK), BF16),
            jax.ShapeDtypeStruct((tok_count, vheads * WIDE), BF16),
            jax.ShapeDtypeStruct((chunks, vheads, DK, WIDE), BF16),
            jax.ShapeDtypeStruct((vheads, DK, DK), BF16),
            jax.ShapeDtypeStruct((vheads, DK, DV), F32),
        ],
        scratch_shapes=[
            pltpu.VMEM((tiles, span + HALO, 128), F32),
            pltpu.VMEM((vheads, DK, WIDE), F32),
            pltpu.VMEM((count, CHUNK, CHUNK), BF16),
            pltpu.VMEM((items, CHUNK, CHUNK), F32),
            pltpu.VMEM((items, CHUNK, CHUNK), BF16),
            pltpu.VMEM((items, CHUNK, WIDE), BF16),
            pltpu.VMEM((span // CHUNK, all_vheads, CHUNK), F32),
        ],
        compiler_params=pltpu.CompilerParams(vmem_limit_bytes=32 * 1024 * 1024),
        cost_estimate=pl.CostEstimate(
            flops=2 * tok_count * vheads * 1000 * 1000, bytes_accessed=1 << 23, transcendentals=0
        ),
        name="memory_pass",
    )(key_raw, value_raw, rim, conv_key, conv_value, gate_flat, logit_flat)


def rows_kernel(
    kheads,
    vheads,
    group,
    span,
    query_ref,
    rim_ref,
    tap_ref,
    key_ref,
    gate_ref,
    logit_ref,
    solved_ref,
    before_ref,
    rows_ref,
    local_ref,
    wide,
):
    ratio = vheads // kheads
    first_head = group * vheads
    query_from = group * kheads * DK
    for tile in range(kheads):
        unpack_rim(rim_ref[...].astype(F32), wide, tile, query_from + tile * DK)

    def advance(step, carry):
        base = pl.multiple_of(step * span, span)
        now_rows = pl.ds(base, span)
        taps = tap_ref[...].astype(F32) * 0.5
        queries = []
        for tile in range(kheads):
            at = slice(query_from + tile * DK, query_from + (tile + 1) * DK)
            queries.append(unit(conv(query_ref[now_rows, at], wide, tile, taps[:, at]), DK**-0.5))

        for tile in range(kheads):
            wide[tile, 0:HALO] = wide[tile, span : span + HALO]
        rows, cols = iotas((CHUNK, CHUNK))
        lower = rows >= cols
        cums = sums(gate_ref[:, now_rows] * LOG2E, span)
        strengths = log_weights(logit_ref[:, now_rows])
        for part in range(span // CHUNK):
            here = slice(part * CHUNK, (part + 1) * CHUNK)
            place_rows = pl.ds(base + part * CHUNK, CHUNK)
            cum_flat = cums[part]
            cum = cum_flat.T
            lift = strengths[:, here] - cum_flat
            for khead in range(kheads):
                query = queries[khead][here]
                gram = lax.dot_general(
                    query,
                    key_ref[place_rows, khead * DK : (khead + 1) * DK],
                    (((1,), (1,)), ((), ())),
                    preferred_element_type=F32,
                )
                for which in range(ratio):
                    head = khead * ratio + which
                    place = first_head + head
                    there = slice(head * DV, (head + 1) * DV)
                    cum_col = jnp.broadcast_to(cum[:, place : place + 1], (CHUNK, CHUNK))
                    powers = cum_col + lift[place : place + 1]
                    scores = (gram * jnp.exp2(jnp.where(lower, powers, -jnp.inf))).astype(BF16)
                    product = dot(scores, solved_ref[place_rows, head * WIDE : (head + 1) * WIDE])
                    meet = query.astype(F32) * jnp.exp2(cum_col) - product[:, :DK]
                    final = dot(meet.astype(BF16), before_ref[step * (span // CHUNK) + part, head])
                    rows_ref[place_rows, there] = final[:, :DK].astype(BF16)
                    local_ref[place_rows, there] = (final[:, DK:] + product[:, DK:]).astype(BF16)
        return carry

    lax.fori_loop(0, query_ref.shape[0] // span, advance, 0)


def rows_pass(part, query_raw, rim, conv_query, keys, gate_flat, logit_flat, solved, before):
    tok_count = query_raw.shape[0]
    kheads = query_raw.shape[1] // DK // PARTS
    all_vheads = gate_flat.shape[0]
    vheads = all_vheads // PARTS
    span = min(SPAN_Y, tok_count)

    def kernel(*refs):
        rows_kernel(kheads, vheads, part, span, *refs)

    return pl.pallas_call(
        kernel,
        in_specs=[VMEM] * 8,
        out_specs=[VMEM] * 2,
        out_shape=[
            jax.ShapeDtypeStruct((tok_count, vheads * DV), BF16),
            jax.ShapeDtypeStruct((tok_count, vheads * DV), BF16),
        ],
        scratch_shapes=[pltpu.VMEM((kheads, span + HALO, 128), F32)],
        compiler_params=pltpu.CompilerParams(vmem_limit_bytes=16 * 1024 * 1024),
        cost_estimate=pl.CostEstimate(
            flops=2 * tok_count * vheads * 1000 * 500, bytes_accessed=1 << 23, transcendentals=0
        ),
        name="rows_pass",
    )(query_raw, rim, conv_query, keys, gate_flat, logit_flat, solved, before)


def final_kernel(vheads, rows_ref, local_ref, early_ref, late_ref, gain_ref, *rest):
    out_ref = rest[-1]
    gain = gain_ref[...]
    span = out_ref.shape[0]
    now_rows = pl.ds(pl.multiple_of(pl.program_id(0) * span, span), span)
    for head in range(vheads):
        there = slice(head * DV, (head + 1) * DV)
        start = early_ref[head] + late_ref[head]
        output = dot(rows_ref[now_rows, there], start) + local_ref[now_rows, there].astype(F32)
        square = output * output
        if head % 2:
            total = row_sums(square)
        else:
            total = jnp.sum(square, axis=-1, keepdims=True)
        mean = total * (1.0 / DV)
        out_ref[:, there] = (output * lax.rsqrt(mean + EPSILON) * gain).astype(BF16)


def final_pass(part, rows, local, early, late, gain, earlier):
    tok_count = rows.shape[0]
    vheads = early.shape[0]
    span = min(512, tok_count)

    def along(width, column):
        return pl.BlockSpec((span, width), lambda i: (i, column))

    def kernel(*refs):
        final_kernel(vheads, *refs)

    arrays = [rows, local, early, late, gain]
    specs = [VMEM] * 5
    if earlier is not None:
        arrays.append(earlier)
        specs.append(pl.BlockSpec(memory_space=pl.ANY))
    return pl.pallas_call(
        kernel,
        grid=(tok_count // span,),
        in_specs=specs,
        out_specs=along(vheads * DV, part),
        out_shape=jax.ShapeDtypeStruct((tok_count, PARTS * vheads * DV), BF16),
        input_output_aliases={} if earlier is None else {5: 0},
        compiler_params=pltpu.CompilerParams(vmem_limit_bytes=12 * 1024 * 1024),
        name="final_pass",
    )(*arrays)


def shards(
    query_raw, key_raw, value_raw, conv_query, conv_key, conv_value, gate_log, beta_logit, norm_gain
):
    count = lax.axis_size("ctx")
    rim = lax.ppermute(
        pack_rim(query_raw, key_raw, value_raw), "ctx", [(at, at + 1) for at in range(count - 1)]
    )
    gate_flat, logit_flat = gate_log.T, beta_logit.T
    gain = norm_gain.reshape(1, DV)
    first = [
        memory_pass(part, key_raw, value_raw, rim, conv_key, conv_value, gate_flat, logit_flat)
        for part in range(PARTS)
    ]
    def after(value, *others):
        return lax.optimization_barrier((value, *others))[0]

    moved = [[found[4].astype(BF16)] for found in first]
    got = [[] for _ in first]
    second = [None] * PARTS

    def send(part):
        source = len(got[part])
        got[part].append(lax.ppermute(moved[part][source], "ctx", [(source, source + 1)]))

    def carry(part, *others):
        transit, memory = first[part][3:]
        arrived = after(got[part][-1], *others)
        ahead = jnp.einsum("hab,hbc->hac", transit, arrived, preferred_element_type=F32)
        moved[part].append((ahead + memory).astype(BF16))

    def rows_of(part, *others):
        keys, solved, before = first[part][:3]
        second[part] = rows_pass(
            part,
            query_raw,
            rim,
            conv_query,
            keys,
            gate_flat,
            logit_flat,
            after(solved, *others),
            before,
        )

    for turn in range(count - 1):
        for part in range(PARTS):
            send(part)
            if turn + 1 < count - 1:
                waits = [] if part == 0 or turn >= PARTS else [second[turn][1]]
                carry(part, *waits)
            if part == 0 and turn < PARTS:
                ready = [moved[part][-1] for part in range(PARTS)]
                rows_of(turn, *ready)
    out = None
    for part in range(PARTS):
        rows, local = second[part]
        early = sum(got[part][:-1], jnp.zeros_like(got[part][-1]))
        late = got[part][-1]
        if part + 1 < PARTS:
            late = after(late, moved[part + 1][-1])
        out = final_pass(part, rows, local, early, late, gain, out)
    return out


def solution(mesh):
    return jax.shard_map(
        shards,
        mesh=mesh,
        in_specs=(
            P(("groups", "ctx"), "head"),
            P(("groups", "ctx"), "head"),
            P(("groups", "ctx"), "head"),
            P(None, "head"),
            P(None, "head"),
            P(None, "head"),
            P(("groups", "ctx"), "head"),
            P(("groups", "ctx"), "head"),
            P(),
        ),
        out_specs=P(("groups", "ctx"), "head"),
        check_vma=False,
    )
```

```python
import jax
import jax.numpy as jnp
from jax import lax
from jax.experimental import pallas as pl
from jax.experimental.pallas import tpu as pltpu
from jax.sharding import PartitionSpec as P

DK = 128
DV = 128
KW = 4
CHUNK = 128
HALF = 64
BASE = 8
HALO = 8
RIM = 16
FOLD = 4
PARTS = 2
SPAN_X = 1024
SPAN_Y = 1024
EPSILON = 1e-06
LOG2E = 1.4426950408889634
F32 = jnp.float32
BF16 = jnp.bfloat16
WIDE = DK + DV
VMEM = pl.BlockSpec(memory_space=pltpu.VMEM)


def dot(left, right):
    return jnp.dot(left, right, preferred_element_type=F32)


def levels():
    sizes = []
    size = BASE
    while size < HALF:
        sizes.append(size)
        size *= 2
    return sizes


def iotas(shape):
    return lax.broadcasted_iota(jnp.int32, shape, 0), lax.broadcasted_iota(jnp.int32, shape, 1)


def fill_masks(diag_ref):
    rows, cols = iotas((CHUNK, CHUNK))
    for place, size in enumerate(levels()):
        diag_ref[place] = (rows // size == cols // size).astype(BF16)


def packed(strip):
    if strip.shape[0] < 16:
        strip = jnp.concatenate([strip] * (16 // strip.shape[0]), axis=0)
    return strip.astype(BF16)


def spread(strip, mask):
    count = CHUNK // strip.shape[0]
    return jnp.concatenate([strip] * count, axis=0) * mask


def strips(neg, size, step, first):
    lanes = lax.broadcasted_iota(jnp.int32, (1, CHUNK), 1)
    out = neg[first : first + size]
    for turn in range(1, CHUNK // step):
        start = turn * step + first
        out = jnp.where(lanes // step == turn, neg[start : start + size], out)
    return out


def substitute(strip):
    rows, cols = iotas((8, CHUNK))
    halves = [strip[at : at + 8] for at in range(0, BASE, 8)]
    found = [(rows + at == cols % BASE).astype(F32) for at in range(0, BASE, 8)]
    for row in range(BASE - 1):
        at = cols // BASE * BASE + row
        solved = found[row // 8][row % 8 : row % 8 + 1]
        for half in range((row + 1) // 8, BASE // 8):
            column = jnp.take_along_axis(halves[half], at, axis=1)
            found[half] = found[half] + column * solved
    return jnp.concatenate(found, axis=0)


def half_inverses(negs, diag_ref):
    lanes = lax.broadcasted_iota(jnp.int32, (1, CHUNK), 1)
    found = [substitute(strips(neg, BASE, BASE, 0)) for neg in negs]
    pairs = range(0, len(negs), 2)
    for place, size in enumerate(levels()):
        even = (lanes // size) % 2 == 0

        def up(value):
            return pltpu.roll(value, size, 1)

        def down(value):
            return pltpu.roll(value, CHUNK - size, 1)

        lowers = [strips(neg, size, 2 * size, size) for neg in negs]
        evens = [packed(jnp.where(even, found[i], up(found[i + 1]))) for i in pairs]
        odds = [packed(jnp.where(even, down(found[i]), found[i + 1])) for i in pairs]
        both = [packed(jnp.where(even, lowers[i], up(lowers[i + 1]))) for i in pairs]
        weights = [spread(value, diag_ref[place]) for value in evens]
        middles = [dot(value, weight).astype(BF16) for value, weight in zip(both, weights)]
        weights = [spread(value, diag_ref[place]) for value in middles]
        corners = [dot(value, weight)[:size] for value, weight in zip(odds, weights)]
        wider = []
        for i, f in enumerate(found):
            corner = corners[i // 2] if i % 2 == 0 else down(corners[i // 2])
            wider.append(
                jnp.concatenate([jnp.where(even, f, 0.0), jnp.where(even, corner, f)], axis=0)
            )
        found = wider
    return [f.astype(BF16) for f in found]


def conv(raw, wide, tile, tap):
    span = raw.shape[0]
    raw = raw.astype(F32)
    wide[tile, HALO : HALO + span] = raw
    total = raw * tap[KW - 1 : KW]
    for back in range(1, KW):
        total += wide[tile, HALO - back : HALO - back + span] * tap[KW - 1 - back : KW - back]
    return (total + total * jnp.tanh(total)).astype(BF16)


def row_sums(values):
    return dot(values.astype(BF16), jnp.ones((values.shape[1], values.shape[1]), BF16))


def unit(values, factor):
    values = values.astype(F32)
    scale = lax.rsqrt(jnp.sum(values * values, axis=-1, keepdims=True) + EPSILON)
    if factor != 1.0:
        scale = scale * factor
    return (values * scale).astype(BF16)


def sums(gates, span):
    rows, cols = iotas((CHUNK, CHUNK))
    stacked = jnp.concatenate(
        [gates[:, at : at + CHUNK] for at in range(0, span, CHUNK)], axis=0
    )
    total = jnp.dot(
        stacked,
        (rows <= cols).astype(F32),
        precision=lax.Precision.HIGHEST,
        preferred_element_type=F32,
    )
    heads = gates.shape[0]
    return [total[at * heads : (at + 1) * heads] for at in range(span // CHUNK)]


def rim_kernel(query_ref, key_ref, value_ref, out_ref, rows):
    piece = rows.shape[1]
    rows[...] = jnp.zeros_like(rows)
    at = 0
    for ref in (query_ref, key_ref, value_ref):
        last = ref[...].astype(F32)
        for tile in range(0, ref.shape[1], 128):
            place, lane = (at + tile) // piece, (at + tile) % piece
            for back in range(KW - 1):
                row = back * FOLD + place
                source = RIM - (KW - 1) + back
                rows[row : row + 1, lane : lane + 128] = last[source : source + 1, tile : tile + 128]
        at += ref.shape[1]
    out_ref[...] = rows[...].astype(BF16)


def pack_rim(query_raw, key_raw, value_raw):
    last = query_raw.shape[0] // RIM - 1
    widths = [array.shape[1] for array in (query_raw, key_raw, value_raw)]
    piece = sum(widths) // FOLD
    return pl.pallas_call(
        rim_kernel,
        grid=(1,),
        in_specs=[pl.BlockSpec((RIM, width), lambda i: (last, 0)) for width in widths],
        out_specs=pl.BlockSpec((RIM, piece), lambda i: (0, 0)),
        out_shape=jax.ShapeDtypeStruct((RIM, piece), BF16),
        scratch_shapes=[pltpu.VMEM((RIM, piece), F32)],
        name="pack_rim",
    )(query_raw, key_raw, value_raw)


def unpack_rim(rim, wide, tile, at):
    piece = rim.shape[1]
    for back in range(KW - 1):
        row = back * FOLD + at // piece
        place = HALO - (KW - 1) + back
        wide[tile, place : place + 1] = rim[row : row + 1, at % piece : at % piece + 128]


def log_weights(logit):
    return (jnp.minimum(logit, 0.0) - jnp.log(1.0 + jnp.exp(-jnp.abs(logit)))) * LOG2E


def memory_kernel(
    kheads,
    vheads,
    part,
    span,
    key_ref,
    value_ref,
    rim_ref,
    tap_key_ref,
    tap_value_ref,
    gate_ref,
    logit_ref,
    unit_ref,
    solved_ref,
    before_ref,
    transit_ref,
    memory_ref,
    wide,
    state,
    diag_ref,
    neg_ref,
    tail_ref,
    right_ref,
    sum_ref,
):
    ratio = vheads // kheads
    tiles = kheads + vheads
    parts = span // CHUNK
    first_head = part * vheads
    key_from = part * kheads * DK
    value_from = part * vheads * DV
    rim_from = (key_ref.shape[1] + key_from, 2 * key_ref.shape[1] + value_from)
    places = [(chunk, head) for chunk in range(parts) for head in range(vheads)]

    def set_up():
        fill_masks(diag_ref)
        rows, cols = iotas((DK, WIDE))
        for head in range(vheads):
            state[head] = (rows == cols).astype(F32)
        rim = rim_ref[...].astype(F32)
        for tile in range(tiles):
            at = rim_from[0] + tile * DK if tile < kheads else rim_from[1] + (tile - kheads) * DV
            unpack_rim(rim, wide, tile, at)

    def prepare(step):
        now_rows = pl.ds(pl.multiple_of(step * span, span), span)
        tap_key = tap_key_ref[...].astype(F32) * 0.5
        tap_value = tap_value_ref[...].astype(F32) * 0.5
        keys = []
        for tile in range(kheads):
            at = slice(tile * DK, (tile + 1) * DK)
            place = slice(key_from + tile * DK, key_from + (tile + 1) * DK)
            keys.append(unit(conv(key_ref[now_rows, place], wide, tile, tap_key[:, place]), 1.0))
            unit_ref[now_rows, at] = keys[tile]
        for tile in range(vheads):
            place = slice(value_from + tile * DV, value_from + (tile + 1) * DV)
            value = conv(value_ref[now_rows, place], wide, kheads + tile, tap_value[:, place])
            for chunk in range(parts):
                right_ref[chunk * vheads + tile, :, DK:] = value[
                    chunk * CHUNK : (chunk + 1) * CHUNK
                ]
        for tile in range(tiles):
            wide[tile, 0:HALO] = wide[tile, span : span + HALO]
        rows, cols = iotas((CHUNK, CHUNK))
        strict = rows > cols
        cums = sums(gate_ref[:, now_rows] * LOG2E, span)
        strengths = log_weights(logit_ref[:, now_rows])
        for chunk in range(parts):
            here = slice(chunk * CHUNK, (chunk + 1) * CHUNK)
            cum_flat = cums[chunk]
            cum = cum_flat.T
            lift = strengths[:, here] - cum_flat
            last = cum_flat[:, CHUNK - 1 :]
            ends = jnp.exp2(last + lift)
            sum_ref[chunk] = jnp.broadcast_to(jnp.exp2(last), cum_flat.shape)
            for khead in range(kheads):
                key = keys[khead][here]
                flat = (-key).T
                gram = dot(key, flat)
                for which in range(ratio):
                    head = khead * ratio + which
                    item = chunk * vheads + head
                    place = first_head + head
                    cum_col = jnp.broadcast_to(cum[:, place : place + 1], (CHUNK, CHUNK))
                    powers = cum_col + lift[place : place + 1]
                    decays = jnp.exp2(jnp.where(strict, powers, -jnp.inf))
                    neg_ref[item] = gram * decays
                    tail_ref[item] = flat * ends[place : place + 1].astype(BF16)
                    right_ref[item, :, :DK] = key * jnp.exp2(cum_col).astype(BF16)

    def finish(step):
        base = pl.multiple_of(step * span, span)
        negs = [neg_ref[item] for item in range(len(places))]
        found = half_inverses(negs, diag_ref)
        tops = [
            dot(f[:, :HALF], right_ref[item, :HALF]).astype(BF16)
            for item, f in enumerate(found)
        ]
        rests = [
            (
                right_ref[item, HALF:].astype(F32)
                + dot(neg_ref[item, HALF:, :HALF].astype(BF16), top)
            ).astype(BF16)
            for item, top in enumerate(tops)
        ]
        lows = [dot(f[:, HALF:], rest).astype(BF16) for f, rest in zip(found, rests)]
        erases, writes = [], []
        for item, (chunk, head) in enumerate(places):
            there = slice(head * WIDE, (head + 1) * WIDE)
            solved = jnp.concatenate([tops[item], lows[item]], axis=0)
            solved_ref[pl.ds(base + chunk * CHUNK, CHUNK), there] = solved
            product = dot(tail_ref[item], solved)
            erases.append(product[:, :DK].astype(BF16))
            writes.append(product[:, DK:])
        for item, (chunk, head) in enumerate(places):
            now = state[head]
            short = now.astype(BF16)
            before_ref[step * parts + chunk, head] = short
            tail = sum_ref[chunk, first_head + head : first_head + head + 1]
            change = dot(erases[item], short)
            state[head, :, :DK] = now[:, :DK] * tail + change[:, :DK]
            state[head, :, DK:] = now[:, DK:] * tail + (change[:, DK:] - writes[item])

    def advance(step, carry):
        prepare(step)
        finish(step)
        return carry

    set_up()
    lax.fori_loop(0, key_ref.shape[0] // span, advance, 0)
    for head in range(vheads):
        transit_ref[head] = state[head, :, :DK].astype(BF16)
        memory_ref[head] = state[head, :, DK:]


def memory_pass(part, key_raw, value_raw, rim, conv_key, conv_value, gate_flat, logit_flat):
    tok_count = key_raw.shape[0]
    all_kheads = key_raw.shape[1] // DK
    all_vheads = value_raw.shape[1] // DV
    kheads, vheads = all_kheads // PARTS, all_vheads // PARTS
    tiles = kheads + vheads
    span = min(SPAN_X, tok_count)
    chunks = tok_count // CHUNK
    items = span // CHUNK * vheads
    count = len(levels())

    def kernel(*refs):
        memory_kernel(kheads, vheads, part, span, *refs)

    return pl.pallas_call(
        kernel,
        in_specs=[VMEM] * 7,
        out_specs=[VMEM] * 5,
        out_shape=[
            jax.ShapeDtypeStruct((tok_count, kheads * DK), BF16),
            jax.ShapeDtypeStruct((tok_count, vheads * WIDE), BF16),
            jax.ShapeDtypeStruct((chunks, vheads, DK, WIDE), BF16),
            jax.ShapeDtypeStruct((vheads, DK, DK), BF16),
            jax.ShapeDtypeStruct((vheads, DK, DV), F32),
        ],
        scratch_shapes=[
            pltpu.VMEM((tiles, span + HALO, 128), F32),
            pltpu.VMEM((vheads, DK, WIDE), F32),
            pltpu.VMEM((count, CHUNK, CHUNK), BF16),
            pltpu.VMEM((items, CHUNK, CHUNK), F32),
            pltpu.VMEM((items, CHUNK, CHUNK), BF16),
            pltpu.VMEM((items, CHUNK, WIDE), BF16),
            pltpu.VMEM((span // CHUNK, all_vheads, CHUNK), F32),
        ],
        compiler_params=pltpu.CompilerParams(vmem_limit_bytes=32 * 1024 * 1024),
        cost_estimate=pl.CostEstimate(
            flops=2 * tok_count * vheads * 1000 * 1000, bytes_accessed=1 << 23, transcendentals=0
        ),
        name="memory_pass",
    )(key_raw, value_raw, rim, conv_key, conv_value, gate_flat, logit_flat)


def rows_kernel(
    kheads,
    vheads,
    group,
    span,
    query_ref,
    rim_ref,
    tap_ref,
    key_ref,
    gate_ref,
    logit_ref,
    solved_ref,
    before_ref,
    rows_ref,
    local_ref,
    wide,
):
    ratio = vheads // kheads
    first_head = group * vheads
    query_from = group * kheads * DK
    for tile in range(kheads):
        unpack_rim(rim_ref[...].astype(F32), wide, tile, query_from + tile * DK)

    def advance(step, carry):
        base = pl.multiple_of(step * span, span)
        now_rows = pl.ds(base, span)
        taps = tap_ref[...].astype(F32) * 0.5
        queries = []
        for tile in range(kheads):
            at = slice(query_from + tile * DK, query_from + (tile + 1) * DK)
            queries.append(unit(conv(query_ref[now_rows, at], wide, tile, taps[:, at]), DK**-0.5))

        for tile in range(kheads):
            wide[tile, 0:HALO] = wide[tile, span : span + HALO]
        rows, cols = iotas((CHUNK, CHUNK))
        lower = rows >= cols
        cums = sums(gate_ref[:, now_rows] * LOG2E, span)
        strengths = log_weights(logit_ref[:, now_rows])
        for part in range(span // CHUNK):
            here = slice(part * CHUNK, (part + 1) * CHUNK)
            place_rows = pl.ds(base + part * CHUNK, CHUNK)
            cum_flat = cums[part]
            cum = cum_flat.T
            lift = strengths[:, here] - cum_flat
            for khead in range(kheads):
                query = queries[khead][here]
                gram = lax.dot_general(
                    query,
                    key_ref[place_rows, khead * DK : (khead + 1) * DK],
                    (((1,), (1,)), ((), ())),
                    preferred_element_type=F32,
                )
                for which in range(ratio):
                    head = khead * ratio + which
                    place = first_head + head
                    there = slice(head * DV, (head + 1) * DV)
                    cum_col = jnp.broadcast_to(cum[:, place : place + 1], (CHUNK, CHUNK))
                    powers = cum_col + lift[place : place + 1]
                    scores = (gram * jnp.exp2(jnp.where(lower, powers, -jnp.inf))).astype(BF16)
                    product = dot(scores, solved_ref[place_rows, head * WIDE : (head + 1) * WIDE])
                    meet = query.astype(F32) * jnp.exp2(cum_col) - product[:, :DK]
                    final = dot(meet.astype(BF16), before_ref[step * (span // CHUNK) + part, head])
                    rows_ref[place_rows, there] = final[:, :DK].astype(BF16)
                    local_ref[place_rows, there] = (final[:, DK:] + product[:, DK:]).astype(BF16)
        return carry

    lax.fori_loop(0, query_ref.shape[0] // span, advance, 0)


def rows_pass(part, query_raw, rim, conv_query, keys, gate_flat, logit_flat, solved, before):
    tok_count = query_raw.shape[0]
    kheads = query_raw.shape[1] // DK // PARTS
    all_vheads = gate_flat.shape[0]
    vheads = all_vheads // PARTS
    span = min(SPAN_Y, tok_count)

    def kernel(*refs):
        rows_kernel(kheads, vheads, part, span, *refs)

    return pl.pallas_call(
        kernel,
        in_specs=[VMEM] * 8,
        out_specs=[VMEM] * 2,
        out_shape=[
            jax.ShapeDtypeStruct((tok_count, vheads * DV), BF16),
            jax.ShapeDtypeStruct((tok_count, vheads * DV), BF16),
        ],
        scratch_shapes=[pltpu.VMEM((kheads, span + HALO, 128), F32)],
        compiler_params=pltpu.CompilerParams(vmem_limit_bytes=24 * 1024 * 1024),
        cost_estimate=pl.CostEstimate(
            flops=2 * tok_count * vheads * 1000 * 500, bytes_accessed=1 << 23, transcendentals=0
        ),
        name="rows_pass",
    )(query_raw, rim, conv_query, keys, gate_flat, logit_flat, solved, before)


def final_kernel(vheads, rows_ref, local_ref, early_ref, late_ref, gain_ref, *rest):
    out_ref = rest[-1]
    gain = gain_ref[...]
    span = out_ref.shape[0]
    now_rows = pl.ds(pl.multiple_of(pl.program_id(0) * span, span), span)
    for head in range(vheads):
        there = slice(head * DV, (head + 1) * DV)
        start = early_ref[head] + late_ref[head]
        output = dot(rows_ref[now_rows, there], start) + local_ref[now_rows, there].astype(F32)
        square = output * output
        if head % 2:
            total = row_sums(square)
        else:
            total = jnp.sum(square, axis=-1, keepdims=True)
        mean = total * (1.0 / DV)
        out_ref[:, there] = (output * lax.rsqrt(mean + EPSILON) * gain).astype(BF16)


def final_pass(part, rows, local, early, late, gain, earlier):
    tok_count = rows.shape[0]
    vheads = early.shape[0]
    span = min(512, tok_count)

    def along(width, column):
        return pl.BlockSpec((span, width), lambda i: (i, column))

    def kernel(*refs):
        final_kernel(vheads, *refs)

    arrays = [rows, local, early, late, gain]
    specs = [VMEM] * 5
    if earlier is not None:
        arrays.append(earlier)
        specs.append(pl.BlockSpec(memory_space=pl.ANY))
    return pl.pallas_call(
        kernel,
        grid=(tok_count // span,),
        in_specs=specs,
        out_specs=along(vheads * DV, part),
        out_shape=jax.ShapeDtypeStruct((tok_count, PARTS * vheads * DV), BF16),
        input_output_aliases={} if earlier is None else {5: 0},
        compiler_params=pltpu.CompilerParams(vmem_limit_bytes=12 * 1024 * 1024),
        name="final_pass",
    )(*arrays)


def shards(
    query_raw, key_raw, value_raw, conv_query, conv_key, conv_value, gate_log, beta_logit, norm_gain
):
    count = lax.axis_size("ctx")
    rim = lax.ppermute(
        pack_rim(query_raw, key_raw, value_raw), "ctx", [(at, at + 1) for at in range(count - 1)]
    )
    gate_flat, logit_flat = gate_log.T, beta_logit.T
    gain = norm_gain.reshape(1, DV)
    first = [
        memory_pass(part, key_raw, value_raw, rim, conv_key, conv_value, gate_flat, logit_flat)
        for part in range(PARTS)
    ]
    def after(value, *others):
        return lax.optimization_barrier((value, *others))[0]

    moved = [[found[4].astype(BF16)] for found in first]
    got = [[] for _ in first]
    second = [None] * PARTS

    def send(part):
        source = len(got[part])
        got[part].append(lax.ppermute(moved[part][source], "ctx", [(source, source + 1)]))

    def carry(part, *others):
        transit, memory = first[part][3:]
        arrived = after(got[part][-1], *others)
        ahead = jnp.einsum("hab,hbc->hac", transit, arrived, preferred_element_type=F32)
        moved[part].append((ahead + memory).astype(BF16))

    def rows_of(part, *others):
        keys, solved, before = first[part][:3]
        second[part] = rows_pass(
            part,
            query_raw,
            rim,
            conv_query,
            keys,
            gate_flat,
            logit_flat,
            after(solved, *others),
            before,
        )

    for turn in range(count - 1):
        for part in range(PARTS):
            send(part)
            if turn + 1 < count - 1:
                waits = [] if part == 0 or turn >= PARTS else [second[turn][1]]
                carry(part, *waits)
            if part == 0 and turn < PARTS:
                ready = [moved[part][-1] for part in range(PARTS)]
                rows_of(turn, *ready)
    out = None
    for part in range(PARTS):
        rows, local = second[part]
        early = sum(got[part][:-1], jnp.zeros_like(got[part][-1]))
        late = got[part][-1]
        if part + 1 < PARTS:
            late = after(late, moved[part + 1][-1])
        out = final_pass(part, rows, local, early, late, gain, out)
    return out


def solution(mesh):
    return jax.shard_map(
        shards,
        mesh=mesh,
        in_specs=(
            P(("groups", "ctx"), "head"),
            P(("groups", "ctx"), "head"),
            P(("groups", "ctx"), "head"),
            P(None, "head"),
            P(None, "head"),
            P(None, "head"),
            P(("groups", "ctx"), "head"),
            P(("groups", "ctx"), "head"),
            P(),
        ),
        out_specs=P(("groups", "ctx"), "head"),
        check_vma=False,
    )
```

```python
import jax
import jax.numpy as jnp
from jax import lax
from jax.experimental import pallas as pl
from jax.experimental.pallas import tpu as pltpu
from jax.sharding import PartitionSpec as P

DK = 128
DV = 128
KW = 4
CHUNK = 128
HALF = 64
BASE = 8
HALO = 8
RIM = 16
FOLD = 4
PARTS = 2
SPAN_X = 1024
SPAN_Y = 1024
EPSILON = 1e-06
LOG2E = 1.4426950408889634
F32 = jnp.float32
BF16 = jnp.bfloat16
WIDE = DK + DV
VMEM = pl.BlockSpec(memory_space=pltpu.VMEM)


def dot(left, right):
    return jnp.dot(left, right, preferred_element_type=F32)


def levels():
    sizes = []
    size = BASE
    while size < HALF:
        sizes.append(size)
        size *= 2
    return sizes


def iotas(shape):
    return lax.broadcasted_iota(jnp.int32, shape, 0), lax.broadcasted_iota(jnp.int32, shape, 1)


def fill_masks(diag_ref):
    rows, cols = iotas((CHUNK, CHUNK))
    for place, size in enumerate(levels()):
        diag_ref[place] = (rows // size == cols // size).astype(BF16)


def packed(strip):
    if strip.shape[0] < 16:
        strip = jnp.concatenate([strip] * (16 // strip.shape[0]), axis=0)
    return strip.astype(BF16)


def spread(strip, mask):
    count = CHUNK // strip.shape[0]
    return jnp.concatenate([strip] * count, axis=0) * mask


def strips(neg, size, step, first):
    lanes = lax.broadcasted_iota(jnp.int32, (1, CHUNK), 1)
    out = neg[first : first + size]
    for turn in range(1, CHUNK // step):
        start = turn * step + first
        out = jnp.where(lanes // step == turn, neg[start : start + size], out)
    return out


def substitute(strip):
    rows, cols = iotas((8, CHUNK))
    halves = [strip[at : at + 8] for at in range(0, BASE, 8)]
    found = [(rows + at == cols % BASE).astype(F32) for at in range(0, BASE, 8)]
    for row in range(BASE - 1):
        at = cols // BASE * BASE + row
        solved = found[row // 8][row % 8 : row % 8 + 1]
        for half in range((row + 1) // 8, BASE // 8):
            column = jnp.take_along_axis(halves[half], at, axis=1)
            found[half] = found[half] + column * solved
    return jnp.concatenate(found, axis=0)


def half_inverses(negs, diag_ref):
    lanes = lax.broadcasted_iota(jnp.int32, (1, CHUNK), 1)
    found = [substitute(strips(neg, BASE, BASE, 0)) for neg in negs]
    pairs = range(0, len(negs), 2)
    for place, size in enumerate(levels()):
        even = (lanes // size) % 2 == 0

        def up(value):
            return pltpu.roll(value, size, 1)

        def down(value):
            return pltpu.roll(value, CHUNK - size, 1)

        lowers = [strips(neg, size, 2 * size, size) for neg in negs]
        evens = [packed(jnp.where(even, found[i], up(found[i + 1]))) for i in pairs]
        odds = [packed(jnp.where(even, down(found[i]), found[i + 1])) for i in pairs]
        both = [packed(jnp.where(even, lowers[i], up(lowers[i + 1]))) for i in pairs]
        weights = [spread(value, diag_ref[place]) for value in evens]
        middles = [dot(value, weight).astype(BF16) for value, weight in zip(both, weights)]
        weights = [spread(value, diag_ref[place]) for value in middles]
        corners = [dot(value, weight)[:size] for value, weight in zip(odds, weights)]
        wider = []
        for i, f in enumerate(found):
            corner = corners[i // 2] if i % 2 == 0 else down(corners[i // 2])
            wider.append(
                jnp.concatenate([jnp.where(even, f, 0.0), jnp.where(even, corner, f)], axis=0)
            )
        found = wider
    return [f.astype(BF16) for f in found]


def conv(raw, wide, tile, tap):
    span = raw.shape[0]
    raw = raw.astype(F32)
    wide[tile, HALO : HALO + span] = raw
    total = raw * tap[KW - 1 : KW]
    for back in range(1, KW):
        total += wide[tile, HALO - back : HALO - back + span] * tap[KW - 1 - back : KW - back]
    return (total + total * jnp.tanh(total)).astype(BF16)


def row_sums(values):
    return dot(values.astype(BF16), jnp.ones((values.shape[1], values.shape[1]), BF16))


def unit(values, factor):
    values = values.astype(F32)
    scale = lax.rsqrt(jnp.sum(values * values, axis=-1, keepdims=True) + EPSILON)
    if factor != 1.0:
        scale = scale * factor
    return (values * scale).astype(BF16)


def sums(gates, span):
    rows, cols = iotas((CHUNK, CHUNK))
    stacked = jnp.concatenate(
        [gates[:, at : at + CHUNK] for at in range(0, span, CHUNK)], axis=0
    )
    total = jnp.dot(
        stacked,
        (rows <= cols).astype(F32),
        precision=lax.Precision.HIGHEST,
        preferred_element_type=F32,
    )
    heads = gates.shape[0]
    return [total[at * heads : (at + 1) * heads] for at in range(span // CHUNK)]


def rim_kernel(query_ref, key_ref, value_ref, out_ref, rows):
    piece = rows.shape[1]
    rows[...] = jnp.zeros_like(rows)
    at = 0
    for ref in (query_ref, key_ref, value_ref):
        last = ref[...].astype(F32)
        for tile in range(0, ref.shape[1], 128):
            place, lane = (at + tile) // piece, (at + tile) % piece
            for back in range(KW - 1):
                row = back * FOLD + place
                source = RIM - (KW - 1) + back
                rows[row : row + 1, lane : lane + 128] = last[source : source + 1, tile : tile + 128]
        at += ref.shape[1]
    out_ref[...] = rows[...].astype(BF16)


def pack_rim(query_raw, key_raw, value_raw):
    last = query_raw.shape[0] // RIM - 1
    widths = [array.shape[1] for array in (query_raw, key_raw, value_raw)]
    piece = sum(widths) // FOLD
    return pl.pallas_call(
        rim_kernel,
        grid=(1,),
        in_specs=[pl.BlockSpec((RIM, width), lambda i: (last, 0)) for width in widths],
        out_specs=pl.BlockSpec((RIM, piece), lambda i: (0, 0)),
        out_shape=jax.ShapeDtypeStruct((RIM, piece), BF16),
        scratch_shapes=[pltpu.VMEM((RIM, piece), F32)],
        name="pack_rim",
    )(query_raw, key_raw, value_raw)


def unpack_rim(rim, wide, tile, at):
    piece = rim.shape[1]
    for back in range(KW - 1):
        row = back * FOLD + at // piece
        place = HALO - (KW - 1) + back
        wide[tile, place : place + 1] = rim[row : row + 1, at % piece : at % piece + 128]


def log_weights(logit):
    return (jnp.minimum(logit, 0.0) - jnp.log(1.0 + jnp.exp(-jnp.abs(logit)))) * LOG2E


def memory_kernel(
    kheads,
    vheads,
    part,
    span,
    key_ref,
    value_ref,
    rim_ref,
    tap_key_ref,
    tap_value_ref,
    gate_ref,
    logit_ref,
    unit_ref,
    solved_ref,
    before_ref,
    transit_ref,
    memory_ref,
    wide,
    state,
    diag_ref,
    neg_ref,
    tail_ref,
    right_ref,
    sum_ref,
):
    ratio = vheads // kheads
    tiles = kheads + vheads
    parts = span // CHUNK
    first_head = part * vheads
    key_from = part * kheads * DK
    value_from = part * vheads * DV
    rim_from = (key_ref.shape[1] + key_from, 2 * key_ref.shape[1] + value_from)
    places = [(chunk, head) for chunk in range(parts) for head in range(vheads)]

    def set_up():
        fill_masks(diag_ref)
        rows, cols = iotas((DK, WIDE))
        for head in range(vheads):
            state[head] = (rows == cols).astype(F32)
        rim = rim_ref[...].astype(F32)
        for tile in range(tiles):
            at = rim_from[0] + tile * DK if tile < kheads else rim_from[1] + (tile - kheads) * DV
            unpack_rim(rim, wide, tile, at)

    def prepare(step):
        now_rows = pl.ds(pl.multiple_of(step * span, span), span)
        tap_key = tap_key_ref[...].astype(F32) * 0.5
        tap_value = tap_value_ref[...].astype(F32) * 0.5
        keys = []
        for tile in range(kheads):
            at = slice(tile * DK, (tile + 1) * DK)
            place = slice(key_from + tile * DK, key_from + (tile + 1) * DK)
            keys.append(unit(conv(key_ref[now_rows, place], wide, tile, tap_key[:, place]), 1.0))
            unit_ref[now_rows, at] = keys[tile]
        for tile in range(vheads):
            place = slice(value_from + tile * DV, value_from + (tile + 1) * DV)
            value = conv(value_ref[now_rows, place], wide, kheads + tile, tap_value[:, place])
            for chunk in range(parts):
                right_ref[chunk * vheads + tile, :, DK:] = value[
                    chunk * CHUNK : (chunk + 1) * CHUNK
                ]
        for tile in range(tiles):
            wide[tile, 0:HALO] = wide[tile, span : span + HALO]
        rows, cols = iotas((CHUNK, CHUNK))
        strict = rows > cols
        cums = sums(gate_ref[:, now_rows] * LOG2E, span)
        strengths = log_weights(logit_ref[:, now_rows])
        for chunk in range(parts):
            here = slice(chunk * CHUNK, (chunk + 1) * CHUNK)
            cum_flat = cums[chunk]
            cum = cum_flat.T
            lift = strengths[:, here] - cum_flat
            last = cum_flat[:, CHUNK - 1 :]
            ends = jnp.exp2(last + lift)
            sum_ref[chunk] = jnp.broadcast_to(jnp.exp2(last), cum_flat.shape)
            for khead in range(kheads):
                key = keys[khead][here]
                flat = (-key).T
                gram = dot(key, flat)
                for which in range(ratio):
                    head = khead * ratio + which
                    item = chunk * vheads + head
                    place = first_head + head
                    cum_col = jnp.broadcast_to(cum[:, place : place + 1], (CHUNK, CHUNK))
                    powers = cum_col + lift[place : place + 1]
                    decays = jnp.exp2(jnp.where(strict, powers, -jnp.inf))
                    neg_ref[item] = gram * decays
                    tail_ref[item] = flat * ends[place : place + 1].astype(BF16)
                    right_ref[item, :, :DK] = key * jnp.exp2(cum_col).astype(BF16)

    def finish(step):
        base = pl.multiple_of(step * span, span)
        negs = [neg_ref[item] for item in range(len(places))]
        found = half_inverses(negs, diag_ref)
        tops = [
            dot(f[:, :HALF], right_ref[item, :HALF]).astype(BF16)
            for item, f in enumerate(found)
        ]
        rests = [
            (
                right_ref[item, HALF:].astype(F32)
                + dot(neg_ref[item, HALF:, :HALF].astype(BF16), top)
            ).astype(BF16)
            for item, top in enumerate(tops)
        ]
        lows = [dot(f[:, HALF:], rest).astype(BF16) for f, rest in zip(found, rests)]
        erases, writes = [], []
        for item, (chunk, head) in enumerate(places):
            there = slice(head * WIDE, (head + 1) * WIDE)
            solved = jnp.concatenate([tops[item], lows[item]], axis=0)
            solved_ref[pl.ds(base + chunk * CHUNK, CHUNK), there] = solved
            product = dot(tail_ref[item], solved)
            erases.append(product[:, :DK].astype(BF16))
            writes.append(product[:, DK:])
        for item, (chunk, head) in enumerate(places):
            now = state[head]
            short = now.astype(BF16)
            before_ref[step * parts + chunk, head] = short
            tail = sum_ref[chunk, first_head + head : first_head + head + 1]
            change = dot(erases[item], short)
            state[head, :, :DK] = now[:, :DK] * tail + change[:, :DK]
            state[head, :, DK:] = now[:, DK:] * tail + (change[:, DK:] - writes[item])

    def advance(step, carry):
        prepare(step)
        finish(step)
        return carry

    set_up()
    lax.fori_loop(0, key_ref.shape[0] // span, advance, 0)
    for head in range(vheads):
        transit_ref[head] = state[head, :, :DK].astype(BF16)
        memory_ref[head] = state[head, :, DK:]


def memory_pass(part, key_raw, value_raw, rim, conv_key, conv_value, gate_flat, logit_flat):
    tok_count = key_raw.shape[0]
    all_kheads = key_raw.shape[1] // DK
    all_vheads = value_raw.shape[1] // DV
    kheads, vheads = all_kheads // PARTS, all_vheads // PARTS
    tiles = kheads + vheads
    span = min(SPAN_X, tok_count)
    chunks = tok_count // CHUNK
    items = span // CHUNK * vheads
    count = len(levels())

    def kernel(*refs):
        memory_kernel(kheads, vheads, part, span, *refs)

    return pl.pallas_call(
        kernel,
        in_specs=[VMEM] * 7,
        out_specs=[VMEM] * 5,
        out_shape=[
            jax.ShapeDtypeStruct((tok_count, kheads * DK), BF16),
            jax.ShapeDtypeStruct((tok_count, vheads * WIDE), BF16),
            jax.ShapeDtypeStruct((chunks, vheads, DK, WIDE), BF16),
            jax.ShapeDtypeStruct((vheads, DK, DK), BF16),
            jax.ShapeDtypeStruct((vheads, DK, DV), F32),
        ],
        scratch_shapes=[
            pltpu.VMEM((tiles, span + HALO, 128), F32),
            pltpu.VMEM((vheads, DK, WIDE), F32),
            pltpu.VMEM((count, CHUNK, CHUNK), BF16),
            pltpu.VMEM((items, CHUNK, CHUNK), F32),
            pltpu.VMEM((items, CHUNK, CHUNK), BF16),
            pltpu.VMEM((items, CHUNK, WIDE), BF16),
            pltpu.VMEM((span // CHUNK, all_vheads, CHUNK), F32),
        ],
        compiler_params=pltpu.CompilerParams(vmem_limit_bytes=32 * 1024 * 1024),
        cost_estimate=pl.CostEstimate(
            flops=2 * tok_count * vheads * 1000 * 1000, bytes_accessed=1 << 23, transcendentals=0
        ),
        name="memory_pass",
    )(key_raw, value_raw, rim, conv_key, conv_value, gate_flat, logit_flat)


def rows_kernel(
    kheads,
    vheads,
    group,
    span,
    query_ref,
    rim_ref,
    tap_ref,
    key_ref,
    gate_ref,
    logit_ref,
    solved_ref,
    before_ref,
    rows_ref,
    local_ref,
    wide,
):
    ratio = vheads // kheads
    first_head = group * vheads
    query_from = group * kheads * DK
    for tile in range(kheads):
        unpack_rim(rim_ref[...].astype(F32), wide, tile, query_from + tile * DK)

    def advance(step, carry):
        base = pl.multiple_of(step * span, span)
        now_rows = pl.ds(base, span)
        taps = tap_ref[...].astype(F32) * 0.5
        queries = []
        for tile in range(kheads):
            at = slice(query_from + tile * DK, query_from + (tile + 1) * DK)
            queries.append(unit(conv(query_ref[now_rows, at], wide, tile, taps[:, at]), DK**-0.5))

        for tile in range(kheads):
            wide[tile, 0:HALO] = wide[tile, span : span + HALO]
        rows, cols = iotas((CHUNK, CHUNK))
        lower = rows >= cols
        cums = sums(gate_ref[:, now_rows] * LOG2E, span)
        strengths = log_weights(logit_ref[:, now_rows])
        for part in range(span // CHUNK):
            here = slice(part * CHUNK, (part + 1) * CHUNK)
            place_rows = pl.ds(base + part * CHUNK, CHUNK)
            cum_flat = cums[part]
            cum = cum_flat.T
            lift = strengths[:, here] - cum_flat
            for khead in range(kheads):
                query = queries[khead][here]
                gram = lax.dot_general(
                    query,
                    key_ref[place_rows, khead * DK : (khead + 1) * DK],
                    (((1,), (1,)), ((), ())),
                    preferred_element_type=F32,
                )
                for which in range(ratio):
                    head = khead * ratio + which
                    place = first_head + head
                    there = slice(head * DV, (head + 1) * DV)
                    cum_col = jnp.broadcast_to(cum[:, place : place + 1], (CHUNK, CHUNK))
                    powers = cum_col + lift[place : place + 1]
                    scores = (gram * jnp.exp2(jnp.where(lower, powers, -jnp.inf))).astype(BF16)
                    product = dot(scores, solved_ref[place_rows, head * WIDE : (head + 1) * WIDE])
                    meet = query.astype(F32) * jnp.exp2(cum_col) - product[:, :DK]
                    final = dot(meet.astype(BF16), before_ref[step * (span // CHUNK) + part, head])
                    rows_ref[place_rows, there] = final[:, :DK].astype(BF16)
                    local_ref[place_rows, there] = (final[:, DK:] + product[:, DK:]).astype(BF16)
        return carry

    lax.fori_loop(0, query_ref.shape[0] // span, advance, 0)


def rows_pass(part, query_raw, rim, conv_query, keys, gate_flat, logit_flat, solved, before):
    tok_count = query_raw.shape[0]
    kheads = query_raw.shape[1] // DK // PARTS
    all_vheads = gate_flat.shape[0]
    vheads = all_vheads // PARTS
    span = min(SPAN_Y, tok_count)

    def kernel(*refs):
        rows_kernel(kheads, vheads, part, span, *refs)

    return pl.pallas_call(
        kernel,
        in_specs=[VMEM] * 8,
        out_specs=[VMEM] * 2,
        out_shape=[
            jax.ShapeDtypeStruct((tok_count, vheads * DV), BF16),
            jax.ShapeDtypeStruct((tok_count, vheads * DV), BF16),
        ],
        scratch_shapes=[pltpu.VMEM((kheads, span + HALO, 128), F32)],
        compiler_params=pltpu.CompilerParams(vmem_limit_bytes=24 * 1024 * 1024),
        cost_estimate=pl.CostEstimate(
            flops=2 * tok_count * vheads * 1000 * 500, bytes_accessed=1 << 23, transcendentals=0
        ),
        name="rows_pass",
    )(query_raw, rim, conv_query, keys, gate_flat, logit_flat, solved, before)


def final_kernel(vheads, rows_ref, local_ref, early_ref, late_ref, gain_ref, *rest):
    out_ref = rest[-1]
    gain = gain_ref[...]
    span = out_ref.shape[0]
    now_rows = pl.ds(pl.multiple_of(pl.program_id(0) * span, span), span)
    for head in range(vheads):
        there = slice(head * DV, (head + 1) * DV)
        start = early_ref[head] + late_ref[head]
        output = dot(rows_ref[now_rows, there], start) + local_ref[now_rows, there].astype(F32)
        square = output * output
        if head % 2:
            total = row_sums(square)
        else:
            total = jnp.sum(square, axis=-1, keepdims=True)
        mean = total * (1.0 / DV)
        out_ref[:, there] = (output * lax.rsqrt(mean + EPSILON) * gain).astype(BF16)


def final_pass(part, rows, local, early, late, gain, earlier):
    tok_count = rows.shape[0]
    vheads = early.shape[0]
    span = min(1024, tok_count)

    def along(width, column):
        return pl.BlockSpec((span, width), lambda i: (i, column))

    def kernel(*refs):
        final_kernel(vheads, *refs)

    arrays = [rows, local, early, late, gain]
    specs = [VMEM] * 5
    if earlier is not None:
        arrays.append(earlier)
        specs.append(pl.BlockSpec(memory_space=pl.ANY))
    return pl.pallas_call(
        kernel,
        grid=(tok_count // span,),
        in_specs=specs,
        out_specs=along(vheads * DV, part),
        out_shape=jax.ShapeDtypeStruct((tok_count, PARTS * vheads * DV), BF16),
        input_output_aliases={} if earlier is None else {5: 0},
        compiler_params=pltpu.CompilerParams(vmem_limit_bytes=16 * 1024 * 1024),
        name="final_pass",
    )(*arrays)


def shards(
    query_raw, key_raw, value_raw, conv_query, conv_key, conv_value, gate_log, beta_logit, norm_gain
):
    count = lax.axis_size("ctx")
    rim = lax.ppermute(
        pack_rim(query_raw, key_raw, value_raw), "ctx", [(at, at + 1) for at in range(count - 1)]
    )
    gate_flat, logit_flat = gate_log.T, beta_logit.T
    gain = norm_gain.reshape(1, DV)
    first = [
        memory_pass(part, key_raw, value_raw, rim, conv_key, conv_value, gate_flat, logit_flat)
        for part in range(PARTS)
    ]
    def after(value, *others):
        return lax.optimization_barrier((value, *others))[0]

    moved = [[found[4].astype(BF16)] for found in first]
    got = [[] for _ in first]
    second = [None] * PARTS

    def send(part):
        source = len(got[part])
        got[part].append(lax.ppermute(moved[part][source], "ctx", [(source, source + 1)]))

    def carry(part, *others):
        transit, memory = first[part][3:]
        arrived = after(got[part][-1], *others)
        ahead = jnp.einsum("hab,hbc->hac", transit, arrived, preferred_element_type=F32)
        moved[part].append((ahead + memory).astype(BF16))

    def rows_of(part, *others):
        keys, solved, before = first[part][:3]
        second[part] = rows_pass(
            part,
            query_raw,
            rim,
            conv_query,
            keys,
            gate_flat,
            logit_flat,
            after(solved, *others),
            before,
        )

    for turn in range(count - 1):
        for part in range(PARTS):
            send(part)
            if turn + 1 < count - 1:
                waits = [] if part == 0 or turn >= PARTS else [second[turn][1]]
                carry(part, *waits)
            if part == 0 and turn < PARTS:
                ready = [moved[part][-1] for part in range(PARTS)]
                rows_of(turn, *ready)
    out = None
    for part in range(PARTS):
        rows, local = second[part]
        early = sum(got[part][:-1], jnp.zeros_like(got[part][-1]))
        late = got[part][-1]
        if part + 1 < PARTS:
            late = after(late, moved[part + 1][-1])
        out = final_pass(part, rows, local, early, late, gain, out)
    return out


def solution(mesh):
    return jax.shard_map(
        shards,
        mesh=mesh,
        in_specs=(
            P(("groups", "ctx"), "head"),
            P(("groups", "ctx"), "head"),
            P(("groups", "ctx"), "head"),
            P(None, "head"),
            P(None, "head"),
            P(None, "head"),
            P(("groups", "ctx"), "head"),
            P(("groups", "ctx"), "head"),
            P(),
        ),
        out_specs=P(("groups", "ctx"), "head"),
        check_vma=False,
    )
```
